32 devices in a mesh: dp: 8 (over z, y), mp: 4 (over x, core).
Axes of the slice: x: 2, y: 2, z: 4, core: 2. Of those that a mesh axis runs over, the one named last changes fastest.
Arguments:
- texts: bfloat16 [192, 128, 1024], P('dp')
- w_qkv: bfloat16 [1024, 3072], P(None, 'mp'), may hold values from -0.1875 to 0.1875
- w_out: bfloat16 [1024, 1024], P('mp'), may hold values from -0.75 to 0.75
- w_self: bfloat16 [1024, 1024], P('mp'), may hold values from -0.1875 to 0.1875
- w_neigh: bfloat16 [1024, 1024], P('mp'), may hold values from -0.1875 to 0.1875
- neighbours: int32 [192, 16], P('dp'), may hold values from -1 to 191, as said below
- cotangent: bfloat16 [192, 1024], P('dp', 'mp'), may hold values from -6 to 6
Outputs:
- mixed: bfloat16 [192, 1024], P('dp', 'mp')
- node_grad: bfloat16 [192, 1024], P('dp', 'mp')
- grad_w_self: float32 [1024, 1024], P('mp')
- grad_w_neigh: float32 [1024, 1024], P('mp')
- grad_w_out: float32 [1024, 1024], P('mp')
The draws below stay inside these ranges and needn't reach their ends.
Inputs may be any that keep to these rules, and one draw needn't show every extreme that they name: `neighbours`: A node id j lives with index j // 24 of dp. In the rows of one dp device (aligned blocks of 24 rows) at most 48 entries fall in any one owner's id range, and some owner gets exactly 48; entries are -1 or ids below 192. Some targets have every slot -1.
All inputs are finite; a program needn't handle non-finite values.
Results may differ from the reference program's by a relative error of at most 0.029.
The reference program's roundings to bfloat16 on the way (of `qkv`, `probs`, `pooled`, `embed`, `agg`, `dz` and `msg`) count: a program that leaves them out, or rounds other values in their place, can miss the bound.
Values may be sent and summed in bfloat16 or wider, within the bound.
No kernel may reach another device: no remote copies, remote signals or barrier semaphores. Data moves between devices by JAX's collectives and lax.ppermute only.
A program may use at most 64 MiB of HBM per device.

```python
import jax
import jax.numpy as jnp
from jax import lax

D = 1024
HEADS = 16
HD = 64
L = 128
FAN = 16
NODE_DEV = 24
NODES = 192


def draw_texts(key, part):
    key = jax.random.fold_in(key, 5)
    first = jax.random.fold_in(key, 0)
    base = jax.random.normal(first, (NODES, L, D), jnp.float32)
    return base.astype(jnp.bfloat16)


def draw_neighbours(key, part):
    key = jax.random.fold_in(key, 11)
    groups = NODES // NODE_DEV
    slots = NODE_DEV * FAN
    limit = slots // groups
    room = slots - FAN

    def one_group(gkey):
        k_count, k_full, k_local, k_order, k_empty = jax.random.split(gkey, 5)
        counts = jax.random.randint(k_count, (groups,), 0, limit + 1)
        full_owner = jax.random.randint(k_full, (), 0, groups)
        counts = jnp.where(jnp.arange(groups) == full_owner, limit, counts)
        rotated = (jnp.arange(groups) + full_owner) % groups
        counts_rot = counts[rotated]
        before = jnp.cumsum(counts_rot) - counts_rot
        kept_rot = jnp.clip(room - before, 0, counts_rot)
        kept = jnp.zeros((groups,), jnp.int32).at[rotated].set(kept_rot.astype(jnp.int32))
        slot = jnp.arange(slots)
        owner = slot // limit
        rank = slot % limit
        local = jax.random.randint(k_local, (slots,), 0, NODE_DEV)
        ids = jnp.where(rank < kept[owner], owner * NODE_DEV + local, -1)
        live_first = jnp.argsort((ids < 0).astype(jnp.int32) * slots + slot, stable=True)
        packed = ids[live_first]
        empty_row = jax.random.randint(k_empty, (), 0, NODE_DEV)
        shuffled = jax.random.permutation(k_order, slots)
        in_empty = (shuffled // FAN == empty_row).astype(jnp.int32)
        places = shuffled[jnp.argsort(in_empty * slots + slot, stable=True)]
        result = jnp.full((slots,), -1, jnp.int32).at[places].set(packed.astype(jnp.int32))
        return result.reshape(NODE_DEV, FAN)
    group_keys = jax.random.split(key, groups)
    return jax.vmap(one_group)(group_keys).reshape(NODES, FAN).astype(jnp.int32)


def block_levels(key, extent, pieces, low, top_value):
    level, own = 1.0, jax.random.fold_in(key, 6)
    for axis_at, parts in pieces:
        heights = jnp.exp(jax.random.uniform(jax.random.fold_in(own, axis_at), (parts,), jnp.float32, low / len(pieces), top_value / len(pieces)))
        level = level * jnp.repeat(heights, extent[axis_at] // parts).reshape([-1 if axis == axis_at else 1 for axis in range(len(extent))])
    return level


def centred(key, shape, width, most, pieces=(), kind=jnp.bfloat16):
    factor_of = block_levels(key, shape, pieces, -0.22, 0.18) if pieces else 1.0
    entries = jax.random.normal(key, shape, jnp.float32) * width * factor_of
    return jnp.minimum(jnp.maximum(entries, -most), most).astype(kind)


def setup_inputs(seed: int = 0) -> dict:
    splits = jax.random.split(jax.random.key(seed), 8)
    return {
        "texts": draw_texts(jax.random.fold_in(splits[7], 71), 0),
        "w_qkv": centred(splits[1], (D, 3 * D), D ** -0.5, 0.1875, ((1, 4),)),
        "w_out": centred(splits[2], (D, D), HD ** -0.5, 0.75, ((0, 4),)),
        "w_self": centred(splits[3], (D, D), D ** -0.5, 0.1875, ((0, 4),)),
        "w_neigh": centred(splits[4], (D, D), D ** -0.5, 0.1875, ((0, 4),)),
        "neighbours": draw_neighbours(jax.random.fold_in(splits[7], 71), 0),
        "cotangent": centred(splits[6], (NODES, D), 1.0, 6.0, ((0, 8), (1, 4))),
    }


def encode_block(block, w_qkv):
    count = block.shape[0]
    qkv = jnp.einsum('nld,de->nle', block.astype(jnp.float32), w_qkv.astype(jnp.float32)).astype(jnp.bfloat16)
    qkv = qkv.reshape(count, L, HEADS, 3, HD)
    query = qkv[:, :, :, 0, :].astype(jnp.float32)
    keys = qkv[:, :, :, 1, :].astype(jnp.float32)
    values = qkv[:, :, :, 2, :].astype(jnp.float32)
    scores = jnp.einsum('nqhd,nkhd->nhqk', query, keys) / jnp.sqrt(jnp.float32(HD))
    probs = jax.nn.softmax(scores, axis=-1).astype(jnp.bfloat16)
    context = jnp.einsum('nhqk,nkhd->nhd', probs.astype(jnp.float32), values) / jnp.float32(L)
    return context.reshape(count, D).astype(jnp.bfloat16)

def reference(texts, w_qkv, w_out, w_self, w_neigh, neighbours, cotangent):
    blocks = texts.reshape(NODES // 8, 8, L, D)
    pooled = lax.map(lambda blk: encode_block(blk, w_qkv), blocks).reshape(NODES, D)
    token_mean = lax.optimization_barrier(jnp.mean(texts.astype(jnp.float32), axis=1))
    embed = (token_mean + jnp.dot(pooled, w_out, preferred_element_type=jnp.float32)).astype(jnp.bfloat16)
    valid = neighbours >= 0
    safe_ids = jnp.where(valid, neighbours, 0).astype(jnp.int32)
    cnt = jnp.maximum(lax.optimization_barrier(jnp.sum(valid, axis=1)).astype(jnp.float32), 1.0)
    picked = embed[safe_ids].astype(jnp.float32) * valid[:, :, None].astype(jnp.float32)
    agg = (lax.optimization_barrier(jnp.sum(picked, axis=1)) / cnt[:, None]).astype(jnp.bfloat16)
    z = jnp.dot(embed, w_self, preferred_element_type=jnp.float32) + jnp.dot(agg, w_neigh, preferred_element_type=jnp.float32)
    mixed = jax.nn.gelu(z).astype(jnp.bfloat16)
    _, pullback = jax.vjp(jax.nn.gelu, z)
    dz = pullback(cotangent.astype(jnp.float32))[0].astype(jnp.bfloat16)
    d_agg = jnp.dot(dz, w_neigh.T, preferred_element_type=jnp.float32)
    msg = (d_agg / cnt[:, None]).astype(jnp.bfloat16)
    spread = jnp.broadcast_to(msg.astype(jnp.float32)[:, None, :], (NODES, FAN, D)) * valid[:, :, None].astype(jnp.float32)
    neighbour_sum = jnp.zeros((NODES, D), jnp.float32).at[safe_ids.reshape(-1)].add(spread.reshape(NODES * FAN, D))
    node_grad = (jnp.dot(dz, w_self.T, preferred_element_type=jnp.float32) + neighbour_sum).astype(jnp.bfloat16)
    factor = 1.0 / jnp.sqrt(jnp.float32(NODES))
    grad_w_self = jnp.dot(embed.T, dz, preferred_element_type=jnp.float32) * factor
    grad_w_neigh = jnp.dot(agg.T, dz, preferred_element_type=jnp.float32) * factor
    grad_w_out = jnp.dot(pooled.T, node_grad, preferred_element_type=jnp.float32) * factor
    return (mixed, node_grad, grad_w_self, grad_w_neigh, grad_w_out)
```

```python
import jax
import jax.numpy as jnp
from jax import lax
from jax.sharding import PartitionSpec as P

HD = 64
BF = jnp.bfloat16
F32 = jnp.float32


def attention(texts, w_qkv):
    node_dev, seq_len, width = texts.shape
    heads_here = w_qkv.shape[1] // (3 * HD)
    qkv = jnp.einsum("nld,de->nle", texts, w_qkv, preferred_element_type=F32).astype(BF)
    qkv = qkv.reshape(node_dev, seq_len, heads_here, 3, HD)
    scores = jnp.einsum(
        "nqhd,nkhd->nhqk", qkv[:, :, :, 0, :], qkv[:, :, :, 1, :], preferred_element_type=F32
    )
    probs = jax.nn.softmax(scores / jnp.sqrt(jnp.float32(HD)), axis=-1).astype(BF)
    context = jnp.einsum("nhqk,nkhd->nhd", probs, qkv[:, :, :, 2, :], preferred_element_type=F32)
    return (context / jnp.float32(seq_len)).reshape(node_dev, heads_here * HD).astype(BF)


def gather_all(block):
    whole = lax.all_gather(block, ("dp", "mp"), axis=0, tiled=False)
    dp, mp = lax.axis_size("dp"), lax.axis_size("mp")
    rows, cols = block.shape
    whole = whole.reshape(dp, mp, rows, cols).transpose(0, 2, 1, 3)
    return whole.reshape(dp * rows, mp * cols)


def dot_t(a, b):
    return lax.dot_general(a, b, (((1,), (1,)), ((), ())), preferred_element_type=F32)


def t_dot(a, b):
    return lax.dot_general(a, b, (((0,), (0,)), ((), ())), preferred_element_type=F32)


def per_device(texts, w_qkv, w_out, w_self, w_neigh, neighbours, cotangent):
    node_dev, seq_len, width = texts.shape
    cols = w_self.shape[0]
    nodes = node_dev * lax.axis_size("dp")
    factor = 1.0 / jnp.sqrt(jnp.float32(nodes))
    row0 = lax.axis_index("dp") * node_dev
    col0 = lax.axis_index("mp") * cols

    def own_cols(a):
        return lax.dynamic_slice_in_dim(a, col0, cols, 1)

    w_out = lax.all_gather(w_out, "mp", axis=0, tiled=True)
    w_self = lax.all_gather(w_self, "mp", axis=0, tiled=True)
    w_neigh = lax.all_gather(w_neigh, "mp", axis=0, tiled=True)
    ids = lax.all_gather(neighbours, "dp", axis=0, tiled=True)
    cot = gather_all(cotangent)
    my_texts = lax.dynamic_slice_in_dim(texts, col0, cols, 2)
    token_mean = gather_all(jnp.mean(my_texts.astype(F32), axis=1))

    pooled = gather_all(attention(texts, w_qkv))
    embed = (token_mean + jnp.dot(pooled, w_out, preferred_element_type=F32)).astype(BF)
    cnt = jnp.maximum(jnp.sum(ids >= 0, axis=1).astype(F32), 1.0)[:, None]
    counts = jnp.sum(ids[:, :, None] == jnp.arange(nodes)[None, None, :], axis=1).astype(BF)
    agg = (jnp.dot(counts, embed, preferred_element_type=F32) / cnt).astype(BF)
    z = jnp.dot(embed, w_self, preferred_element_type=F32) + jnp.dot(
        agg, w_neigh, preferred_element_type=F32
    )
    out, pullback = jax.vjp(jax.nn.gelu, z)
    mixed = out.astype(BF)
    dz = pullback(cot.astype(F32))[0].astype(BF)
    msg = (dot_t(dz, w_neigh) / cnt).astype(BF)
    node_grad = (dot_t(dz, w_self) + t_dot(counts, msg)).astype(BF)
    grads = [
        t_dot(own_cols(left), right) * factor
        for left, right in ((embed, dz), (agg, dz), (pooled, node_grad))
    ]
    own = [
        lax.dynamic_slice(a, (row0, col0), (node_dev, cols)) for a in (mixed, node_grad)
    ]
    return (*own, *grads)


def solution(mesh):
    return jax.shard_map(
        per_device,
        mesh=mesh,
        in_specs=(
            P("dp", None, None),
            P(None, "mp"),
            P("mp", None),
            P("mp", None),
            P("mp", None),
            P("dp", None),
            P("dp", "mp"),
        ),
        out_specs=(P("dp", "mp"), P("dp", "mp"), P("mp", None), P("mp", None), P("mp", None)),
        check_vma=False,
    )
```

```python
import jax
import jax.numpy as jnp
from jax import lax
from jax.sharding import PartitionSpec as P

HD = 64
BF = jnp.bfloat16
F32 = jnp.float32


def attention(texts, w_qkv):
    node_dev, seq_len, width = texts.shape
    heads_here = w_qkv.shape[1] // (3 * HD)
    qkv = jnp.einsum("nld,de->nle", texts, w_qkv, preferred_element_type=F32).astype(BF)
    qkv = qkv.reshape(node_dev, seq_len, heads_here, 3, HD)
    scores = jnp.einsum(
        "nqhd,nkhd->nhqk", qkv[:, :, :, 0, :], qkv[:, :, :, 1, :], preferred_element_type=F32
    )
    probs = jax.nn.softmax(scores / jnp.sqrt(jnp.float32(HD)), axis=-1).astype(BF)
    context = jnp.einsum("nhqk,nkhd->nhd", probs, qkv[:, :, :, 2, :], preferred_element_type=F32)
    return (context / jnp.float32(seq_len)).reshape(node_dev, heads_here * HD).astype(BF)


def hop(x, axis, bit):
    size = lax.axis_size(axis)
    return lax.ppermute(x, axis, [(i, i ^ bit) for i in range(size)])


def gather_dp(block):
    size = lax.axis_size("dp")
    if size > 8:
        return lax.all_gather(block, "dp", axis=0, tiled=True)
    parts = jnp.stack([block] + [hop(block, "dp", i) for i in range(1, size)])
    parts = parts[jnp.arange(size) ^ lax.axis_index("dp")]
    return parts.reshape(size * block.shape[0], block.shape[1])


def gather_mp(block):
    across = hop(block, "mp", 2)
    here = hop(block, "mp", 1)
    there = hop(across, "mp", 1)
    parts = jnp.stack([block, here, across, there])
    return parts[jnp.arange(4) ^ lax.axis_index("mp")]


def gather_all(block):
    return jnp.concatenate(list(gather_mp(gather_dp(block))), axis=1)


def gather_weight(w):
    rows = w.shape[0] // 2
    side = lax.axis_index("dp") % 2
    first = hop(lax.dynamic_slice_in_dim(w, side * rows, rows, 0), "mp", 2)
    second = hop(first, "dp", 1)
    across = [first, second]
    here = hop(w, "mp", 1)
    there = [hop(a, "mp", 1) for a in across]

    def order(pair):
        low = jnp.where(side == 0, pair[0], pair[1])
        high = jnp.where(side == 0, pair[1], pair[0])
        return jnp.concatenate([low, high])

    parts = jnp.stack([w, here, order(across), order(there)])
    return parts[jnp.arange(4) ^ lax.axis_index("mp")].reshape(4 * w.shape[0], w.shape[1])


def dot_t(a, b):
    return lax.dot_general(a, b, (((1,), (1,)), ((), ())), preferred_element_type=F32)


def t_dot(a, b):
    return lax.dot_general(a, b, (((0,), (0,)), ((), ())), preferred_element_type=F32)


def per_device(texts, w_qkv, w_out, w_self, w_neigh, neighbours, cotangent):
    node_dev, seq_len, width = texts.shape
    cols = w_self.shape[0]
    nodes = node_dev * lax.axis_size("dp")
    factor = 1.0 / jnp.sqrt(jnp.float32(nodes))
    row0 = lax.axis_index("dp") * node_dev
    col0 = lax.axis_index("mp") * cols

    def own_cols(a):
        return lax.dynamic_slice_in_dim(a, col0, cols, 1)

    w_out = gather_weight(w_out)
    w_self = gather_weight(w_self)
    w_neigh = gather_weight(w_neigh)
    ids = gather_dp(neighbours)
    cot = gather_all(cotangent)
    my_texts = lax.dynamic_slice_in_dim(texts, col0, cols, 2)
    token_mean = gather_all(jnp.mean(my_texts.astype(F32), axis=1))

    pooled = gather_all(attention(texts, w_qkv))
    embed = (token_mean + jnp.dot(pooled, w_out, preferred_element_type=F32)).astype(BF)
    cnt = jnp.maximum(jnp.sum(ids >= 0, axis=1).astype(F32), 1.0)[:, None]
    counts = jnp.sum(ids[:, :, None] == jnp.arange(nodes)[None, None, :], axis=1).astype(BF)
    agg = (jnp.dot(counts, embed, preferred_element_type=F32) / cnt).astype(BF)
    z = jnp.dot(embed, w_self, preferred_element_type=F32) + jnp.dot(
        agg, w_neigh, preferred_element_type=F32
    )
    out, pullback = jax.vjp(jax.nn.gelu, z)
    mixed = out.astype(BF)
    dz = pullback(cot.astype(F32))[0].astype(BF)
    msg = (dot_t(dz, w_neigh) / cnt).astype(BF)
    node_grad = (dot_t(dz, w_self) + t_dot(counts, msg)).astype(BF)
    grads = [
        t_dot(own_cols(left), right) * factor
        for left, right in ((embed, dz), (agg, dz), (pooled, node_grad))
    ]
    own = [
        lax.dynamic_slice(a, (row0, col0), (node_dev, cols)) for a in (mixed, node_grad)
    ]
    return (*own, *grads)


def solution(mesh):
    return jax.shard_map(
        per_device,
        mesh=mesh,
        in_specs=(
            P("dp", None, None),
            P(None, "mp"),
            P("mp", None),
            P("mp", None),
            P("mp", None),
            P("dp", None),
            P("dp", "mp"),
        ),
        out_specs=(P("dp", "mp"), P("dp", "mp"), P("mp", None), P("mp", None), P("mp", None)),
        check_vma=False,
    )
```

```python
import functools

import jax
import jax.numpy as jnp
from jax import lax
from jax.experimental import pallas as pl
from jax.experimental.pallas import tpu as pltpu
from jax.sharding import PartitionSpec as P

HD = 64
BF = jnp.bfloat16
F32 = jnp.float32
NODES_STEP = 3
WIDE_LIMIT = 256
IDS_COLS = 128
MIB = 1 << 20


def dot_t(a, b):
    return lax.dot_general(a, b, (((1,), (1,)), ((), ())), preferred_element_type=F32)


def t_dot(a, b):
    return lax.dot_general(a, b, (((0,), (0,)), ((), ())), preferred_element_type=F32)


def dot(a, b):
    return jnp.dot(a, b, preferred_element_type=F32)


def attention_kernel(heads, place_ref, x_ref, w_ref, cot_ref, ids_ref, out_ref, wp, acc_p, acc_m):
    step = pl.program_id(0)
    nodes, seq, width = x_ref.shape
    cols = heads * HD

    @pl.when(step == 0)
    def _():
        for part in range(3):
            for h in range(0, heads, 2):
                a = h * 3 * HD + part * HD
                b = a + 3 * HD
                wp[:, part * cols + h * HD : part * cols + (h + 2) * HD] = jnp.concatenate(
                    [w_ref[:, a : a + HD], w_ref[:, b : b + HD]], axis=1
                )

    own = pl.ds(pl.multiple_of(place_ref[0] * cols, 128), cols)
    qkv = dot(x_ref[...].reshape(nodes * seq, width), wp[...]).astype(BF)
    lane = lax.broadcasted_iota(jnp.int32, (seq, cols), 1) // HD
    row = lax.broadcasted_iota(jnp.int32, (heads * seq, cols), 0) // seq
    column = lax.broadcasted_iota(jnp.int32, (heads * seq, cols), 1) // HD
    ones = (row == column).astype(F32).astype(BF)
    zero = jnp.zeros((seq, cols), BF)
    for n in range(nodes):
        at = slice(n * seq, (n + 1) * seq)
        q, k, v = (qkv[at, i * cols : (i + 1) * cols] for i in range(3))
        spread = jnp.concatenate([jnp.where(lane == h, q, zero) for h in range(heads)], axis=0)
        s = dot_t(k, spread)
        e = jnp.exp((s - jnp.max(s, axis=0, keepdims=True)) * (HD**-0.5))
        p = (e * (1.0 / jnp.sum(e, axis=0, keepdims=True))).astype(BF)
        weight = dot(p, ones)
        context = jnp.sum(weight * v.astype(F32), axis=0, keepdims=True)
        acc_p[pl.ds(step * nodes + n, 1), :] = context * (1.0 / seq)
        mean = jnp.sum(x_ref[n, :, own].astype(F32), axis=0, keepdims=True)
        acc_m[pl.ds(step * nodes + n, 1), :] = mean * (1.0 / seq)

    @pl.when(step == pl.num_programs(0) - 1)
    def _():
        out_ref[:, :cols] = acc_p[...].astype(BF)
        out_ref[:, cols : 2 * cols] = cot_ref[...]
        out_ref[:, 2 * cols : 3 * cols] = acc_m[...].astype(BF)
        out_ref[:, 3 * cols :] = ids_ref[...]


def attention(place, texts, w_qkv, cotangent, ids):
    node_dev, seq, width = texts.shape
    cols = w_qkv.shape[1] // 3
    heads = cols // HD
    tokens = node_dev * seq
    return pl.pallas_call(
        functools.partial(attention_kernel, heads),
        out_shape=jax.ShapeDtypeStruct((node_dev, 3 * cols + IDS_COLS), BF),
        grid_spec=pltpu.PrefetchScalarGridSpec(
            num_scalar_prefetch=1,
            grid=(node_dev // NODES_STEP,),
            in_specs=[
                pl.BlockSpec((NODES_STEP, seq, width), lambda i, _: (i, 0, 0)),
                pl.BlockSpec((width, 3 * cols), lambda i, _: (0, 0)),
                pl.BlockSpec((node_dev, cols), lambda i, _: (0, 0)),
                pl.BlockSpec((node_dev, IDS_COLS), lambda i, _: (0, 0)),
            ],
            out_specs=pl.BlockSpec((node_dev, 3 * cols + IDS_COLS), lambda i, _: (0, 0)),
            scratch_shapes=[
                pltpu.VMEM((width, 3 * cols), BF),
                pltpu.VMEM((node_dev, cols), F32),
                pltpu.VMEM((node_dev, cols), F32),
            ],
        ),
        compiler_params=pltpu.CompilerParams(vmem_limit_bytes=40 * MIB),
        cost_estimate=pl.CostEstimate(
            flops=2 * tokens * width * 3 * cols + 8 * tokens * seq * cols,
            bytes_accessed=2 * tokens * width + 6 * width * cols,
            transcendentals=tokens * seq * heads,
        ),
    )(place, texts, w_qkv, cotangent, ids)


def gelu_parts(z):
    root = 0.7978845608028654
    cube = 0.044715
    t = jnp.tanh(root * (z + cube * (z * z * z)))
    half = 0.5 * (1.0 + t)
    slope = half + 0.5 * z * (1.0 - t * t) * (root * (1.0 + 3.0 * cube * (z * z)))
    return z * half, slope


def graph_kernel(
    place_ref, got_ref, *refs
):
    blocks, (mixed_ref, grad_ref, g_self, g_neigh, g_out), scratch = refs[:6], refs[6:11], refs[11:]
    w, pooled, embed, agg, dz, node_grad, wide, sem = scratch
    mp, dp = place_ref[0], place_ref[1]
    rows, cols = g_self.shape[0], g_self.shape[0]
    groups, node_dev = got_ref.shape[1], got_ref.shape[2]
    nodes = groups * node_dev
    parts = got_ref.shape[0]
    width = parts * cols
    own = pl.ds(pl.multiple_of(mp * cols, 128), cols)

    copies = []
    for k in range(3):
        pair = [pltpu.make_async_copy(blocks[k], w.at[k, mp], sem.at[k, 0])]
        for r in range(1, parts):
            pair.append(
                pltpu.make_async_copy(
                    blocks[2 + r].at[pl.ds(k * rows, rows)], w.at[k, mp ^ r], sem.at[k, r]
                )
            )
        copies.append(pair)
    for pair in copies:
        for c in pair:
            c.start()

    def part(m, i, size=cols):
        return got_ref[m, :, :, i : i + size].astype(F32).reshape(nodes, size)

    for m in range(parts):
        pooled[:, m * cols : (m + 1) * cols] = part(m, 0).astype(BF)

    packed = part(0, 3 * cols, IDS_COLS)
    fan = IDS_COLS // 8
    ids = packed[:, :fan] * 16.0 + packed[:, fan : 2 * fan] - 1.0
    cnt = jnp.maximum(jnp.sum((ids >= 0.0).astype(F32), axis=1, keepdims=True), 1.0)
    every = lax.broadcasted_iota(jnp.int32, (nodes, nodes), 1).astype(F32)
    counts = jnp.zeros((nodes, nodes), F32)
    for s in range(fan):
        counts += (ids[:, s : s + 1] == every).astype(F32)
    counts_t = counts.T.astype(BF)
    counts = counts.astype(BF)

    def whole(k):
        return w[k].reshape(width, width)

    for c in copies[0]:
        c.wait()
    sums = dot(pooled[...], whole(0))
    for m in range(parts):
        at = slice(m * cols, (m + 1) * cols)
        embed[:, at] = (part(m, 2 * cols) + sums[:, at]).astype(BF)
    agg[...] = (dot(counts, embed[...]) / cnt).astype(BF)
    for c in copies[1] + copies[2]:
        c.wait()
    z = dot(embed[...], whole(1)) + dot(agg[...], whole(2))
    mixed, slope = gelu_parts(z)
    wide[...] = mixed.reshape(groups, node_dev, width)
    mixed_ref[...] = wide[dp, :, own].astype(BF)
    for m in range(parts):
        at = slice(m * cols, (m + 1) * cols)
        dz[:, at] = (part(m, cols) * slope[:, at]).astype(BF)
    msg = (dot_t(dz[...], whole(2)) / cnt).astype(BF)
    total = dot_t(dz[...], whole(1)) + dot(counts_t, msg)
    node_grad[...] = total.astype(BF)
    wide[...] = total.reshape(groups, node_dev, width)
    grad_ref[...] = wide[dp, :, own].astype(BF)
    factor = 1.0 / jnp.sqrt(jnp.float32(nodes))
    g_self[...] = t_dot(embed[:, own], dz[...]) * factor
    g_neigh[...] = t_dot(agg[:, own], dz[...]) * factor
    g_out[...] = t_dot(pooled[:, own], node_grad[...]) * factor


def graph(place, got, weights, moved):
    parts, groups, node_dev, _ = got.shape
    cols, width = weights[0].shape
    nodes = groups * node_dev
    vmem = pl.BlockSpec(memory_space=pltpu.VMEM)
    slab = jax.ShapeDtypeStruct((node_dev, cols), BF)
    big = jax.ShapeDtypeStruct((cols, width), F32)
    return pl.pallas_call(
        graph_kernel,
        out_shape=(slab, slab, big, big, big),
        in_specs=[pl.BlockSpec(memory_space=pltpu.SMEM), vmem] + [pl.BlockSpec(memory_space=pl.ANY)] * 6,
        out_specs=(vmem,) * 5,
        scratch_shapes=[
            pltpu.VMEM((3, parts, cols, width), BF),
            pltpu.VMEM((nodes, width), BF),
            pltpu.VMEM((nodes, width), BF),
            pltpu.VMEM((nodes, width), BF),
            pltpu.VMEM((nodes, width), BF),
            pltpu.VMEM((nodes, width), BF),
            pltpu.VMEM((groups, node_dev, width), F32),
            pltpu.SemaphoreType.DMA((3, parts)),
        ],
        compiler_params=pltpu.CompilerParams(vmem_limit_bytes=48 * MIB),
        cost_estimate=pl.CostEstimate(
            flops=2 * nodes * width * width * 6, bytes_accessed=10 * MIB, transcendentals=nodes * width
        ),
    )(place, got, *weights, *moved)


def graph_wide(place, got, weights, moved):
    mp, dp = place[0], place[1]
    parts, groups, node_dev, _ = got.shape
    cols, width = weights[0].shape
    nodes = groups * node_dev
    order = jnp.arange(parts) ^ mp
    blocks = jnp.stack([jnp.concatenate(weights), *moved])[order].reshape(parts, 3, cols, width)
    w_out, w_self, w_neigh = (blocks[:, k].reshape(width, width) for k in range(3))

    def part(i):
        return got[..., i * cols : (i + 1) * cols].reshape(parts, nodes, cols).transpose(1, 0, 2).reshape(nodes, width)

    pooled = part(0)
    packed = got[0, :, :, 3 * cols :].reshape(nodes, IDS_COLS).astype(jnp.int32)
    fan = IDS_COLS // 8
    ids = packed[:, :fan] * 16 + packed[:, fan : 2 * fan] - 1
    cnt = jnp.maximum(jnp.sum(ids >= 0, axis=1).astype(F32), 1.0)[:, None]
    counts = jnp.sum(ids[:, :, None] == jnp.arange(nodes)[None, None, :], axis=1).astype(BF)
    embed = (part(2).astype(F32) + dot(pooled, w_out)).astype(BF)
    agg = (dot(counts, embed) / cnt).astype(BF)
    mixed, slope = gelu_parts(dot(embed, w_self) + dot(agg, w_neigh))
    dz = (part(1).astype(F32) * slope).astype(BF)
    msg = (dot_t(dz, w_neigh) / cnt).astype(BF)
    node_grad = (dot_t(dz, w_self) + t_dot(counts, msg)).astype(BF)
    factor = 1.0 / jnp.sqrt(jnp.float32(nodes))
    grads = [
        t_dot(lax.dynamic_slice_in_dim(a, mp * cols, cols, 1), b) * factor
        for a, b in ((embed, dz), (agg, dz), (pooled, node_grad))
    ]
    own = [
        lax.dynamic_slice(a, (dp * node_dev, mp * cols), (node_dev, cols)).astype(BF)
        for a in (mixed, node_grad)
    ]
    return (*own, *grads)


def hop(x, axis, bit):
    return lax.ppermute(x, axis, [(i, i ^ bit) for i in range(lax.axis_size(axis))])


def per_device(texts, w_qkv, w_out, w_self, w_neigh, neighbours, cotangent):
    node_dev = texts.shape[0]
    nodes = node_dev * lax.axis_size("dp")
    place = jnp.stack([lax.axis_index("mp"), lax.axis_index("dp")]).astype(jnp.int32)
    weights = (w_out, w_self, w_neigh)
    stacked = jnp.concatenate(weights)
    across = hop(stacked, "mp", 2)
    here = hop(stacked, "mp", 1)
    there = hop(across, "mp", 1)

    shifted = neighbours + 1
    fan = neighbours.shape[1]
    ids = jnp.concatenate([shifted // 16, shifted % 16], axis=1).astype(BF)
    ids = jnp.pad(ids, ((0, 0), (0, IDS_COLS - 2 * fan)))
    sent = attention(place, texts, w_qkv, cotangent, ids)
    got = lax.all_gather(sent, "dp", axis=0, tiled=False)
    got = lax.all_gather(got, "mp", axis=0, tiled=False)
    body = graph if nodes <= WIDE_LIMIT else graph_wide
    return body(place, got, weights, (here, across, there))


def solution(mesh):
    return jax.shard_map(
        per_device,
        mesh=mesh,
        in_specs=(
            P("dp", None, None),
            P(None, "mp"),
            P("mp", None),
            P("mp", None),
            P("mp", None),
            P("dp", None),
            P("dp", "mp"),
        ),
        out_specs=(P("dp", "mp"), P("dp", "mp"), P("mp", None), P("mp", None), P("mp", None)),
        check_vma=False,
    )
```

```python
import functools

import jax
import jax.numpy as jnp
from jax import lax
from jax.experimental import pallas as pl
from jax.experimental.pallas import tpu as pltpu
from jax.sharding import PartitionSpec as P

HD = 64
BF = jnp.bfloat16
F32 = jnp.float32
NODES_STEP = 3
WIDE_LIMIT = 256
IDS_COLS = 128
MIB = 1 << 20


def dot_t(a, b):
    return lax.dot_general(a, b, (((1,), (1,)), ((), ())), preferred_element_type=F32)


def t_dot(a, b):
    return lax.dot_general(a, b, (((0,), (0,)), ((), ())), preferred_element_type=F32)


def dot(a, b):
    return jnp.dot(a, b, preferred_element_type=F32)


def attention_kernel(heads, place_ref, x_ref, w_ref, cot_ref, ids_ref, out_ref, wp, acc_p, acc_m):
    step = pl.program_id(0)
    nodes, seq, width = x_ref.shape
    cols = heads * HD

    @pl.when(step == 0)
    def _():
        for part in range(3):
            for h in range(0, heads, 2):
                a = h * 3 * HD + part * HD
                b = a + 3 * HD
                wp[:, part * cols + h * HD : part * cols + (h + 2) * HD] = jnp.concatenate(
                    [w_ref[:, a : a + HD], w_ref[:, b : b + HD]], axis=1
                )

    own = pl.ds(pl.multiple_of(place_ref[0] * cols, 128), cols)
    qkv = dot(x_ref[...].reshape(nodes * seq, width), wp[...]).astype(BF)
    lane = lax.broadcasted_iota(jnp.int32, (seq, cols), 1) // HD
    row = lax.broadcasted_iota(jnp.int32, (heads * seq, cols), 0) // seq
    column = lax.broadcasted_iota(jnp.int32, (heads * seq, cols), 1) // HD
    ones = (row == column).astype(F32).astype(BF)
    zero = jnp.zeros((seq, cols), BF)
    for n in range(nodes):
        at = slice(n * seq, (n + 1) * seq)
        q, k, v = (qkv[at, i * cols : (i + 1) * cols] for i in range(3))
        spread = jnp.concatenate([jnp.where(lane == h, q, zero) for h in range(heads)], axis=0)
        s = dot_t(k, spread)
        e = jnp.exp((s - jnp.max(s, axis=0, keepdims=True)) * (HD**-0.5))
        p = (e * (1.0 / jnp.sum(e, axis=0, keepdims=True))).astype(BF)
        weight = dot(p, ones)
        context = jnp.sum(weight * v.astype(F32), axis=0, keepdims=True)
        acc_p[pl.ds(step * nodes + n, 1), :] = context * (1.0 / seq)
        mean = jnp.sum(x_ref[n, :, own].astype(F32), axis=0, keepdims=True)
        acc_m[pl.ds(step * nodes + n, 1), :] = mean * (1.0 / seq)

    @pl.when(step == pl.num_programs(0) - 1)
    def _():
        out_ref[:, :cols] = acc_p[...].astype(BF)
        out_ref[:, cols : 2 * cols] = cot_ref[...]
        out_ref[:, 2 * cols : 3 * cols] = acc_m[...].astype(BF)
        out_ref[:, 3 * cols :] = ids_ref[...]


def attention(place, texts, w_qkv, cotangent, ids):
    node_dev, seq, width = texts.shape
    cols = w_qkv.shape[1] // 3
    heads = cols // HD
    tokens = node_dev * seq
    return pl.pallas_call(
        functools.partial(attention_kernel, heads),
        out_shape=jax.ShapeDtypeStruct((node_dev, 3 * cols + IDS_COLS), BF),
        grid_spec=pltpu.PrefetchScalarGridSpec(
            num_scalar_prefetch=1,
            grid=(node_dev // NODES_STEP,),
            in_specs=[
                pl.BlockSpec((NODES_STEP, seq, width), lambda i, _: (i, 0, 0)),
                pl.BlockSpec((width, 3 * cols), lambda i, _: (0, 0)),
                pl.BlockSpec((node_dev, cols), lambda i, _: (0, 0)),
                pl.BlockSpec((node_dev, IDS_COLS), lambda i, _: (0, 0)),
            ],
            out_specs=pl.BlockSpec((node_dev, 3 * cols + IDS_COLS), lambda i, _: (0, 0)),
            scratch_shapes=[
                pltpu.VMEM((width, 3 * cols), BF),
                pltpu.VMEM((node_dev, cols), F32),
                pltpu.VMEM((node_dev, cols), F32),
            ],
        ),
        compiler_params=pltpu.CompilerParams(vmem_limit_bytes=60 * MIB),
        cost_estimate=pl.CostEstimate(
            flops=2 * tokens * width * 3 * cols + 8 * tokens * seq * cols,
            bytes_accessed=2 * tokens * width + 6 * width * cols,
            transcendentals=tokens * seq * heads,
        ),
    )(place, texts, w_qkv, cotangent, ids)


def gelu_parts(z):
    root = 0.7978845608028654
    cube = 0.044715
    t = jnp.tanh(root * (z + cube * (z * z * z)))
    half = 0.5 * (1.0 + t)
    slope = half + 0.5 * z * (1.0 - t * t) * (root * (1.0 + 3.0 * cube * (z * z)))
    return z * half, slope


def graph_kernel(
    place_ref, got_ref, *refs
):
    blocks, (mixed_ref, grad_ref, g_self, g_neigh, g_out), scratch = refs[:6], refs[6:11], refs[11:]
    w, pooled, embed, agg, dz, node_grad, wide, sem = scratch
    mp, dp = place_ref[0], place_ref[1]
    rows, cols = g_self.shape[0], g_self.shape[0]
    groups, parts, node_dev, _ = got_ref.shape
    nodes = groups * node_dev
    width = parts * cols
    own = pl.ds(pl.multiple_of(mp * cols, 128), cols)

    copies = []
    for k in range(3):
        pair = [pltpu.make_async_copy(blocks[k], w.at[k, mp], sem.at[k, 0])]
        for r in range(1, parts):
            pair.append(
                pltpu.make_async_copy(
                    blocks[2 + r].at[pl.ds(k * rows, rows)], w.at[k, mp ^ r], sem.at[k, r]
                )
            )
        copies.append(pair)
    for pair in copies:
        for c in pair:
            c.start()

    def part(m, i, size=cols):
        return got_ref[:, m, :, i : i + size].astype(F32).reshape(nodes, size)

    for m in range(parts):
        pooled[:, m * cols : (m + 1) * cols] = part(m, 0).astype(BF)

    packed = part(0, 3 * cols, IDS_COLS)
    fan = IDS_COLS // 8
    ids = packed[:, :fan] * 16.0 + packed[:, fan : 2 * fan] - 1.0
    cnt = jnp.maximum(jnp.sum((ids >= 0.0).astype(F32), axis=1, keepdims=True), 1.0)
    every = lax.broadcasted_iota(jnp.int32, (nodes, nodes), 1).astype(F32)
    counts = jnp.zeros((nodes, nodes), F32)
    for s in range(fan):
        counts += (ids[:, s : s + 1] == every).astype(F32)
    counts_t = counts.T.astype(BF)
    counts = counts.astype(BF)

    def whole(k):
        return w[k].reshape(width, width)

    for c in copies[0]:
        c.wait()
    sums = dot(pooled[...], whole(0))
    for m in range(parts):
        at = slice(m * cols, (m + 1) * cols)
        embed[:, at] = (part(m, 2 * cols) + sums[:, at]).astype(BF)
    agg[...] = (dot(counts, embed[...]) / cnt).astype(BF)
    for c in copies[1] + copies[2]:
        c.wait()
    z = dot(embed[...], whole(1)) + dot(agg[...], whole(2))
    mixed, slope = gelu_parts(z)
    wide[...] = mixed.reshape(groups, node_dev, width)
    mixed_ref[...] = wide[dp, :, own].astype(BF)
    for m in range(parts):
        at = slice(m * cols, (m + 1) * cols)
        dz[:, at] = (part(m, cols) * slope[:, at]).astype(BF)
    msg = (dot_t(dz[...], whole(2)) / cnt).astype(BF)
    total = dot_t(dz[...], whole(1)) + dot(counts_t, msg)
    node_grad[...] = total.astype(BF)
    wide[...] = total.reshape(groups, node_dev, width)
    grad_ref[...] = wide[dp, :, own].astype(BF)
    factor = 1.0 / jnp.sqrt(jnp.float32(nodes))
    g_self[...] = t_dot(embed[:, own], dz[...]) * factor
    g_neigh[...] = t_dot(agg[:, own], dz[...]) * factor
    g_out[...] = t_dot(pooled[:, own], node_grad[...]) * factor


def graph(place, got, weights, moved):
    groups, parts, node_dev, _ = got.shape
    cols, width = weights[0].shape
    nodes = groups * node_dev
    vmem = pl.BlockSpec(memory_space=pltpu.VMEM)
    slab = jax.ShapeDtypeStruct((node_dev, cols), BF)
    big = jax.ShapeDtypeStruct((cols, width), F32)
    return pl.pallas_call(
        graph_kernel,
        out_shape=(slab, slab, big, big, big),
        in_specs=[pl.BlockSpec(memory_space=pltpu.SMEM), vmem] + [pl.BlockSpec(memory_space=pl.ANY)] * 6,
        out_specs=(vmem,) * 5,
        scratch_shapes=[
            pltpu.VMEM((3, parts, cols, width), BF),
            pltpu.VMEM((nodes, width), BF),
            pltpu.VMEM((nodes, width), BF),
            pltpu.VMEM((nodes, width), BF),
            pltpu.VMEM((nodes, width), BF),
            pltpu.VMEM((nodes, width), BF),
            pltpu.VMEM((groups, node_dev, width), F32),
            pltpu.SemaphoreType.DMA((3, parts)),
        ],
        compiler_params=pltpu.CompilerParams(vmem_limit_bytes=60 * MIB),
        cost_estimate=pl.CostEstimate(
            flops=2 * nodes * width * width * 6, bytes_accessed=10 * MIB, transcendentals=nodes * width
        ),
    )(place, got, *weights, *moved)


def graph_wide(place, got, weights, moved):
    mp, dp = place[0], place[1]
    groups, parts, node_dev, _ = got.shape
    cols, width = weights[0].shape
    nodes = groups * node_dev
    order = jnp.arange(parts) ^ mp
    blocks = jnp.stack([jnp.concatenate(weights), *moved])[order].reshape(parts, 3, cols, width)
    w_out, w_self, w_neigh = (blocks[:, k].reshape(width, width) for k in range(3))

    def part(i):
        block = got[..., i * cols : (i + 1) * cols].transpose(0, 2, 1, 3)
        return block.reshape(nodes, width)

    pooled = part(0)
    packed = got[:, 0, :, 3 * cols :].reshape(nodes, IDS_COLS).astype(jnp.int32)
    fan = IDS_COLS // 8
    ids = packed[:, :fan] * 16 + packed[:, fan : 2 * fan] - 1
    cnt = jnp.maximum(jnp.sum(ids >= 0, axis=1).astype(F32), 1.0)[:, None]
    counts = jnp.sum(ids[:, :, None] == jnp.arange(nodes)[None, None, :], axis=1).astype(BF)
    embed = (part(2).astype(F32) + dot(pooled, w_out)).astype(BF)
    agg = (dot(counts, embed) / cnt).astype(BF)
    mixed, slope = gelu_parts(dot(embed, w_self) + dot(agg, w_neigh))
    dz = (part(1).astype(F32) * slope).astype(BF)
    msg = (dot_t(dz, w_neigh) / cnt).astype(BF)
    node_grad = (dot_t(dz, w_self) + t_dot(counts, msg)).astype(BF)
    factor = 1.0 / jnp.sqrt(jnp.float32(nodes))
    grads = [
        t_dot(lax.dynamic_slice_in_dim(a, mp * cols, cols, 1), b) * factor
        for a, b in ((embed, dz), (agg, dz), (pooled, node_grad))
    ]
    own = [
        lax.dynamic_slice(a, (dp * node_dev, mp * cols), (node_dev, cols)).astype(BF)
        for a in (mixed, node_grad)
    ]
    return (*own, *grads)


def stack_kernel(a, b, c, out, sem):
    rows = a.shape[0]
    copies = [
        pltpu.make_async_copy(ref, out.at[pl.ds(k * rows, rows)], sem.at[k])
        for k, ref in enumerate((a, b, c))
    ]
    for copy in copies:
        copy.start()
    for copy in copies:
        copy.wait()


def stack(weights):
    rows, width = weights[0].shape
    anywhere = pl.BlockSpec(memory_space=pl.ANY)
    return pl.pallas_call(
        stack_kernel,
        out_shape=jax.ShapeDtypeStruct((3 * rows, width), BF),
        in_specs=[anywhere] * 3,
        out_specs=anywhere,
        scratch_shapes=[pltpu.SemaphoreType.DMA((3,))],
        compiler_params=pltpu.CompilerParams(vmem_limit_bytes=60 * MIB),
    )(*weights)


def hop(x, axis, bit):
    return lax.ppermute(x, axis, [(i, i ^ bit) for i in range(lax.axis_size(axis))])


def per_device(texts, w_qkv, w_out, w_self, w_neigh, neighbours, cotangent):
    node_dev = texts.shape[0]
    nodes = node_dev * lax.axis_size("dp")
    place = jnp.stack([lax.axis_index("mp"), lax.axis_index("dp")]).astype(jnp.int32)
    weights = (w_out, w_self, w_neigh)
    stacked = stack(weights)
    across = hop(stacked, "mp", 2)
    here = hop(stacked, "mp", 1)
    there = hop(across, "mp", 1)

    shifted = neighbours + 1
    fan = neighbours.shape[1]
    ids = jnp.concatenate([shifted // 16, shifted % 16], axis=1).astype(BF)
    ids = jnp.pad(ids, ((0, 0), (0, IDS_COLS - 2 * fan)))
    sent = attention(place, texts, w_qkv, cotangent, ids)
    got = lax.all_gather(sent, ("dp", "mp"), axis=0, tiled=False)
    got = got.reshape(lax.axis_size("dp"), lax.axis_size("mp"), *sent.shape)
    body = graph if nodes <= WIDE_LIMIT else graph_wide
    return body(place, got, weights, (here, across, there))


def solution(mesh):
    return jax.shard_map(
        per_device,
        mesh=mesh,
        in_specs=(
            P("dp", None, None),
            P(None, "mp"),
            P("mp", None),
            P("mp", None),
            P("mp", None),
            P("dp", None),
            P("dp", "mp"),
        ),
        out_specs=(P("dp", "mp"), P("dp", "mp"), P("mp", None), P("mp", None), P("mp", None)),
        check_vma=False,
    )
```

```python
import functools

import jax
import jax.numpy as jnp
from jax import lax
from jax.experimental import pallas as pl
from jax.experimental.pallas import tpu as pltpu
from jax.sharding import PartitionSpec as P

HD = 64
BF = jnp.bfloat16
F32 = jnp.float32
NODES_STEP = 3
WIDE_LIMIT = 256
IDS_COLS = 128
MIB = 1 << 20


def dot_t(a, b):
    return lax.dot_general(a, b, (((1,), (1,)), ((), ())), preferred_element_type=F32)


def t_dot(a, b):
    return lax.dot_general(a, b, (((0,), (0,)), ((), ())), preferred_element_type=F32)


def dot(a, b):
    return jnp.dot(a, b, preferred_element_type=F32)


def attention_kernel(heads, place_ref, x_ref, w_ref, cot_ref, ids_ref, out_ref, wp, acc_p, acc_m):
    step = pl.program_id(0)
    nodes, seq, width = x_ref.shape
    cols = heads * HD

    @pl.when(step == 0)
    def _():
        for part in range(3):
            for h in range(0, heads, 2):
                a = h * 3 * HD + part * HD
                b = a + 3 * HD
                wp[:, part * cols + h * HD : part * cols + (h + 2) * HD] = jnp.concatenate(
                    [w_ref[:, a : a + HD], w_ref[:, b : b + HD]], axis=1
                )

    own = pl.ds(pl.multiple_of(place_ref[0] * cols, 128), cols)
    qkv = dot(x_ref[...].reshape(nodes * seq, width), wp[...]).astype(BF)
    lane = lax.broadcasted_iota(jnp.int32, (seq, cols), 1) // HD
    row = lax.broadcasted_iota(jnp.int32, (heads * seq, cols), 0) // seq
    column = lax.broadcasted_iota(jnp.int32, (heads * seq, cols), 1) // HD
    ones = (row == column).astype(F32).astype(BF)
    zero = jnp.zeros((seq, cols), BF)
    for n in range(nodes):
        at = slice(n * seq, (n + 1) * seq)
        q, k, v = (qkv[at, i * cols : (i + 1) * cols] for i in range(3))
        spread = jnp.concatenate([jnp.where(lane == h, q, zero) for h in range(heads)], axis=0)
        s = dot_t(k, spread)
        e = jnp.exp((s - jnp.max(s, axis=0, keepdims=True)) * (HD**-0.5))
        p = (e * (1.0 / jnp.sum(e, axis=0, keepdims=True))).astype(BF)
        weight = dot(p, ones)
        context = jnp.sum(weight * v.astype(F32), axis=0, keepdims=True)
        acc_p[pl.ds(step * nodes + n, 1), :] = context * (1.0 / seq)
        mean = jnp.sum(x_ref[n, :, own].astype(F32), axis=0, keepdims=True)
        acc_m[pl.ds(step * nodes + n, 1), :] = mean * (1.0 / seq)

    @pl.when(step == pl.num_programs(0) - 1)
    def _():
        out_ref[:, :cols] = acc_p[...].astype(BF)
        out_ref[:, cols : 2 * cols] = cot_ref[...]
        out_ref[:, 2 * cols : 3 * cols] = acc_m[...].astype(BF)
        out_ref[:, 3 * cols :] = ids_ref[...]


def attention(place, texts, w_qkv, cotangent, ids):
    node_dev, seq, width = texts.shape
    cols = w_qkv.shape[1] // 3
    heads = cols // HD
    tokens = node_dev * seq
    return pl.pallas_call(
        functools.partial(attention_kernel, heads),
        out_shape=jax.ShapeDtypeStruct((node_dev, 3 * cols + IDS_COLS), BF),
        grid_spec=pltpu.PrefetchScalarGridSpec(
            num_scalar_prefetch=1,
            grid=(node_dev // NODES_STEP,),
            in_specs=[
                pl.BlockSpec((NODES_STEP, seq, width), lambda i, _: (i, 0, 0)),
                pl.BlockSpec((width, 3 * cols), lambda i, _: (0, 0)),
                pl.BlockSpec((node_dev, cols), lambda i, _: (0, 0)),
                pl.BlockSpec((node_dev, IDS_COLS), lambda i, _: (0, 0)),
            ],
            out_specs=pl.BlockSpec((node_dev, 3 * cols + IDS_COLS), lambda i, _: (0, 0)),
            scratch_shapes=[
                pltpu.VMEM((width, 3 * cols), BF),
                pltpu.VMEM((node_dev, cols), F32),
                pltpu.VMEM((node_dev, cols), F32),
            ],
        ),
        compiler_params=pltpu.CompilerParams(vmem_limit_bytes=60 * MIB),
        cost_estimate=pl.CostEstimate(
            flops=2 * tokens * width * 3 * cols + 8 * tokens * seq * cols,
            bytes_accessed=2 * tokens * width + 6 * width * cols,
            transcendentals=tokens * seq * heads,
        ),
    )(place, texts, w_qkv, cotangent, ids)


def gelu_parts(z):
    root = 0.7978845608028654
    cube = 0.044715
    t = jnp.tanh(root * (z + cube * (z * z * z)))
    half = 0.5 * (1.0 + t)
    slope = half + 0.5 * z * (1.0 - t * t) * (root * (1.0 + 3.0 * cube * (z * z)))
    return z * half, slope


def graph_kernel(place_ref, names_ref, *refs):
    parts = 4
    got, blocks, refs = refs[:parts], refs[parts : parts + 6], refs[parts + 6 :]
    (mixed_ref, grad_ref, g_self, g_neigh, g_out), scratch = refs[:5], refs[5:]
    w, pooled, embed, agg, dz, node_grad, mean, cot, sem = scratch
    mp = place_ref[0]
    groups, node_dev, _ = got[0].shape
    nodes = groups * node_dev
    rows = cols = g_self.shape[0]
    width = parts * cols

    def place(r):
        return pl.ds(pl.multiple_of((mp ^ r) * cols, 128), cols)

    own = place(0)
    copies = []
    for k in range(3):
        pair = [pltpu.make_async_copy(blocks[k], w.at[k, mp], sem.at[k, 0])]
        for r in range(1, parts):
            pair.append(
                pltpu.make_async_copy(
                    blocks[2 + r].at[pl.ds(k * rows, rows)], w.at[k, mp ^ r], sem.at[k, r]
                )
            )
        copies.append(pair)
    for pair in copies:
        for c in pair:
            c.start()

    def part(r, i, size=cols):
        return got[r][:, :, i : i + size].astype(F32).reshape(nodes, size)

    for r in range(parts):
        pooled[:, place(r)] = part(r, 0).astype(BF)
        cot[:, place(r)] = part(r, cols)
        mean[:, place(r)] = part(r, 2 * cols)

    packed = part(0, 3 * cols, IDS_COLS)
    fan = IDS_COLS // 8
    ids = packed[:, :fan] * 16.0 + packed[:, fan : 2 * fan] - 1.0
    cnt = jnp.maximum(jnp.sum((ids >= 0.0).astype(F32), axis=1, keepdims=True), 1.0)
    names = names_ref[...]
    counts = jnp.zeros((nodes, nodes), F32)
    for s in range(fan):
        counts += (ids[:, s : s + 1] == names).astype(F32)
    counts_t = counts.T.astype(BF)
    counts = counts.astype(BF)

    def whole(k):
        return w[k].reshape(width, width)

    for c in copies[0]:
        c.wait()
    embed[...] = (mean[...] + dot(pooled[...], whole(0))).astype(BF)
    agg[...] = (dot(counts, embed[...]) / cnt).astype(BF)
    for c in copies[1] + copies[2]:
        c.wait()
    z = dot(embed[...], whole(1)) + dot(agg[...], whole(2))
    mixed, slope = gelu_parts(z)
    mean[:node_dev, :] = mixed[:node_dev, :]
    mixed_ref[...] = mean[:node_dev, own].astype(BF)
    dz[...] = (cot[...] * slope).astype(BF)
    msg = (dot_t(dz[...], whole(2)) / cnt).astype(BF)
    total = dot_t(dz[...], whole(1)) + dot(counts_t, msg)
    node_grad[...] = total.astype(BF)
    cot[:node_dev, :] = total[:node_dev, :]
    grad_ref[...] = cot[:node_dev, own].astype(BF)
    factor = 1.0 / jnp.sqrt(jnp.float32(nodes))
    g_self[...] = t_dot(embed[:, own], dz[...]) * factor
    g_neigh[...] = t_dot(agg[:, own], dz[...]) * factor
    g_out[...] = t_dot(pooled[:, own], node_grad[...]) * factor


def graph(place, names, got, weights, moved):
    parts = len(got)
    groups, node_dev, _ = got[0].shape
    cols, width = weights[0].shape
    nodes = groups * node_dev
    vmem = pl.BlockSpec(memory_space=pltpu.VMEM)
    slab = jax.ShapeDtypeStruct((node_dev, cols), BF)
    big = jax.ShapeDtypeStruct((cols, width), F32)
    return pl.pallas_call(
        graph_kernel,
        out_shape=(slab, slab, big, big, big),
        in_specs=[pl.BlockSpec(memory_space=pltpu.SMEM)]
        + [vmem] * (1 + parts)
        + [pl.BlockSpec(memory_space=pl.ANY)] * 6,
        out_specs=(vmem,) * 5,
        scratch_shapes=[
            pltpu.VMEM((3, parts, cols, width), BF),
            pltpu.VMEM((nodes, width), BF),
            pltpu.VMEM((nodes, width), BF),
            pltpu.VMEM((nodes, width), BF),
            pltpu.VMEM((nodes, width), BF),
            pltpu.VMEM((nodes, width), BF),
            pltpu.VMEM((nodes, width), F32),
            pltpu.VMEM((nodes, width), F32),
            pltpu.SemaphoreType.DMA((3, parts)),
        ],
        compiler_params=pltpu.CompilerParams(vmem_limit_bytes=36 * MIB),
        cost_estimate=pl.CostEstimate(
            flops=2 * nodes * width * width * 6, bytes_accessed=10 * MIB, transcendentals=nodes * width
        ),
    )(place, names, *got, *weights, *moved)


def graph_wide(place, names, got, weights, moved):
    mp = place[0]
    parts = len(got)
    groups, node_dev, _ = got[0].shape
    cols, width = weights[0].shape
    nodes = groups * node_dev
    order = jnp.arange(parts) ^ mp
    blocks = jnp.stack([jnp.concatenate(weights), *moved])[order].reshape(parts, 3, cols, width)
    w_out, w_self, w_neigh = (blocks[:, k].reshape(width, width) for k in range(3))

    def part(i):
        block = jnp.stack([g[:, :, i * cols : (i + 1) * cols] for g in got])[order]
        return block.transpose(1, 2, 0, 3).reshape(nodes, width)

    pooled = part(0)
    packed = got[0][:, :, 3 * cols :].reshape(nodes, IDS_COLS).astype(jnp.int32)
    fan = IDS_COLS // 8
    ids = packed[:, :fan] * 16 + packed[:, fan : 2 * fan] - 1
    cnt = jnp.maximum(jnp.sum(ids >= 0, axis=1).astype(F32), 1.0)[:, None]
    names = names.astype(jnp.int32)[:, None, :]
    counts = jnp.sum(ids[:, :, None] == names, axis=1).astype(BF)
    embed = (part(2).astype(F32) + dot(pooled, w_out)).astype(BF)
    agg = (dot(counts, embed) / cnt).astype(BF)
    mixed, slope = gelu_parts(dot(embed, w_self) + dot(agg, w_neigh))
    dz = (part(1).astype(F32) * slope).astype(BF)
    msg = (dot_t(dz, w_neigh) / cnt).astype(BF)
    node_grad = (dot_t(dz, w_self) + t_dot(counts, msg)).astype(BF)
    factor = 1.0 / jnp.sqrt(jnp.float32(nodes))

    def own(a):
        return lax.dynamic_slice_in_dim(a, mp * cols, cols, 1)

    grads = [t_dot(own(a), b) * factor for a, b in ((embed, dz), (agg, dz), (pooled, node_grad))]
    return (own(mixed[:node_dev]).astype(BF), own(node_grad[:node_dev]), *grads)


def stack_kernel(a, b, c, out, sem):
    rows = a.shape[0]
    copies = [
        pltpu.make_async_copy(ref, out.at[pl.ds(k * rows, rows)], sem.at[k])
        for k, ref in enumerate((a, b, c))
    ]
    for copy in copies:
        copy.start()
    for copy in copies:
        copy.wait()


def stack(weights):
    rows, width = weights[0].shape
    return pl.pallas_call(
        stack_kernel,
        out_shape=jax.ShapeDtypeStruct((3 * rows, width), BF),
        in_specs=[pl.BlockSpec(memory_space=pltpu.VMEM)] * 3,
        out_specs=pl.BlockSpec(memory_space=pl.ANY),
        scratch_shapes=[pltpu.SemaphoreType.DMA((3,))],
        compiler_params=pltpu.CompilerParams(vmem_limit_bytes=60 * MIB),
    )(*weights)


def hop(x, axis, bit):
    return lax.ppermute(x, axis, [(i, i ^ bit) for i in range(lax.axis_size(axis))])


def per_device(texts, w_qkv, w_out, w_self, w_neigh, neighbours, cotangent):
    node_dev = texts.shape[0]
    nodes = node_dev * lax.axis_size("dp")
    place = jnp.stack([lax.axis_index("mp"), lax.axis_index("dp")]).astype(jnp.int32)
    weights = (w_out, w_self, w_neigh)
    stacked = stack(weights)
    across = hop(stacked, "mp", 2)
    here = hop(stacked, "mp", 1)

    shifted = neighbours + 1
    fan = neighbours.shape[1]
    ids = jnp.concatenate([shifted // 16, shifted % 16], axis=1).astype(BF)
    ids = jnp.pad(ids, ((0, 0), (0, IDS_COLS - 2 * fan)))
    sent = attention(place, texts, w_qkv, cotangent, ids)[None]

    order, bit = [0], lax.axis_size("dp") // 2
    while bit:
        sent = jnp.concatenate([sent, hop(sent, "dp", bit)])
        order = order + [i ^ bit for i in order]
        bit //= 2
    owners = jnp.array(order, jnp.int32) ^ lax.axis_index("dp")
    names = owners[:, None] * node_dev + jnp.arange(node_dev)[None, :]
    names = names.reshape(1, nodes).astype(F32)
    across, sent = lax.optimization_barrier((across, sent))
    there = hop(across, "mp", 1)
    got_across = hop(sent, "mp", 2)
    got = (sent, hop(sent, "mp", 1), got_across, hop(got_across, "mp", 1))
    body = graph if nodes <= WIDE_LIMIT else graph_wide
    return body(place, names, got, weights, (here, across, there))


def solution(mesh):
    return jax.shard_map(
        per_device,
        mesh=mesh,
        in_specs=(
            P("dp", None, None),
            P(None, "mp"),
            P("mp", None),
            P("mp", None),
            P("mp", None),
            P("dp", None),
            P("dp", "mp"),
        ),
        out_specs=(P("dp", "mp"), P("dp", "mp"), P("mp", None), P("mp", None), P("mp", None)),
        check_vma=False,
    )
```

```python
import functools

import jax
import jax.numpy as jnp
from jax import lax
from jax.experimental import pallas as pl
from jax.experimental.pallas import tpu as pltpu
from jax.sharding import PartitionSpec as P

HD = 64
BF = jnp.bfloat16
F32 = jnp.float32
NODES_STEP = 3
WIDE_LIMIT = 256
IDS_COLS = 128
MIB = 1 << 20


def dot_t(a, b):
    return lax.dot_general(a, b, (((1,), (1,)), ((), ())), preferred_element_type=F32)


def t_dot(a, b):
    return lax.dot_general(a, b, (((0,), (0,)), ((), ())), preferred_element_type=F32)


def dot(a, b):
    return jnp.dot(a, b, preferred_element_type=F32)


def attention_kernel(heads, x_ref, w_ref, cot_ref, ids_ref, out_ref, wp, acc_p, acc_m):
    step = pl.program_id(0)
    nodes, seq, width = x_ref.shape
    cols = heads * HD

    @pl.when(step == 0)
    def _():
        for part in range(3):
            for h in range(0, heads, 2):
                a = h * 3 * HD + part * HD
                b = a + 3 * HD
                wp[:, part * cols + h * HD : part * cols + (h + 2) * HD] = jnp.concatenate(
                    [w_ref[:, a : a + HD], w_ref[:, b : b + HD]], axis=1
                )

    own = pl.ds(pl.multiple_of(lax.axis_index("mp") * cols, 128), cols)
    qkv = dot(x_ref[...].reshape(nodes * seq, width), wp[...]).astype(BF)
    lane = lax.broadcasted_iota(jnp.int32, (seq, cols), 1) // HD
    row = lax.broadcasted_iota(jnp.int32, (heads * seq, cols), 0) // seq
    column = lax.broadcasted_iota(jnp.int32, (heads * seq, cols), 1) // HD
    ones = (row == column).astype(F32).astype(BF)
    zero = jnp.zeros((seq, cols), BF)
    for n in range(nodes):
        at = slice(n * seq, (n + 1) * seq)
        q, k, v = (qkv[at, i * cols : (i + 1) * cols] for i in range(3))
        spread = jnp.concatenate([jnp.where(lane == h, q, zero) for h in range(heads)], axis=0)
        s = dot_t(k, spread)
        e = jnp.exp((s - jnp.max(s, axis=0, keepdims=True)) * (HD**-0.5))
        p = (e * (1.0 / jnp.sum(e, axis=0, keepdims=True))).astype(BF)
        weight = dot(p, ones)
        context = jnp.sum(weight * v.astype(F32), axis=0, keepdims=True)
        acc_p[pl.ds(step * nodes + n, 1), :] = context * (1.0 / seq)
        mean = jnp.sum(x_ref[n, :, own].astype(F32), axis=0, keepdims=True)
        acc_m[pl.ds(step * nodes + n, 1), :] = mean * (1.0 / seq)

    @pl.when(step == pl.num_programs(0) - 1)
    def _():
        out_ref[:, :cols] = acc_p[...].astype(BF)
        out_ref[:, cols : 2 * cols] = cot_ref[...]
        out_ref[:, 2 * cols : 3 * cols] = acc_m[...].astype(BF)
        shifted = ids_ref[...] + 1
        rows, fan = shifted.shape
        blank = jnp.zeros((rows, IDS_COLS - 2 * fan), F32)
        pair = [(shifted >> 4).astype(F32), (shifted & 15).astype(F32)]
        out_ref[:, 3 * cols :] = jnp.concatenate(pair + [blank], axis=1).astype(BF)


def attention(texts, w_qkv, cotangent, neighbours):
    node_dev, seq, width = texts.shape
    cols = w_qkv.shape[1] // 3
    heads = cols // HD
    tokens = node_dev * seq
    return pl.pallas_call(
        functools.partial(attention_kernel, heads),
        out_shape=jax.ShapeDtypeStruct((node_dev, 3 * cols + IDS_COLS), BF),
        grid=(node_dev // NODES_STEP,),
        in_specs=[
            pl.BlockSpec((NODES_STEP, seq, width), lambda i: (i, 0, 0)),
            pl.BlockSpec((width, 3 * cols), lambda i: (0, 0)),
            pl.BlockSpec((node_dev, cols), lambda i: (0, 0)),
            pl.BlockSpec(neighbours.shape, lambda i: (0, 0)),
        ],
        out_specs=pl.BlockSpec((node_dev, 3 * cols + IDS_COLS), lambda i: (0, 0)),
        scratch_shapes=[
            pltpu.VMEM((width, 3 * cols), BF),
            pltpu.VMEM((node_dev, cols), F32),
            pltpu.VMEM((node_dev, cols), F32),
        ],
        compiler_params=pltpu.CompilerParams(vmem_limit_bytes=60 * MIB),
        cost_estimate=pl.CostEstimate(
            flops=2 * tokens * width * 3 * cols + 8 * tokens * seq * cols,
            bytes_accessed=2 * tokens * width + 6 * width * cols,
            transcendentals=tokens * seq * heads,
        ),
    )(texts, w_qkv, cotangent, neighbours)


def gelu_parts(z):
    root = 0.7978845608028654
    cube = 0.044715
    t = jnp.tanh(root * (z + cube * (z * z * z)))
    half = 0.5 * (1.0 + t)
    slope = half + 0.5 * z * (1.0 - t * t) * (root * (1.0 + 3.0 * cube * (z * z)))
    return z * half, slope


def graph_kernel(order, fan, *refs):
    parts = 4
    got, blocks, refs = refs[:parts], refs[parts : parts + 12], refs[parts + 12 :]
    (mixed_ref, grad_ref, g_self, g_neigh, g_out), scratch = refs[:5], refs[5:]
    w, pooled, embed, agg, dz, node_grad, mean, cot, sem = scratch
    mp, dp = lax.axis_index("mp"), lax.axis_index("dp")
    side = dp % 2
    groups, node_dev, _ = got[0].shape
    nodes = groups * node_dev
    cols = g_self.shape[0]
    width = parts * cols

    def place(r):
        return pl.ds(pl.multiple_of((mp ^ r) * cols, 128), cols)

    own = place(0)
    copies = []
    for r in range(parts):
        kinds = (0, 1, 2) if r < 2 else (0, 1 + side, 2 - side)
        for i, k in enumerate(kinds):
            copies.append(pltpu.make_async_copy(blocks[3 * r + i], w.at[k, mp ^ r], sem.at[i, r]))
    copies = copies[::3], copies[1::3] + copies[2::3]
    for c in copies[0] + copies[1]:
        c.start()

    def part(r, i, size=cols):
        return got[r][:, :, i : i + size].astype(F32).reshape(nodes, size)

    for r in range(parts):
        pooled[:, place(r)] = part(r, 0).astype(BF)
        cot[:, place(r)] = part(r, cols)
        mean[:, place(r)] = part(r, 2 * cols)

    packed = part(0, 3 * cols, IDS_COLS)
    ids = packed[:, :fan] * 16.0 + packed[:, fan : 2 * fan] - 1.0
    cnt = jnp.maximum(jnp.sum((ids >= 0.0).astype(F32), axis=1, keepdims=True), 1.0)
    place_of = lax.broadcasted_iota(jnp.int32, (1, nodes), 1)
    names = place_of
    for i, o in enumerate(order):
        shift = ((dp ^ o) - i) * node_dev
        inside = (place_of >= i * node_dev) & (place_of < (i + 1) * node_dev)
        names = jnp.where(inside, place_of + shift, names)
    names = names.astype(F32)
    counts = jnp.zeros((nodes, nodes), F32)
    for s in range(fan):
        counts += (ids[:, s : s + 1] == names).astype(F32)
    counts_t = counts.T.astype(BF)
    counts = counts.astype(BF)

    def whole(k):
        return w[k].reshape(width, width)

    for c in copies[0]:
        c.wait()
    embed[...] = (mean[...] + dot(pooled[...], whole(0))).astype(BF)
    agg[...] = (dot(counts, embed[...]) / cnt).astype(BF)
    for c in copies[1]:
        c.wait()
    z = dot(embed[...], whole(1)) + dot(agg[...], whole(2))
    mixed, slope = gelu_parts(z)
    mean[:node_dev, :] = mixed[:node_dev, :]
    mixed_ref[...] = mean[:node_dev, own].astype(BF)
    dz[...] = (cot[...] * slope).astype(BF)
    msg = (dot_t(dz[...], whole(2)) / cnt).astype(BF)
    total = dot_t(dz[...], whole(1)) + dot(counts_t, msg)
    node_grad[...] = total.astype(BF)
    cot[:node_dev, :] = total[:node_dev, :]
    grad_ref[...] = cot[:node_dev, own].astype(BF)
    factor = 1.0 / jnp.sqrt(jnp.float32(nodes))
    g_self[...] = t_dot(embed[:, own], dz[...]) * factor
    g_neigh[...] = t_dot(agg[:, own], dz[...]) * factor
    g_out[...] = t_dot(pooled[:, own], node_grad[...]) * factor


def graph(order, fan, got, weights):
    parts = len(got)
    groups, node_dev, _ = got[0].shape
    cols, width = weights[0][0].shape
    nodes = groups * node_dev
    vmem = pl.BlockSpec(memory_space=pltpu.VMEM)
    slab = jax.ShapeDtypeStruct((node_dev, cols), BF)
    big = jax.ShapeDtypeStruct((cols, width), F32)
    return pl.pallas_call(
        functools.partial(graph_kernel, order, fan),
        out_shape=(slab, slab, big, big, big),
        in_specs=[vmem] * parts + [pl.BlockSpec(memory_space=pl.ANY)] * (3 * parts),
        out_specs=(vmem,) * 5,
        scratch_shapes=[
            pltpu.VMEM((3, parts, cols, width), BF),
            pltpu.VMEM((nodes, width), BF),
            pltpu.VMEM((nodes, width), BF),
            pltpu.VMEM((nodes, width), BF),
            pltpu.VMEM((nodes, width), BF),
            pltpu.VMEM((nodes, width), BF),
            pltpu.VMEM((nodes, width), F32),
            pltpu.VMEM((nodes, width), F32),
            pltpu.SemaphoreType.DMA((3, parts)),
        ],
        compiler_params=pltpu.CompilerParams(vmem_limit_bytes=36 * MIB),
        cost_estimate=pl.CostEstimate(
            flops=2 * nodes * width * width * 6, bytes_accessed=10 * MIB, transcendentals=nodes * width
        ),
    )(*got, *sum(weights, ()))


def graph_wide(order, fan, got, weights):
    mp, dp = lax.axis_index("mp"), lax.axis_index("dp")
    parts = len(got)
    groups, node_dev, _ = got[0].shape
    cols, width = weights[0][0].shape
    nodes = groups * node_dev
    owners = jnp.array(order, jnp.int32) ^ dp
    names = (owners[:, None] * node_dev + jnp.arange(node_dev)[None, :]).reshape(1, 1, nodes)
    order = jnp.arange(parts) ^ mp
    even = dp % 2 == 0
    kinds = [
        [group[0], jnp.where(even, group[1], group[2]), jnp.where(even, group[2], group[1])]
        for group in weights[2:]
    ]
    blocks = [*weights[:2], *kinds]
    w_out, w_self, w_neigh = (
        jnp.stack([group[k] for group in blocks])[order].reshape(width, width) for k in range(3)
    )

    def part(i):
        block = jnp.stack([g[:, :, i * cols : (i + 1) * cols] for g in got])[order]
        return block.transpose(1, 2, 0, 3).reshape(nodes, width)

    pooled = part(0)
    packed = got[0][:, :, 3 * cols :].reshape(nodes, IDS_COLS).astype(jnp.int32)
    ids = packed[:, :fan] * 16 + packed[:, fan : 2 * fan] - 1
    cnt = jnp.maximum(jnp.sum(ids >= 0, axis=1).astype(F32), 1.0)[:, None]
    counts = jnp.sum(ids[:, :, None] == names, axis=1).astype(BF)
    embed = (part(2).astype(F32) + dot(pooled, w_out)).astype(BF)
    agg = (dot(counts, embed) / cnt).astype(BF)
    mixed, slope = gelu_parts(dot(embed, w_self) + dot(agg, w_neigh))
    dz = (part(1).astype(F32) * slope).astype(BF)
    msg = (dot_t(dz, w_neigh) / cnt).astype(BF)
    node_grad = (dot_t(dz, w_self) + t_dot(counts, msg)).astype(BF)
    factor = 1.0 / jnp.sqrt(jnp.float32(nodes))

    def own(a):
        return lax.dynamic_slice_in_dim(a, mp * cols, cols, 1)

    grads = [t_dot(own(a), b) * factor for a, b in ((embed, dz), (agg, dz), (pooled, node_grad))]
    return (own(mixed[:node_dev]).astype(BF), own(node_grad[:node_dev]), *grads)


def join_kernel(*refs):
    out, at = refs[-1], 0
    for ref in refs[:-1]:
        out[at : at + ref.shape[0]] = ref[...]
        at += ref.shape[0]


def join(*blocks):
    count = sum(b.shape[0] for b in blocks)
    if count > 8:
        return jnp.concatenate(blocks)
    vmem = pl.BlockSpec(memory_space=pltpu.VMEM)
    return pl.pallas_call(
        join_kernel,
        out_shape=jax.ShapeDtypeStruct((count, *blocks[0].shape[1:]), BF),
        in_specs=[vmem] * len(blocks),
        out_specs=vmem,
        compiler_params=pltpu.CompilerParams(vmem_limit_bytes=8 * MIB),
    )(*blocks)


def hop(x, axis, bit):
    return lax.ppermute(x, axis, [(i, i ^ bit) for i in range(lax.axis_size(axis))])


def gather_dp(block):
    size = lax.axis_size("dp")
    if size == 8:
        block = join(block, *[hop(block, "dp", i) for i in (2, 4, 6)])
        order, bit = [0, 2, 4, 6], 1
    else:
        order, bit = [0], size // 2
    while bit:
        block = join(block, hop(block, "dp", bit))
        order = order + [i ^ bit for i in order]
        bit //= 2
    return block, order


def per_device(texts, w_qkv, w_out, w_self, w_neigh, neighbours, cotangent):
    node_dev, fan = neighbours.shape
    nodes = node_dev * lax.axis_size("dp")
    even = lax.axis_index("dp") % 2 == 0
    x_half = hop(jnp.where(even, w_self, w_neigh), "mp", 2)
    x_out = hop(w_out, "mp", 2)
    own = (w_out, w_self, w_neigh)

    sent = attention(texts, w_qkv, cotangent, neighbours)[None]
    sent, order = gather_dp(sent)
    y_half = hop(x_half, "dp", 1)
    here = tuple(hop(a, "mp", 1) for a in own)
    across = (x_out, x_half, y_half)
    there = tuple(hop(a, "mp", 1) for a in across)

    got_across = hop(sent, "mp", 2)
    got = (sent, hop(sent, "mp", 1), got_across, hop(got_across, "mp", 1))
    body = graph if nodes <= WIDE_LIMIT else graph_wide
    return body(order, fan, got, (own, here, across, there))


def solution(mesh):
    return jax.shard_map(
        per_device,
        mesh=mesh,
        in_specs=(
            P("dp", None, None),
            P(None, "mp"),
            P("mp", None),
            P("mp", None),
            P("mp", None),
            P("dp", None),
            P("dp", "mp"),
        ),
        out_specs=(P("dp", "mp"), P("dp", "mp"), P("mp", None), P("mp", None), P("mp", None)),
        check_vma=False,
    )
```

```python
import functools

import jax
import jax.numpy as jnp
from jax import lax
from jax.experimental import pallas as pl
from jax.experimental.pallas import tpu as pltpu
from jax.sharding import PartitionSpec as P

HD = 64
BF = jnp.bfloat16
F32 = jnp.float32
NODES_STEP = 3
WIDE_LIMIT = 256
IDS_COLS = 128
IDS_AT = 32
LOG2E = 1.4426950408889634
ATTENTION_VMEM = 58
MIB = 1 << 20


def dot_t(a, b):
    return lax.dot_general(a, b, (((1,), (1,)), ((), ())), preferred_element_type=F32)


def t_dot(a, b):
    return lax.dot_general(a, b, (((0,), (0,)), ((), ())), preferred_element_type=F32)


def dot(a, b):
    return jnp.dot(a, b, preferred_element_type=F32)


def attend(qkv, heads, seq, ones_ref, row, acc_p):
    cols = heads * HD
    lane = lax.broadcasted_iota(jnp.int32, (seq, cols), 1) // HD
    zero = jnp.zeros((seq, cols), BF)
    for n in range(NODES_STEP):
        at = slice(n * seq, (n + 1) * seq)
        q, k, v = (qkv[at, i * cols : (i + 1) * cols] for i in range(3))
        spread = jnp.concatenate([jnp.where(lane == h, q, zero) for h in range(heads)], axis=0)
        s = dot_t(k, spread)
        e = jnp.exp2((s - jnp.max(s, axis=0, keepdims=True)) * (HD**-0.5 * LOG2E))
        p = (e * (1.0 / jnp.sum(e, axis=0, keepdims=True))).astype(BF)
        context = jnp.sum(dot(p, ones_ref[...]) * v.astype(F32), axis=0, keepdims=True)
        acc_p[pl.ds(row + n, 1), :] = context * (1.0 / seq)


def attention_kernel(heads, x_ref, w_ref, cot_ref, ids_ref, out_ref, wp, ones, last, acc_p, acc_m):
    step = pl.program_id(0)
    nodes, seq, width = x_ref.shape
    node_dev = cot_ref.shape[0]
    cols = heads * HD
    half = NODES_STEP * seq

    @pl.when(step == 0)
    def _():
        for part in range(3):
            for h in range(0, heads, 2):
                a = h * 3 * HD + part * HD
                b = a + 3 * HD
                wp[:, part * cols + h * HD : part * cols + (h + 2) * HD] = jnp.concatenate(
                    [w_ref[:, a : a + HD], w_ref[:, b : b + HD]], axis=1
                )
        row = lax.broadcasted_iota(jnp.int32, (heads * seq, cols), 0) // seq
        column = lax.broadcasted_iota(jnp.int32, (heads * seq, cols), 1) // HD
        ones[...] = (row == column).astype(F32).astype(BF)
        last[...] = jnp.zeros_like(last)

    own = pl.ds(pl.multiple_of(lax.axis_index("mp") * cols, 128), cols)
    begin = step * nodes

    def product(first):
        return dot(x_ref[first : first + NODES_STEP].reshape(half, width), wp[...]).astype(BF)

    def attend_at(qkv, row):
        attend(qkv, heads, seq, ones, row, acc_p)

    before = jnp.where(step == 0, node_dev, begin - NODES_STEP)
    qkv = product(0)
    attend_at(last, before)
    last[...] = product(NODES_STEP)
    attend_at(qkv, begin)
    for n in range(nodes):
        mean = jnp.sum(x_ref[n, :, own].astype(F32), axis=0, keepdims=True)
        acc_m[pl.ds(begin + n, 1), :] = mean * (1.0 / seq)

    @pl.when(step == pl.num_programs(0) - 1)
    def _():
        attend_at(last, node_dev - NODES_STEP)
        out_ref[:, :cols] = acc_p[:node_dev, :].astype(BF)
        out_ref[:, cols : 2 * cols] = cot_ref[...]
        out_ref[:, 2 * cols : 3 * cols] = acc_m[...].astype(BF)
        shifted = ids_ref[...] + 1
        fan = shifted.shape[0]
        blank = jnp.zeros((fan, IDS_COLS - 2 * IDS_AT), F32)
        gap = jnp.zeros((fan, IDS_AT - node_dev), F32)
        high, low = (shifted >> 4).astype(F32), (shifted & 15).astype(F32)
        packed = jnp.concatenate([high, gap, low, gap, blank], axis=1)
        rest = jnp.zeros((node_dev - fan, IDS_COLS), F32)
        out_ref[:, 3 * cols :] = jnp.concatenate([packed, rest], axis=0).astype(BF)


def attention(texts, w_qkv, cotangent, ids):
    node_dev, seq, width = texts.shape
    cols = w_qkv.shape[1] // 3
    heads = cols // HD
    tokens = node_dev * seq
    nodes = 2 * NODES_STEP
    return pl.pallas_call(
        functools.partial(attention_kernel, heads),
        out_shape=jax.ShapeDtypeStruct((node_dev, 3 * cols + IDS_COLS), BF),
        grid=(node_dev // nodes,),
        in_specs=[
            pl.BlockSpec((nodes, seq, width), lambda i: (i, 0, 0)),
            pl.BlockSpec((width, 3 * cols), lambda i: (0, 0)),
            pl.BlockSpec((node_dev, cols), lambda i: (0, 0)),
            pl.BlockSpec(ids.shape, lambda i: (0, 0)),
        ],
        out_specs=pl.BlockSpec((node_dev, 3 * cols + IDS_COLS), lambda i: (0, 0)),
        scratch_shapes=[
            pltpu.VMEM((width, 3 * cols), BF),
            pltpu.VMEM((heads * seq, cols), BF),
            pltpu.VMEM((NODES_STEP * seq, 3 * cols), BF),
            pltpu.VMEM((node_dev + 8, cols), F32),
            pltpu.VMEM((node_dev, cols), F32),
        ],
        compiler_params=pltpu.CompilerParams(vmem_limit_bytes=ATTENTION_VMEM * MIB),
        cost_estimate=pl.CostEstimate(
            flops=2 * tokens * width * 3 * cols + 8 * tokens * seq * cols,
            bytes_accessed=2 * tokens * width + 6 * width * cols,
            transcendentals=tokens * seq * heads,
        ),
    )(texts, w_qkv, cotangent, ids)


def gelu_parts(z):
    root = 0.7978845608028654
    cube = 0.044715
    t = jnp.tanh(root * (z + cube * (z * z * z)))
    half = 0.5 * (1.0 + t)
    slope = half + 0.5 * z * (1.0 - t * t) * (root * (1.0 + 3.0 * cube * (z * z)))
    return z * half, slope


def graph_kernel(order, fan, *refs):
    parts = 4
    got, blocks, refs = refs[:parts], refs[parts : parts + 12], refs[parts + 12 :]
    (mixed_ref, grad_ref, g_self, g_neigh, g_out), scratch = refs[:5], refs[5:]
    w, pooled, embed, agg, dz, node_grad, mean, cot, sem = scratch
    mp, dp = lax.axis_index("mp"), lax.axis_index("dp")
    side = (dp // 2) % 2
    groups, node_dev, _ = got[0].shape
    nodes = groups * node_dev
    cols = g_self.shape[0]
    width = parts * cols

    def place(r):
        return pl.ds(pl.multiple_of((mp ^ r) * cols, 128), cols)

    own = place(0)
    copies = []
    for r in range(parts):
        kinds = (0, 1, 2) if r < 2 else (0, 1 + side, 2 - side)
        for i, k in enumerate(kinds):
            copies.append(pltpu.make_async_copy(blocks[3 * r + i], w.at[k, mp ^ r], sem.at[i, r]))
    copies = copies[::3], copies[1::3] + copies[2::3]
    for c in copies[0] + copies[1]:
        c.start()

    def part(r, i, size=cols):
        return got[r][:, :, i : i + size].astype(F32).reshape(nodes, size)

    for r in range(parts):
        pooled[:, place(r)] = part(r, 0).astype(BF)
        cot[:, place(r)] = part(r, cols)
        mean[:, place(r)] = part(r, 2 * cols)

    packed = got[0][:, :, 3 * cols :].astype(F32)
    ids = jnp.concatenate(
        [
            packed[i, :fan, :node_dev] * 16.0 + packed[i, :fan, IDS_AT : IDS_AT + node_dev] - 1.0
            for i in range(groups)
        ],
        axis=1,
    )
    place_of = lax.broadcasted_iota(jnp.int32, (nodes, 1), 0)
    names = place_of
    for i, o in enumerate(order):
        shift = ((dp ^ o) - i) * node_dev
        inside = (place_of >= i * node_dev) & (place_of < (i + 1) * node_dev)
        names = jnp.where(inside, place_of + shift, names)
    names = names.astype(F32)
    counts_t = jnp.zeros((nodes, nodes), F32)
    for s in range(fan):
        counts_t += (ids[s : s + 1, :] == names).astype(F32)
    counts = counts_t.T
    cnt = jnp.maximum(jnp.sum(counts, axis=1, keepdims=True), 1.0)
    counts, counts_t = counts.astype(BF), counts_t.astype(BF)

    def whole(k):
        return w[k].reshape(width, width)

    for c in copies[0]:
        c.wait()
    embed[...] = (mean[...] + dot(pooled[...], whole(0))).astype(BF)
    agg[...] = (dot(counts, embed[...]) / cnt).astype(BF)
    for c in copies[1]:
        c.wait()
    z = dot(embed[...], whole(1)) + dot(agg[...], whole(2))
    mixed, slope = gelu_parts(z)
    mean[:node_dev, :] = mixed[:node_dev, :]
    mixed_ref[...] = mean[:node_dev, own].astype(BF)
    dz[...] = (cot[...] * slope).astype(BF)
    msg = (dot_t(dz[...], whole(2)) / cnt).astype(BF)
    total = dot_t(dz[...], whole(1)) + dot(counts_t, msg)
    node_grad[...] = total.astype(BF)
    cot[:node_dev, :] = total[:node_dev, :]
    grad_ref[...] = cot[:node_dev, own].astype(BF)
    factor = 1.0 / jnp.sqrt(jnp.float32(nodes))
    g_self[...] = t_dot(embed[:, own], dz[...]) * factor
    g_neigh[...] = t_dot(agg[:, own], dz[...]) * factor
    g_out[...] = t_dot(pooled[:, own], node_grad[...]) * factor


def graph(order, fan, got, weights):
    parts = len(got)
    groups, node_dev, _ = got[0].shape
    cols, width = weights[0][0].shape
    nodes = groups * node_dev
    vmem = pl.BlockSpec(memory_space=pltpu.VMEM)
    slab = jax.ShapeDtypeStruct((node_dev, cols), BF)
    big = jax.ShapeDtypeStruct((cols, width), F32)
    return pl.pallas_call(
        functools.partial(graph_kernel, order, fan),
        out_shape=(slab, slab, big, big, big),
        in_specs=[vmem] * parts + [pl.BlockSpec(memory_space=pl.ANY)] * (3 * parts),
        out_specs=(vmem,) * 5,
        scratch_shapes=[
            pltpu.VMEM((3, parts, cols, width), BF),
            pltpu.VMEM((nodes, width), BF),
            pltpu.VMEM((nodes, width), BF),
            pltpu.VMEM((nodes, width), BF),
            pltpu.VMEM((nodes, width), BF),
            pltpu.VMEM((nodes, width), BF),
            pltpu.VMEM((nodes, width), F32),
            pltpu.VMEM((nodes, width), F32),
            pltpu.SemaphoreType.DMA((3, parts)),
        ],
        compiler_params=pltpu.CompilerParams(vmem_limit_bytes=36 * MIB),
        cost_estimate=pl.CostEstimate(
            flops=2 * nodes * width * width * 6, bytes_accessed=10 * MIB, transcendentals=nodes * width
        ),
    )(*got, *sum(weights, ()))


def graph_wide(order, fan, got, weights):
    mp, dp = lax.axis_index("mp"), lax.axis_index("dp")
    parts = len(got)
    groups, node_dev, _ = got[0].shape
    cols, width = weights[0][0].shape
    nodes = groups * node_dev
    owners = jnp.array(order, jnp.int32) ^ dp
    names = (owners[:, None] * node_dev + jnp.arange(node_dev)[None, :]).reshape(1, 1, nodes)
    order = jnp.arange(parts) ^ mp
    even = (dp // 2) % 2 == 0
    kinds = [
        [group[0], jnp.where(even, group[1], group[2]), jnp.where(even, group[2], group[1])]
        for group in weights[2:]
    ]
    blocks = [*weights[:2], *kinds]
    w_out, w_self, w_neigh = (
        jnp.stack([group[k] for group in blocks])[order].reshape(width, width) for k in range(3)
    )

    def part(i):
        block = jnp.stack([g[:, :, i * cols : (i + 1) * cols] for g in got])[order]
        return block.transpose(1, 2, 0, 3).reshape(nodes, width)

    pooled = part(0)
    packed = got[0][:, :fan, 3 * cols :].astype(jnp.int32)
    ids = packed[:, :, :node_dev] * 16 + packed[:, :, IDS_AT : IDS_AT + node_dev] - 1
    ids = ids.transpose(0, 2, 1).reshape(nodes, fan)
    cnt = jnp.maximum(jnp.sum(ids >= 0, axis=1).astype(F32), 1.0)[:, None]
    counts = jnp.sum(ids[:, :, None] == names, axis=1).astype(BF)
    embed = (part(2).astype(F32) + dot(pooled, w_out)).astype(BF)
    agg = (dot(counts, embed) / cnt).astype(BF)
    mixed, slope = gelu_parts(dot(embed, w_self) + dot(agg, w_neigh))
    dz = (part(1).astype(F32) * slope).astype(BF)
    msg = (dot_t(dz, w_neigh) / cnt).astype(BF)
    node_grad = (dot_t(dz, w_self) + t_dot(counts, msg)).astype(BF)
    factor = 1.0 / jnp.sqrt(jnp.float32(nodes))

    def own(a):
        return lax.dynamic_slice_in_dim(a, mp * cols, cols, 1)

    grads = [t_dot(own(a), b) * factor for a, b in ((embed, dz), (agg, dz), (pooled, node_grad))]
    return (own(mixed[:node_dev]).astype(BF), own(node_grad[:node_dev]), *grads)


def join_kernel(*refs):
    out, at = refs[-1], 0
    for ref in refs[:-1]:
        out[at : at + ref.shape[0]] = ref[...]
        at += ref.shape[0]


def join(*blocks):
    count = sum(b.shape[0] for b in blocks)
    if count > 8:
        return jnp.concatenate(blocks)
    vmem = pl.BlockSpec(memory_space=pltpu.VMEM)
    return pl.pallas_call(
        join_kernel,
        out_shape=jax.ShapeDtypeStruct((count, *blocks[0].shape[1:]), BF),
        in_specs=[vmem] * len(blocks),
        out_specs=vmem,
        compiler_params=pltpu.CompilerParams(vmem_limit_bytes=8 * MIB),
    )(*blocks)


def pick_kernel(first, second, out, sem):
    side = (lax.axis_index("dp") // 2) % 2

    @pl.when(side == 0)
    def _():
        copy = pltpu.make_async_copy(first, out, sem)
        copy.start()
        copy.wait()

    @pl.when(side == 1)
    def _():
        copy = pltpu.make_async_copy(second, out, sem)
        copy.start()
        copy.wait()


def pick(first, second):
    anywhere = pl.BlockSpec(memory_space=pl.ANY)
    return pl.pallas_call(
        pick_kernel,
        out_shape=jax.ShapeDtypeStruct(first.shape, first.dtype),
        in_specs=[anywhere, anywhere],
        out_specs=pl.BlockSpec(memory_space=pltpu.VMEM),
        scratch_shapes=[pltpu.SemaphoreType.DMA],
        compiler_params=pltpu.CompilerParams(vmem_limit_bytes=60 * MIB),
    )(first, second)


def hop(x, axis, bit):
    return lax.ppermute(x, axis, [(i, i ^ bit) for i in range(lax.axis_size(axis))])


def gather_dp(block, later):
    size = lax.axis_size("dp")
    if size == 8:
        block = join(block, *[hop(block, "dp", i) for i in (2, 4, 6)])
        order, bit = [0, 2, 4, 6], 1
        block, later = lax.optimization_barrier((block, later))
    else:
        order, bit = [0], size // 2
    while bit:
        block = join(block, hop(block, "dp", bit))
        order = order + [i ^ bit for i in order]
        bit //= 2
    return block, order, later


def per_device(texts, w_qkv, w_out, w_self, w_neigh, neighbours, cotangent):
    node_dev, fan = neighbours.shape
    nodes = node_dev * lax.axis_size("dp")
    x_half = hop(pick(w_self, w_neigh), "mp", 2)
    x_out = hop(w_out, "mp", 2)
    own = (w_out, w_self, w_neigh)

    sent = attention(texts, w_qkv, cotangent, neighbours.T)[None]
    sent, order, late = gather_dp(sent, own)
    z_half = hop(x_half, "dp", 2)
    here = tuple(hop(a, "mp", 1) for a in late)
    across = (x_out, x_half, z_half)
    there = tuple(hop(a, "mp", 1) for a in across)

    got_across = hop(sent, "mp", 2)
    got = (sent, hop(sent, "mp", 1), got_across, hop(got_across, "mp", 1))
    body = graph if nodes <= WIDE_LIMIT else graph_wide
    return body(order, fan, got, (own, here, across, there))


def solution(mesh):
    return jax.shard_map(
        per_device,
        mesh=mesh,
        in_specs=(
            P("dp", None, None),
            P(None, "mp"),
            P("mp", None),
            P("mp", None),
            P("mp", None),
            P("dp", None),
            P("dp", "mp"),
        ),
        out_specs=(P("dp", "mp"), P("dp", "mp"), P("mp", None), P("mp", None), P("mp", None)),
        check_vma=False,
    )
```

```python
import functools

import jax
import jax.numpy as jnp
from jax import lax
from jax.experimental import pallas as pl
from jax.experimental.pallas import tpu as pltpu
from jax.sharding import PartitionSpec as P

HD = 64
BF = jnp.bfloat16
F32 = jnp.float32
NODES_STEP = 6
WIDE_LIMIT = 256
IDS_COLS = 128
IDS_AT = 32
LOG2E = 1.4426950408889634
ATTENTION_VMEM = 58
MIB = 1 << 20


def dot_t(a, b):
    return lax.dot_general(a, b, (((1,), (1,)), ((), ())), preferred_element_type=F32)


def t_dot(a, b):
    return lax.dot_general(a, b, (((0,), (0,)), ((), ())), preferred_element_type=F32)


def dot(a, b):
    return jnp.dot(a, b, preferred_element_type=F32)


def attend(q, k, v, heads):
    seq, cols = q.shape
    lane = lax.broadcasted_iota(jnp.int32, (seq, cols), 1) // HD
    zero = jnp.zeros((seq, cols), BF)
    spread = jnp.concatenate([jnp.where(lane == h, k, zero) for h in range(heads)], axis=0)
    s = dot_t(spread, q).reshape(heads, seq, seq)
    e = jnp.exp2((s - jnp.max(s, axis=1, keepdims=True)) * (HD**-0.5 * LOG2E))
    p = (e * (1.0 / jnp.sum(e, axis=1, keepdims=True))).astype(BF)
    weight = jnp.sum(p.astype(F32), axis=2, keepdims=True)
    left = lax.broadcasted_iota(jnp.int32, (seq, 2 * HD), 1) < HD
    pairs = [jnp.where(left, weight[h], weight[h + 1]) for h in range(0, heads, 2)]
    context = jnp.concatenate(pairs, axis=1) * v.astype(F32)
    return jnp.sum(context, axis=0, keepdims=True) * (1.0 / seq)


def attention_kernel(heads, x_ref, w_ref, cot_ref, ids_ref, out_ref, wp, acc_p, acc_m):
    step = pl.program_id(0)
    nodes, seq, width = x_ref.shape
    node_dev = cot_ref.shape[0]
    cols = heads * HD

    @pl.when(step == 0)
    def _():
        for part in range(3):
            for h in range(0, heads, 2):
                a = h * 3 * HD + part * HD
                b = a + 3 * HD
                wp[:, part * cols + h * HD : part * cols + (h + 2) * HD] = jnp.concatenate(
                    [w_ref[:, a : a + HD], w_ref[:, b : b + HD]], axis=1
                )

    own = pl.ds(pl.multiple_of(lax.axis_index("mp") * cols, 128), cols)
    qkv = dot(x_ref[...].reshape(nodes * seq, width), wp[...]).astype(BF)
    for n in range(nodes):
        at = slice(n * seq, (n + 1) * seq)
        row = pl.ds(step * nodes + n, 1)
        acc_p[row, :] = attend(*(qkv[at, i * cols : (i + 1) * cols] for i in range(3)), heads)
        mean = jnp.sum(x_ref[n, :, own].astype(F32), axis=0, keepdims=True)
        acc_m[row, :] = mean * (1.0 / seq)

    @pl.when(step == pl.num_programs(0) - 1)
    def _():
        out_ref[:, :cols] = acc_p[...].astype(BF)
        out_ref[:, cols : 2 * cols] = cot_ref[...]
        out_ref[:, 2 * cols : 3 * cols] = acc_m[...].astype(BF)
        shifted = ids_ref[...] + 1
        fan = shifted.shape[0]
        blank = jnp.zeros((fan, IDS_COLS - 2 * IDS_AT), F32)
        gap = jnp.zeros((fan, IDS_AT - node_dev), F32)
        high, low = (shifted >> 4).astype(F32), (shifted & 15).astype(F32)
        packed = jnp.concatenate([high, gap, low, gap, blank], axis=1)
        rest = jnp.zeros((node_dev - fan, IDS_COLS), F32)
        out_ref[:, 3 * cols :] = jnp.concatenate([packed, rest], axis=0).astype(BF)


def attention(texts, w_qkv, cotangent, ids):
    node_dev, seq, width = texts.shape
    cols = w_qkv.shape[1] // 3
    heads = cols // HD
    tokens = node_dev * seq
    nodes = NODES_STEP
    return pl.pallas_call(
        functools.partial(attention_kernel, heads),
        out_shape=jax.ShapeDtypeStruct((node_dev, 3 * cols + IDS_COLS), BF),
        grid=(node_dev // nodes,),
        in_specs=[
            pl.BlockSpec((nodes, seq, width), lambda i: (i, 0, 0)),
            pl.BlockSpec((width, 3 * cols), lambda i: (0, 0)),
            pl.BlockSpec((node_dev, cols), lambda i: (0, 0)),
            pl.BlockSpec(ids.shape, lambda i: (0, 0)),
        ],
        out_specs=pl.BlockSpec((node_dev, 3 * cols + IDS_COLS), lambda i: (0, 0)),
        scratch_shapes=[
            pltpu.VMEM((width, 3 * cols), BF),
            pltpu.VMEM((node_dev, cols), F32),
            pltpu.VMEM((node_dev, cols), F32),
        ],
        compiler_params=pltpu.CompilerParams(vmem_limit_bytes=ATTENTION_VMEM * MIB),
        cost_estimate=pl.CostEstimate(
            flops=2 * tokens * width * 3 * cols + 8 * tokens * seq * cols,
            bytes_accessed=2 * tokens * width + 6 * width * cols,
            transcendentals=tokens * seq * heads,
        ),
    )(texts, w_qkv, cotangent, ids)


def gelu_parts(z):
    root = 0.7978845608028654
    cube = 0.044715
    t = jnp.tanh(root * (z + cube * (z * z * z)))
    half = 0.5 * (1.0 + t)
    slope = half + 0.5 * z * (1.0 - t * t) * (root * (1.0 + 3.0 * cube * (z * z)))
    return z * half, slope


def graph_kernel(order, fan, *refs):
    parts = 4
    got, blocks, refs = refs[:parts], refs[parts : parts + 12], refs[parts + 12 :]
    (mixed_ref, grad_ref, g_self, g_neigh, g_out), scratch = refs[:5], refs[5:]
    w, pooled, embed, agg, dz, node_grad, mean, cot, sem = scratch
    mp, dp = lax.axis_index("mp"), lax.axis_index("dp")
    side = (dp // 2) % 2
    groups, node_dev, _ = got[0].shape
    nodes = groups * node_dev
    cols = g_self.shape[0]
    width = parts * cols

    def place(r):
        return pl.ds(pl.multiple_of((mp ^ r) * cols, 128), cols)

    own = place(0)
    copies = []
    for r in range(parts):
        kinds = (0, 1, 2) if r < 2 else (0, 1 + side, 2 - side)
        for i, k in enumerate(kinds):
            copies.append(pltpu.make_async_copy(blocks[3 * r + i], w.at[k, mp ^ r], sem.at[i, r]))
    copies = copies[::3], copies[1::3] + copies[2::3]
    for c in copies[0] + copies[1]:
        c.start()

    def part(r, i, size=cols):
        return got[r][:, :, i : i + size].astype(F32).reshape(nodes, size)

    for r in range(parts):
        pooled[:, place(r)] = part(r, 0).astype(BF)
        cot[:, place(r)] = part(r, cols)
        mean[:, place(r)] = part(r, 2 * cols)

    packed = got[0][:, :, 3 * cols :].astype(F32)
    ids = jnp.concatenate(
        [
            packed[i, :fan, :node_dev] * 16.0 + packed[i, :fan, IDS_AT : IDS_AT + node_dev] - 1.0
            for i in range(groups)
        ],
        axis=1,
    )
    place_of = lax.broadcasted_iota(jnp.int32, (nodes, 1), 0)
    names = place_of
    for i, o in enumerate(order):
        shift = ((dp ^ o) - i) * node_dev
        inside = (place_of >= i * node_dev) & (place_of < (i + 1) * node_dev)
        names = jnp.where(inside, place_of + shift, names)
    names = names.astype(F32)
    counts_t = jnp.zeros((nodes, nodes), F32)
    for s in range(fan):
        counts_t += (ids[s : s + 1, :] == names).astype(F32)
    counts = counts_t.T
    cnt = jnp.maximum(jnp.sum(counts, axis=1, keepdims=True), 1.0)
    counts, counts_t = counts.astype(BF), counts_t.astype(BF)

    def whole(k):
        return w[k].reshape(width, width)

    for c in copies[0]:
        c.wait()
    embed[...] = (mean[...] + dot(pooled[...], whole(0))).astype(BF)
    agg[...] = (dot(counts, embed[...]) / cnt).astype(BF)
    for c in copies[1]:
        c.wait()
    z = dot(embed[...], whole(1)) + dot(agg[...], whole(2))
    mixed, slope = gelu_parts(z)
    mean[:node_dev, :] = mixed[:node_dev, :]
    mixed_ref[...] = mean[:node_dev, own].astype(BF)
    dz[...] = (cot[...] * slope).astype(BF)
    msg = (dot_t(dz[...], whole(2)) / cnt).astype(BF)
    total = dot_t(dz[...], whole(1)) + dot(counts_t, msg)
    node_grad[...] = total.astype(BF)
    cot[:node_dev, :] = total[:node_dev, :]
    grad_ref[...] = cot[:node_dev, own].astype(BF)
    factor = 1.0 / jnp.sqrt(jnp.float32(nodes))
    g_self[...] = t_dot(embed[:, own], dz[...]) * factor
    g_neigh[...] = t_dot(agg[:, own], dz[...]) * factor
    g_out[...] = t_dot(pooled[:, own], node_grad[...]) * factor


def graph(order, fan, got, weights):
    parts = len(got)
    groups, node_dev, _ = got[0].shape
    cols, width = weights[0][0].shape
    nodes = groups * node_dev
    vmem = pl.BlockSpec(memory_space=pltpu.VMEM)
    slab = jax.ShapeDtypeStruct((node_dev, cols), BF)
    big = jax.ShapeDtypeStruct((cols, width), F32)
    return pl.pallas_call(
        functools.partial(graph_kernel, order, fan),
        out_shape=(slab, slab, big, big, big),
        in_specs=[vmem] * parts + [pl.BlockSpec(memory_space=pl.ANY)] * (3 * parts),
        out_specs=(vmem,) * 5,
        scratch_shapes=[
            pltpu.VMEM((3, parts, cols, width), BF),
            pltpu.VMEM((nodes, width), BF),
            pltpu.VMEM((nodes, width), BF),
            pltpu.VMEM((nodes, width), BF),
            pltpu.VMEM((nodes, width), BF),
            pltpu.VMEM((nodes, width), BF),
            pltpu.VMEM((nodes, width), F32),
            pltpu.VMEM((nodes, width), F32),
            pltpu.SemaphoreType.DMA((3, parts)),
        ],
        compiler_params=pltpu.CompilerParams(vmem_limit_bytes=36 * MIB),
        cost_estimate=pl.CostEstimate(
            flops=2 * nodes * width * width * 6, bytes_accessed=10 * MIB, transcendentals=nodes * width
        ),
    )(*got, *sum(weights, ()))


def graph_wide(order, fan, got, weights):
    mp, dp = lax.axis_index("mp"), lax.axis_index("dp")
    parts = len(got)
    groups, node_dev, _ = got[0].shape
    cols, width = weights[0][0].shape
    nodes = groups * node_dev
    owners = jnp.array(order, jnp.int32) ^ dp
    names = (owners[:, None] * node_dev + jnp.arange(node_dev)[None, :]).reshape(1, 1, nodes)
    order = jnp.arange(parts) ^ mp
    even = (dp // 2) % 2 == 0
    kinds = [
        [group[0], jnp.where(even, group[1], group[2]), jnp.where(even, group[2], group[1])]
        for group in weights[2:]
    ]
    blocks = [*weights[:2], *kinds]
    w_out, w_self, w_neigh = (
        jnp.stack([group[k] for group in blocks])[order].reshape(width, width) for k in range(3)
    )

    def part(i):
        block = jnp.stack([g[:, :, i * cols : (i + 1) * cols] for g in got])[order]
        return block.transpose(1, 2, 0, 3).reshape(nodes, width)

    pooled = part(0)
    packed = got[0][:, :fan, 3 * cols :].astype(jnp.int32)
    ids = packed[:, :, :node_dev] * 16 + packed[:, :, IDS_AT : IDS_AT + node_dev] - 1
    ids = ids.transpose(0, 2, 1).reshape(nodes, fan)
    cnt = jnp.maximum(jnp.sum(ids >= 0, axis=1).astype(F32), 1.0)[:, None]
    counts = jnp.sum(ids[:, :, None] == names, axis=1).astype(BF)
    embed = (part(2).astype(F32) + dot(pooled, w_out)).astype(BF)
    agg = (dot(counts, embed) / cnt).astype(BF)
    mixed, slope = gelu_parts(dot(embed, w_self) + dot(agg, w_neigh))
    dz = (part(1).astype(F32) * slope).astype(BF)
    msg = (dot_t(dz, w_neigh) / cnt).astype(BF)
    node_grad = (dot_t(dz, w_self) + t_dot(counts, msg)).astype(BF)
    factor = 1.0 / jnp.sqrt(jnp.float32(nodes))

    def own(a):
        return lax.dynamic_slice_in_dim(a, mp * cols, cols, 1)

    grads = [t_dot(own(a), b) * factor for a, b in ((embed, dz), (agg, dz), (pooled, node_grad))]
    return (own(mixed[:node_dev]).astype(BF), own(node_grad[:node_dev]), *grads)


def join_kernel(*refs):
    first, *rest, out, sem = refs
    copy = pltpu.make_async_copy(first, out.at[0 : first.shape[0]], sem)
    copy.start()
    at = first.shape[0]
    for ref in rest:
        out[at : at + ref.shape[0]] = ref[...]
        at += ref.shape[0]
    copy.wait()


def join(*blocks):
    count = sum(b.shape[0] for b in blocks)
    if count > 8:
        return jnp.concatenate(blocks)
    vmem = pl.BlockSpec(memory_space=pltpu.VMEM)
    return pl.pallas_call(
        join_kernel,
        out_shape=jax.ShapeDtypeStruct((count, *blocks[0].shape[1:]), BF),
        in_specs=[pl.BlockSpec(memory_space=pl.ANY)] + [vmem] * (len(blocks) - 1),
        out_specs=vmem,
        scratch_shapes=[pltpu.SemaphoreType.DMA],
        compiler_params=pltpu.CompilerParams(vmem_limit_bytes=8 * MIB),
    )(*blocks)


def hop(x, axis, bit):
    return lax.ppermute(x, axis, [(i, i ^ bit) for i in range(lax.axis_size(axis))])


def gather_dp(block, later):
    size = lax.axis_size("dp")
    if size == 8:
        far = [hop(block, "dp", i) for i in (2, 4, 6)]
        far[0], later = lax.optimization_barrier((far[0], later))
        block = join(block, *far)
        order, bit = [0, 2, 4, 6], 1
    else:
        order, bit = [0], size // 2
    while bit:
        block = join(block, hop(block, "dp", bit))
        order = order + [i ^ bit for i in order]
        bit //= 2
    return block, order, later


def per_device(texts, w_qkv, w_out, w_self, w_neigh, neighbours, cotangent):
    node_dev, fan = neighbours.shape
    nodes = node_dev * lax.axis_size("dp")
    own = (w_out, w_self, w_neigh)
    even = (lax.axis_index("dp") // 2) % 2 == 0
    x_half = hop(jnp.where(even, w_self, w_neigh), "mp", 2)
    x_out = hop(w_out, "mp", 2)
    here = tuple(hop(a, "mp", 1) for a in own)

    sent = attention(texts, w_qkv, cotangent, neighbours.T)[None]
    sent, here = lax.optimization_barrier((sent, here))
    sent, order, x_half = gather_dp(sent, x_half)
    z_half = hop(x_half, "dp", 2)
    across = (x_out, x_half, z_half)
    there = tuple(hop(a, "mp", 1) for a in across)

    got_across = hop(sent, "mp", 2)
    got = (sent, hop(sent, "mp", 1), got_across, hop(got_across, "mp", 1))
    body = graph if nodes <= WIDE_LIMIT else graph_wide
    return body(order, fan, got, (own, here, across, there))


def solution(mesh):
    return jax.shard_map(
        per_device,
        mesh=mesh,
        in_specs=(
            P("dp", None, None),
            P(None, "mp"),
            P("mp", None),
            P("mp", None),
            P("mp", None),
            P("dp", None),
            P("dp", "mp"),
        ),
        out_specs=(P("dp", "mp"), P("dp", "mp"), P("mp", None), P("mp", None), P("mp", None)),
        check_vma=False,
    )
```

```python
import functools

import jax
import jax.numpy as jnp
from jax import lax
from jax.experimental import pallas as pl
from jax.experimental.pallas import tpu as pltpu
from jax.sharding import PartitionSpec as P

HD = 64
BF = jnp.bfloat16
F32 = jnp.float32
NODES_STEP = 6
WIDE_LIMIT = 256
IDS_COLS = 128
IDS_AT = 32
LOG2E = 1.4426950408889634
ATTENTION_VMEM = 58
MIB = 1 << 20


def dot_t(a, b):
    return lax.dot_general(a, b, (((1,), (1,)), ((), ())), preferred_element_type=F32)


def t_dot(a, b):
    return lax.dot_general(a, b, (((0,), (0,)), ((), ())), preferred_element_type=F32)


def dot(a, b):
    return jnp.dot(a, b, preferred_element_type=F32)


def attend(q, k, v, heads):
    seq, cols = q.shape
    lane = lax.broadcasted_iota(jnp.int32, (seq, cols), 1) // HD
    zero = jnp.zeros((seq, cols), BF)
    spread = jnp.concatenate([jnp.where(lane == h, k, zero) for h in range(heads)], axis=0)
    s = dot_t(spread, q).reshape(heads, seq, seq)
    e = jnp.exp2((s - jnp.max(s, axis=1, keepdims=True)) * (HD**-0.5 * LOG2E))
    p = (e * (1.0 / jnp.sum(e, axis=1, keepdims=True))).astype(BF)
    weight = jnp.sum(p.astype(F32), axis=2, keepdims=True)
    left = lax.broadcasted_iota(jnp.int32, (seq, 2 * HD), 1) < HD
    pairs = [jnp.where(left, weight[h], weight[h + 1]) for h in range(0, heads, 2)]
    context = jnp.concatenate(pairs, axis=1) * v.astype(F32)
    return jnp.sum(context, axis=0, keepdims=True) * (1.0 / seq)


def attention_kernel(heads, x_ref, w_ref, cot_ref, ids_ref, out_ref, wp, acc_p, acc_m):
    step = pl.program_id(0)
    nodes, seq, width = x_ref.shape
    node_dev = cot_ref.shape[0]
    cols = heads * HD

    @pl.when(step == 0)
    def _():
        for part in range(3):
            for h in range(0, heads, 2):
                a = h * 3 * HD + part * HD
                b = a + 3 * HD
                wp[:, part * cols + h * HD : part * cols + (h + 2) * HD] = jnp.concatenate(
                    [w_ref[:, a : a + HD], w_ref[:, b : b + HD]], axis=1
                )

    own = pl.ds(pl.multiple_of(lax.axis_index("mp") * cols, 128), cols)
    qkv = dot(x_ref[...].reshape(nodes * seq, width), wp[...]).astype(BF)
    for n in range(nodes):
        at = slice(n * seq, (n + 1) * seq)
        row = pl.ds(step * nodes + n, 1)
        acc_p[row, :] = attend(*(qkv[at, i * cols : (i + 1) * cols] for i in range(3)), heads)
        mean = jnp.sum(x_ref[n, :, own].astype(F32), axis=0, keepdims=True)
        acc_m[row, :] = mean * (1.0 / seq)

    @pl.when(step == pl.num_programs(0) - 1)
    def _():
        out_ref[:, :cols] = acc_p[...].astype(BF)
        out_ref[:, cols : 2 * cols] = cot_ref[...]
        out_ref[:, 2 * cols : 3 * cols] = acc_m[...].astype(BF)
        shifted = ids_ref[...] + 1
        fan = shifted.shape[0]
        blank = jnp.zeros((fan, IDS_COLS - 2 * IDS_AT), F32)
        gap = jnp.zeros((fan, IDS_AT - node_dev), F32)
        high, low = (shifted >> 4).astype(F32), (shifted & 15).astype(F32)
        packed = jnp.concatenate([high, gap, low, gap, blank], axis=1)
        rest = jnp.zeros((node_dev - fan, IDS_COLS), F32)
        out_ref[:, 3 * cols :] = jnp.concatenate([packed, rest], axis=0).astype(BF)


def attention(texts, w_qkv, cotangent, ids):
    node_dev, seq, width = texts.shape
    cols = w_qkv.shape[1] // 3
    heads = cols // HD
    tokens = node_dev * seq
    nodes = NODES_STEP
    return pl.pallas_call(
        functools.partial(attention_kernel, heads),
        out_shape=jax.ShapeDtypeStruct((node_dev, 3 * cols + IDS_COLS), BF),
        grid=(node_dev // nodes,),
        in_specs=[
            pl.BlockSpec((nodes, seq, width), lambda i: (i, 0, 0)),
            pl.BlockSpec((width, 3 * cols), lambda i: (0, 0)),
            pl.BlockSpec((node_dev, cols), lambda i: (0, 0)),
            pl.BlockSpec(ids.shape, lambda i: (0, 0)),
        ],
        out_specs=pl.BlockSpec((node_dev, 3 * cols + IDS_COLS), lambda i: (0, 0)),
        scratch_shapes=[
            pltpu.VMEM((width, 3 * cols), BF),
            pltpu.VMEM((node_dev, cols), F32),
            pltpu.VMEM((node_dev, cols), F32),
        ],
        compiler_params=pltpu.CompilerParams(vmem_limit_bytes=ATTENTION_VMEM * MIB),
        cost_estimate=pl.CostEstimate(
            flops=2 * tokens * width * 3 * cols + 8 * tokens * seq * cols,
            bytes_accessed=2 * tokens * width + 6 * width * cols,
            transcendentals=tokens * seq * heads,
        ),
    )(texts, w_qkv, cotangent, ids)


def gelu_parts(z):
    root = 0.7978845608028654
    cube = 0.044715
    t = jnp.tanh(root * (z + cube * (z * z * z)))
    half = 0.5 * (1.0 + t)
    slope = half + 0.5 * z * (1.0 - t * t) * (root * (1.0 + 3.0 * cube * (z * z)))
    return z * half, slope


def graph_kernel(order, fan, *refs):
    parts = 4
    got, blocks, refs = refs[:parts], refs[parts : parts + 12], refs[parts + 12 :]
    (mixed_ref, grad_ref, g_self, g_neigh, g_out), scratch = refs[:5], refs[5:]
    w, pooled, embed, agg, dz, node_grad, mean, cot, sem = scratch
    mp, dp = lax.axis_index("mp"), lax.axis_index("dp")
    side = (dp // 2) % 2
    groups, node_dev, _ = got[0].shape
    nodes = groups * node_dev
    cols = g_self.shape[0]
    width = parts * cols

    def place(r):
        return pl.ds(pl.multiple_of((mp ^ r) * cols, 128), cols)

    own = place(0)
    copies = []
    for r in range(parts):
        kinds = (0, 1, 2) if r < 2 else (0, 1 + side, 2 - side)
        for i, k in enumerate(kinds):
            copies.append(pltpu.make_async_copy(blocks[3 * r + i], w.at[k, mp ^ r], sem.at[i, r]))
    copies = copies[::3], copies[1::3] + copies[2::3]
    for c in copies[0] + copies[1]:
        c.start()

    def part(r, i, size=cols):
        return got[r][:, :, i : i + size].astype(F32).reshape(nodes, size)

    for r in range(parts):
        pooled[:, place(r)] = part(r, 0).astype(BF)
        cot[:, place(r)] = part(r, cols)
        mean[:, place(r)] = part(r, 2 * cols)

    packed = got[0][:, :, 3 * cols :].astype(F32)
    ids = jnp.concatenate(
        [
            packed[i, :fan, :node_dev] * 16.0 + packed[i, :fan, IDS_AT : IDS_AT + node_dev] - 1.0
            for i in range(groups)
        ],
        axis=1,
    )
    place_of = lax.broadcasted_iota(jnp.int32, (nodes, 1), 0)
    names = place_of
    for i, o in enumerate(order):
        shift = ((dp ^ o) - i) * node_dev
        inside = (place_of >= i * node_dev) & (place_of < (i + 1) * node_dev)
        names = jnp.where(inside, place_of + shift, names)
    names = names.astype(F32)
    counts_t = jnp.zeros((nodes, nodes), F32)
    for s in range(fan):
        counts_t += (ids[s : s + 1, :] == names).astype(F32)
    counts = counts_t.T
    cnt = jnp.maximum(jnp.sum(counts, axis=1, keepdims=True), 1.0)
    counts, counts_t = counts.astype(BF), counts_t.astype(BF)

    def whole(k):
        return w[k].reshape(width, width)

    for c in copies[0]:
        c.wait()
    embed[...] = (mean[...] + dot(pooled[...], whole(0))).astype(BF)
    agg[...] = (dot(counts, embed[...]) / cnt).astype(BF)
    for c in copies[1]:
        c.wait()
    z = dot(embed[...], whole(1)) + dot(agg[...], whole(2))
    mixed, slope = gelu_parts(z)
    mean[:node_dev, :] = mixed[:node_dev, :]
    mixed_ref[...] = mean[:node_dev, own].astype(BF)
    dz[...] = (cot[...] * slope).astype(BF)
    msg = (dot_t(dz[...], whole(2)) / cnt).astype(BF)
    total = dot_t(dz[...], whole(1)) + dot(counts_t, msg)
    node_grad[...] = total.astype(BF)
    cot[:node_dev, :] = total[:node_dev, :]
    grad_ref[...] = cot[:node_dev, own].astype(BF)
    factor = 1.0 / jnp.sqrt(jnp.float32(nodes))
    g_self[...] = t_dot(embed[:, own], dz[...]) * factor
    g_neigh[...] = t_dot(agg[:, own], dz[...]) * factor
    g_out[...] = t_dot(pooled[:, own], node_grad[...]) * factor


def graph(order, fan, got, weights):
    parts = len(got)
    groups, node_dev, _ = got[0].shape
    cols, width = weights[0][0].shape
    nodes = groups * node_dev
    vmem = pl.BlockSpec(memory_space=pltpu.VMEM)
    slab = jax.ShapeDtypeStruct((node_dev, cols), BF)
    big = jax.ShapeDtypeStruct((cols, width), F32)
    return pl.pallas_call(
        functools.partial(graph_kernel, order, fan),
        out_shape=(slab, slab, big, big, big),
        in_specs=[vmem] * parts + [pl.BlockSpec(memory_space=pl.ANY)] * (3 * parts),
        out_specs=(vmem,) * 5,
        scratch_shapes=[
            pltpu.VMEM((3, parts, cols, width), BF),
            pltpu.VMEM((nodes, width), BF),
            pltpu.VMEM((nodes, width), BF),
            pltpu.VMEM((nodes, width), BF),
            pltpu.VMEM((nodes, width), BF),
            pltpu.VMEM((nodes, width), BF),
            pltpu.VMEM((nodes, width), F32),
            pltpu.VMEM((nodes, width), F32),
            pltpu.SemaphoreType.DMA((3, parts)),
        ],
        compiler_params=pltpu.CompilerParams(vmem_limit_bytes=36 * MIB),
        cost_estimate=pl.CostEstimate(
            flops=2 * nodes * width * width * 6, bytes_accessed=10 * MIB, transcendentals=nodes * width
        ),
    )(*got, *sum(weights, ()))


def graph_wide(order, fan, got, weights):
    mp, dp = lax.axis_index("mp"), lax.axis_index("dp")
    parts = len(got)
    groups, node_dev, _ = got[0].shape
    cols, width = weights[0][0].shape
    nodes = groups * node_dev
    owners = jnp.array(order, jnp.int32) ^ dp
    names = (owners[:, None] * node_dev + jnp.arange(node_dev)[None, :]).reshape(1, 1, nodes)
    order = jnp.arange(parts) ^ mp
    even = (dp // 2) % 2 == 0
    kinds = [
        [group[0], jnp.where(even, group[1], group[2]), jnp.where(even, group[2], group[1])]
        for group in weights[2:]
    ]
    blocks = [*weights[:2], *kinds]
    w_out, w_self, w_neigh = (
        jnp.stack([group[k] for group in blocks])[order].reshape(width, width) for k in range(3)
    )

    def part(i):
        block = jnp.stack([g[:, :, i * cols : (i + 1) * cols] for g in got])[order]
        return block.transpose(1, 2, 0, 3).reshape(nodes, width)

    pooled = part(0)
    packed = got[0][:, :fan, 3 * cols :].astype(jnp.int32)
    ids = packed[:, :, :node_dev] * 16 + packed[:, :, IDS_AT : IDS_AT + node_dev] - 1
    ids = ids.transpose(0, 2, 1).reshape(nodes, fan)
    cnt = jnp.maximum(jnp.sum(ids >= 0, axis=1).astype(F32), 1.0)[:, None]
    counts = jnp.sum(ids[:, :, None] == names, axis=1).astype(BF)
    embed = (part(2).astype(F32) + dot(pooled, w_out)).astype(BF)
    agg = (dot(counts, embed) / cnt).astype(BF)
    mixed, slope = gelu_parts(dot(embed, w_self) + dot(agg, w_neigh))
    dz = (part(1).astype(F32) * slope).astype(BF)
    msg = (dot_t(dz, w_neigh) / cnt).astype(BF)
    node_grad = (dot_t(dz, w_self) + t_dot(counts, msg)).astype(BF)
    factor = 1.0 / jnp.sqrt(jnp.float32(nodes))

    def own(a):
        return lax.dynamic_slice_in_dim(a, mp * cols, cols, 1)

    grads = [t_dot(own(a), b) * factor for a, b in ((embed, dz), (agg, dz), (pooled, node_grad))]
    return (own(mixed[:node_dev]).astype(BF), own(node_grad[:node_dev]), *grads)


def join_kernel(*refs):
    out, at = refs[-1], 0
    for ref in refs[:-1]:
        out[at : at + ref.shape[0]] = ref[...]
        at += ref.shape[0]


def join(*blocks):
    count = sum(b.shape[0] for b in blocks)
    if count > 8:
        return jnp.concatenate(blocks)
    vmem = pl.BlockSpec(memory_space=pltpu.VMEM)
    return pl.pallas_call(
        join_kernel,
        out_shape=jax.ShapeDtypeStruct((count, *blocks[0].shape[1:]), BF),
        in_specs=[vmem] * len(blocks),
        out_specs=vmem,
        compiler_params=pltpu.CompilerParams(vmem_limit_bytes=8 * MIB),
    )(*blocks)


def hop(x, axis, bit):
    return lax.ppermute(x, axis, [(i, i ^ bit) for i in range(lax.axis_size(axis))])


def gather_dp(block, later):
    size = lax.axis_size("dp")
    if size == 8:
        far = [hop(block, "dp", i) for i in (2, 4, 6)]
        mine = join(block)
        mine, far, later = lax.optimization_barrier((mine, far, later))
        block = join(mine, *far)
        order, bit = [0, 2, 4, 6], 1
    else:
        order, bit = [0], size // 2
    while bit:
        block = join(block, hop(block, "dp", bit))
        order = order + [i ^ bit for i in order]
        bit //= 2
    return block, order, later


def per_device(texts, w_qkv, w_out, w_self, w_neigh, neighbours, cotangent):
    node_dev, fan = neighbours.shape
    nodes = node_dev * lax.axis_size("dp")
    own = (w_out, w_self, w_neigh)
    even = (lax.axis_index("dp") // 2) % 2 == 0
    x_out = hop(w_out, "mp", 2)
    x_half = hop(jnp.where(even, w_self, w_neigh), "mp", 2)
    here = tuple(hop(a, "mp", 1) for a in own)

    sent = attention(texts, w_qkv, cotangent, neighbours.T)[None]
    sent, here, x_out = lax.optimization_barrier((sent, here, x_out))
    sent, order, x_half = gather_dp(sent, x_half)
    z_half = hop(x_half, "dp", 2)
    across = (x_out, x_half, z_half)
    there = tuple(hop(a, "mp", 1) for a in across)

    got_across = hop(sent, "mp", 2)
    got = (sent, hop(sent, "mp", 1), got_across, hop(got_across, "mp", 1))
    body = graph if nodes <= WIDE_LIMIT else graph_wide
    return body(order, fan, got, (own, here, across, there))


def solution(mesh):
    return jax.shard_map(
        per_device,
        mesh=mesh,
        in_specs=(
            P("dp", None, None),
            P(None, "mp"),
            P("mp", None),
            P("mp", None),
            P("mp", None),
            P("dp", None),
            P("dp", "mp"),
        ),
        out_specs=(P("dp", "mp"), P("dp", "mp"), P("mp", None), P("mp", None), P("mp", None)),
        check_vma=False,
    )
```

```python
import functools

import jax
import jax.numpy as jnp
from jax import lax
from jax.experimental import pallas as pl
from jax.experimental.pallas import tpu as pltpu
from jax.sharding import PartitionSpec as P

HD = 64
BF = jnp.bfloat16
F32 = jnp.float32
NODES_STEP = 6
WIDE_LIMIT = 256
IDS_COLS = 128
IDS_AT = 32
TOP = 16
LOG2E = 1.4426950408889634
ATTENTION_VMEM = 58
MIB = 1 << 20


def dot_t(a, b):
    return lax.dot_general(a, b, (((1,), (1,)), ((), ())), preferred_element_type=F32)


def t_dot(a, b):
    return lax.dot_general(a, b, (((0,), (0,)), ((), ())), preferred_element_type=F32)


def dot(a, b):
    return jnp.dot(a, b, preferred_element_type=F32)


def attend(q, k, v, heads):
    seq, cols = q.shape
    lane = lax.broadcasted_iota(jnp.int32, (seq, cols), 1) // HD
    zero = jnp.zeros((seq, cols), BF)
    spread = jnp.concatenate([jnp.where(lane == h, k, zero) for h in range(heads)], axis=0)
    s = dot_t(spread, q).reshape(heads, seq, seq)
    e = jnp.exp2((s - jnp.max(s, axis=1, keepdims=True)) * (HD**-0.5 * LOG2E))
    p = (e * (1.0 / jnp.sum(e, axis=1, keepdims=True))).astype(BF)
    weight = jnp.sum(p.astype(F32), axis=2, keepdims=True)
    left = lax.broadcasted_iota(jnp.int32, (seq, 2 * HD), 1) < HD
    pairs = [jnp.where(left, weight[h], weight[h + 1]) for h in range(0, heads, 2)]
    context = jnp.concatenate(pairs, axis=1) * v.astype(F32)
    return jnp.sum(context, axis=0, keepdims=True) * (1.0 / seq)


def attention_kernel(heads, x_ref, w_ref, cot_ref, ids_ref, out_ref, wp, acc_p, acc_m):
    step = pl.program_id(0)
    nodes, seq, width = x_ref.shape
    node_dev = cot_ref.shape[0]
    cols = heads * HD

    @pl.when(step == 0)
    def _():
        for part in range(3):
            for h in range(0, heads, 2):
                a = h * 3 * HD + part * HD
                b = a + 3 * HD
                wp[:, part * cols + h * HD : part * cols + (h + 2) * HD] = jnp.concatenate(
                    [w_ref[:, a : a + HD], w_ref[:, b : b + HD]], axis=1
                )

    own = pl.ds(pl.multiple_of(lax.axis_index("mp") * cols, 128), cols)
    qkv = dot(x_ref[...].reshape(nodes * seq, width), wp[...]).astype(BF)
    for n in range(nodes):
        at = slice(n * seq, (n + 1) * seq)
        row = pl.ds(step * nodes + n, 1)
        acc_p[row, :] = attend(*(qkv[at, i * cols : (i + 1) * cols] for i in range(3)), heads)
        mean = jnp.sum(x_ref[n, :, own].astype(F32), axis=0, keepdims=True)
        acc_m[row, :] = mean * (1.0 / seq)

    @pl.when(step == pl.num_programs(0) - 1)
    def _():
        rows = jnp.concatenate([acc_p[...], cot_ref[...].astype(F32), acc_m[...]], axis=1)
        shifted = ids_ref[...] + 1
        fan = shifted.shape[0]
        gap = jnp.zeros((fan, IDS_AT - node_dev), F32)
        high, low = (shifted >> 4).astype(F32), (shifted & 15).astype(F32)
        blank = jnp.zeros((fan, IDS_COLS - 2 * IDS_AT), F32)
        ids = jnp.concatenate([high, gap, low, gap, blank], axis=1)
        wide = 3 * cols
        rest = jnp.concatenate([rows[TOP:, : wide // 2], rows[TOP:, wide // 2 :]], axis=0)
        out_ref[:, :wide] = rows[:TOP].astype(BF)
        out_ref[:, wide : wide + wide // 2] = rest.astype(BF)
        out_ref[:, wide + wide // 2 :] = ids.astype(BF)


def unpack(got, cols, part):
    got = got.astype(F32)
    wide, at = 3 * cols, part * cols
    pieces, left = [], at
    while left < at + cols:
        side, inside = divmod(left, wide // 2)
        right = min(at + cols, (side + 1) * (wide // 2))
        low = wide + inside
        pieces.append(got[:, side * (TOP // 2) : (side + 1) * (TOP // 2), low : low + right - left])
        left = right
    rest = jnp.concatenate(pieces, axis=2) if len(pieces) > 1 else pieces[0]
    return jnp.concatenate([got[:, :, at : at + cols], rest], axis=1)


def attention(texts, w_qkv, cotangent, ids):
    node_dev, seq, width = texts.shape
    cols = w_qkv.shape[1] // 3
    heads = cols // HD
    tokens = node_dev * seq
    nodes = NODES_STEP
    packed = (TOP, 3 * cols + 3 * cols // 2 + IDS_COLS)
    return pl.pallas_call(
        functools.partial(attention_kernel, heads),
        out_shape=jax.ShapeDtypeStruct(packed, BF),
        grid=(node_dev // nodes,),
        in_specs=[
            pl.BlockSpec((nodes, seq, width), lambda i: (i, 0, 0)),
            pl.BlockSpec((width, 3 * cols), lambda i: (0, 0)),
            pl.BlockSpec((node_dev, cols), lambda i: (0, 0)),
            pl.BlockSpec(ids.shape, lambda i: (0, 0)),
        ],
        out_specs=pl.BlockSpec(packed, lambda i: (0, 0)),
        scratch_shapes=[
            pltpu.VMEM((width, 3 * cols), BF),
            pltpu.VMEM((node_dev, cols), F32),
            pltpu.VMEM((node_dev, cols), F32),
        ],
        compiler_params=pltpu.CompilerParams(vmem_limit_bytes=ATTENTION_VMEM * MIB),
        cost_estimate=pl.CostEstimate(
            flops=2 * tokens * width * 3 * cols + 8 * tokens * seq * cols,
            bytes_accessed=2 * tokens * width + 6 * width * cols,
            transcendentals=tokens * seq * heads,
        ),
    )(texts, w_qkv, cotangent, ids)


def gelu_parts(z):
    root = 0.7978845608028654
    cube = 0.044715
    t = jnp.tanh(root * (z + cube * (z * z * z)))
    half = 0.5 * (1.0 + t)
    slope = half + 0.5 * z * (1.0 - t * t) * (root * (1.0 + 3.0 * cube * (z * z)))
    return z * half, slope


def graph_kernel(order, fan, node_dev, *refs):
    parts = 4
    got, blocks, refs = refs[:parts], refs[parts : 4 * parts], refs[4 * parts :]
    mixed_ref, grad_ref, g_self, g_neigh, g_out, both, dz, mean, cot = refs
    mp, dp = lax.axis_index("mp"), lax.axis_index("dp")
    side = (dp // 2) % 2
    groups = got[0].shape[0]
    nodes = groups * node_dev
    cols, width = g_self.shape

    def place(r):
        return pl.ds(pl.multiple_of((mp ^ r) * cols, 128), cols)

    def part(r, i):
        return unpack(got[r][...], cols, i).reshape(nodes, cols)

    own = place(0)
    pooled = [part(r, 0).astype(BF) for r in range(parts)]
    for r in range(parts):
        cot[:, place(r)] = part(r, 1)
        mean[:, place(r)] = part(r, 2)

    packed = got[0][:, :, got[0].shape[2] - IDS_COLS :].astype(F32)
    ids = jnp.concatenate(
        [
            packed[i, :fan, :node_dev] * 16.0 + packed[i, :fan, IDS_AT : IDS_AT + node_dev] - 1.0
            for i in range(groups)
        ],
        axis=1,
    )
    place_of = lax.broadcasted_iota(jnp.int32, (nodes, 1), 0)
    names = place_of
    for i, o in enumerate(order):
        shift = ((dp ^ o) - i) * node_dev
        inside = (place_of >= i * node_dev) & (place_of < (i + 1) * node_dev)
        names = jnp.where(inside, place_of + shift, names)
    names = names.astype(F32)
    counts_t = jnp.zeros((nodes, nodes), F32)
    for s in range(fan):
        counts_t += (ids[s : s + 1, :] == names).astype(F32)
    counts = counts_t.T
    share = 1.0 / jnp.maximum(jnp.sum(counts, axis=1, keepdims=True), 1.0)
    counts, counts_t = counts.astype(BF), counts_t.astype(BF)

    sums = sum(dot(pooled[r], blocks[3 * r][...]) for r in range(parts))
    both[0] = (mean[...] + sums).astype(BF)
    both[1] = (dot(counts, both[0]) * share).astype(BF)
    z = 0.0
    for r in range(parts):
        first = 0 if r < 2 else side
        z += dot(both[first, :, place(r)], blocks[3 * r + 1][...])
        z += dot(both[1 - first, :, place(r)], blocks[3 * r + 2][...])
    mixed, slope = gelu_parts(z)
    mean[:node_dev, :] = mixed[:node_dev, :]
    mixed_ref[...] = mean[:node_dev, own].astype(BF)
    dz[...] = (cot[...] * slope).astype(BF)
    factor = 1.0 / jnp.sqrt(jnp.float32(nodes))
    for r in range(parts):
        to_self = dot_t(dz[...], blocks[3 * r + 1][...])
        to_agg = dot_t(dz[...], blocks[3 * r + 2][...])
        if r >= 2:
            even = side == 0
            to_self, to_agg = jnp.where(even, to_self, to_agg), jnp.where(even, to_agg, to_self)
        total = to_self + dot(counts_t, (to_agg * share).astype(BF))
        if r == 0:
            grad_ref[...] = total[:node_dev, :].astype(BF)
        g_out[:, place(r)] = t_dot(pooled[0], total.astype(BF)) * factor
    g_self[...] = t_dot(both[0, :, own], dz[...]) * factor
    g_neigh[...] = t_dot(both[1, :, own], dz[...]) * factor


def graph(order, fan, node_dev, got, weights):
    parts = len(got)
    cols, width = weights[0][0].shape
    nodes = got[0].shape[0] * node_dev
    vmem = pl.BlockSpec(memory_space=pltpu.VMEM)
    slab = jax.ShapeDtypeStruct((node_dev, cols), BF)
    big = jax.ShapeDtypeStruct((cols, width), F32)
    return pl.pallas_call(
        functools.partial(graph_kernel, order, fan, node_dev),
        out_shape=(slab, slab, big, big, big),
        in_specs=[vmem] * (4 * parts),
        out_specs=(vmem,) * 5,
        scratch_shapes=[
            pltpu.VMEM((2, nodes, width), BF),
            pltpu.VMEM((nodes, width), BF),
            pltpu.VMEM((nodes, width), F32),
            pltpu.VMEM((nodes, width), F32),
        ],
        compiler_params=pltpu.CompilerParams(vmem_limit_bytes=36 * MIB),
        cost_estimate=pl.CostEstimate(
            flops=2 * nodes * width * width * 6, bytes_accessed=10 * MIB, transcendentals=nodes * width
        ),
    )(*got, *sum(weights, ()))


def graph_wide(order, fan, node_dev, got, weights):
    mp, dp = lax.axis_index("mp"), lax.axis_index("dp")
    parts = len(got)
    cols, width = weights[0][0].shape
    nodes = got[0].shape[0] * node_dev
    owners = jnp.array(order, jnp.int32) ^ dp
    names = (owners[:, None] * node_dev + jnp.arange(node_dev)[None, :]).reshape(1, 1, nodes)
    order = jnp.arange(parts) ^ mp
    even = (dp // 2) % 2 == 0
    kinds = [
        [group[0], jnp.where(even, group[1], group[2]), jnp.where(even, group[2], group[1])]
        for group in weights[2:]
    ]
    blocks = [*weights[:2], *kinds]
    w_out, w_self, w_neigh = (
        jnp.stack([group[k] for group in blocks])[order].reshape(width, width) for k in range(3)
    )

    def part(i):
        block = jnp.stack([unpack(g, cols, i) for g in got])[order]
        return block.transpose(1, 2, 0, 3).reshape(nodes, width)

    pooled = part(0).astype(BF)
    packed = got[0][:, :fan, got[0].shape[2] - IDS_COLS :].astype(jnp.int32)
    ids = packed[:, :, :node_dev] * 16 + packed[:, :, IDS_AT : IDS_AT + node_dev] - 1
    ids = ids.transpose(0, 2, 1).reshape(nodes, fan)
    cnt = jnp.maximum(jnp.sum(ids >= 0, axis=1).astype(F32), 1.0)[:, None]
    counts = jnp.sum(ids[:, :, None] == names, axis=1).astype(BF)
    embed = (part(2) + dot(pooled, w_out)).astype(BF)
    agg = (dot(counts, embed) / cnt).astype(BF)
    mixed, slope = gelu_parts(dot(embed, w_self) + dot(agg, w_neigh))
    dz = (part(1) * slope).astype(BF)
    msg = (dot_t(dz, w_neigh) / cnt).astype(BF)
    node_grad = (dot_t(dz, w_self) + t_dot(counts, msg)).astype(BF)
    factor = 1.0 / jnp.sqrt(jnp.float32(nodes))

    def own(a):
        return lax.dynamic_slice_in_dim(a, mp * cols, cols, 1)

    grads = [t_dot(own(a), b) * factor for a, b in ((embed, dz), (agg, dz), (pooled, node_grad))]
    return (own(mixed[:node_dev]).astype(BF), own(node_grad[:node_dev]), *grads)


def join_kernel(*refs):
    out, at = refs[-1], 0
    for ref in refs[:-1]:
        out[at : at + ref.shape[0]] = ref[...]
        at += ref.shape[0]


def join(*blocks):
    count = sum(b.shape[0] for b in blocks)
    if count > 8:
        return jnp.concatenate(blocks)
    vmem = pl.BlockSpec(memory_space=pltpu.VMEM)
    return pl.pallas_call(
        join_kernel,
        out_shape=jax.ShapeDtypeStruct((count, *blocks[0].shape[1:]), BF),
        in_specs=[vmem] * len(blocks),
        out_specs=vmem,
        compiler_params=pltpu.CompilerParams(vmem_limit_bytes=8 * MIB),
    )(*blocks)


def hop(x, axis, bit):
    return lax.ppermute(x, axis, [(i, i ^ bit) for i in range(lax.axis_size(axis))])


def gather_dp(block, later):
    size = lax.axis_size("dp")
    if size == 8:
        far = [hop(block, "dp", i) for i in (2, 4, 6)]
        mine = join(block)
        mine, far, later = lax.optimization_barrier((mine, far, later))
        block = join(mine, *far)
        order, bit = [0, 2, 4, 6], 1
    else:
        order, bit = [0], size // 2
    while bit:
        block = join(block, hop(block, "dp", bit))
        order = order + [i ^ bit for i in order]
        bit //= 2
    return block, order, later


def per_device(texts, w_qkv, w_out, w_self, w_neigh, neighbours, cotangent):
    node_dev, fan = neighbours.shape
    nodes = node_dev * lax.axis_size("dp")
    own = (w_out, w_self, w_neigh)
    even = (lax.axis_index("dp") // 2) % 2 == 0
    x_half = hop(jnp.where(even, w_self, w_neigh), "mp", 2)
    here = tuple(hop(a, "mp", 1) for a in own)

    sent = attention(texts, w_qkv, cotangent, neighbours.T)[None]
    sent, here, x_half, w_out = lax.optimization_barrier((sent, here, x_half, w_out))
    x_out = hop(w_out, "mp", 2)
    sent, order, x_half = gather_dp(sent, x_half)
    sent, x_out = lax.optimization_barrier((sent, x_out))
    z_half = hop(x_half, "dp", 2)
    across = (x_out, x_half, z_half)
    there = tuple(hop(a, "mp", 1) for a in across)

    got_across = hop(sent, "mp", 2)
    got = (sent, hop(sent, "mp", 1), got_across, hop(got_across, "mp", 1))
    body = graph if nodes <= WIDE_LIMIT else graph_wide
    return body(order, fan, node_dev, got, (own, here, across, there))


def solution(mesh):
    return jax.shard_map(
        per_device,
        mesh=mesh,
        in_specs=(
            P("dp", None, None),
            P(None, "mp"),
            P("mp", None),
            P("mp", None),
            P("mp", None),
            P("dp", None),
            P("dp", "mp"),
        ),
        out_specs=(P("dp", "mp"), P("dp", "mp"), P("mp", None), P("mp", None), P("mp", None)),
        check_vma=False,
    )
```

```python
import functools

import jax
import jax.numpy as jnp
from jax import lax
from jax.experimental import pallas as pl
from jax.experimental.pallas import tpu as pltpu
from jax.sharding import PartitionSpec as P

HD = 64
BF = jnp.bfloat16
F32 = jnp.float32
NODES_STEP = 6
WIDE_LIMIT = 256
IDS_COLS = 128
IDS_AT = 32
TOP = 16
LOG2E = 1.4426950408889634
ATTENTION_VMEM = 58
MIB = 1 << 20


def dot_t(a, b):
    return lax.dot_general(a, b, (((1,), (1,)), ((), ())), preferred_element_type=F32)


def t_dot(a, b):
    return lax.dot_general(a, b, (((0,), (0,)), ((), ())), preferred_element_type=F32)


def dot(a, b):
    return jnp.dot(a, b, preferred_element_type=F32)


def attend(q, k, v, heads):
    seq, cols = q.shape
    lane = lax.broadcasted_iota(jnp.int32, (seq, cols), 1) // HD
    zero = jnp.zeros((seq, cols), BF)
    spread = jnp.concatenate([jnp.where(lane == h, k, zero) for h in range(heads)], axis=0)
    s = dot_t(spread, q).reshape(heads, seq, seq)
    e = jnp.exp2((s - jnp.max(s, axis=1, keepdims=True)) * (HD**-0.5 * LOG2E))
    p = (e * (1.0 / jnp.sum(e, axis=1, keepdims=True))).astype(BF)
    weight = jnp.sum(p.astype(F32), axis=2, keepdims=True)
    left = lax.broadcasted_iota(jnp.int32, (seq, 2 * HD), 1) < HD
    pairs = [jnp.where(left, weight[h], weight[h + 1]) for h in range(0, heads, 2)]
    context = jnp.concatenate(pairs, axis=1) * v.astype(F32)
    return jnp.sum(context, axis=0, keepdims=True) * (1.0 / seq)


def attention_kernel(heads, x_ref, w_ref, cot_ref, ids_ref, out_ref, wp, acc_p, acc_m):
    step = pl.program_id(0)
    nodes, seq, width = x_ref.shape
    node_dev = cot_ref.shape[0]
    cols = heads * HD

    @pl.when(step == 0)
    def _():
        for part in range(3):
            for h in range(0, heads, 2):
                a = h * 3 * HD + part * HD
                b = a + 3 * HD
                wp[:, part * cols + h * HD : part * cols + (h + 2) * HD] = jnp.concatenate(
                    [w_ref[:, a : a + HD], w_ref[:, b : b + HD]], axis=1
                )

    own = pl.ds(pl.multiple_of(lax.axis_index("mp") * cols, 128), cols)
    qkv = dot(x_ref[...].reshape(nodes * seq, width), wp[...]).astype(BF)
    for n in range(nodes):
        at = slice(n * seq, (n + 1) * seq)
        row = pl.ds(step * nodes + n, 1)
        acc_p[row, :] = attend(*(qkv[at, i * cols : (i + 1) * cols] for i in range(3)), heads)
        mean = jnp.sum(x_ref[n, :, own].astype(F32), axis=0, keepdims=True)
        acc_m[row, :] = mean * (1.0 / seq)

    @pl.when(step == pl.num_programs(0) - 1)
    def _():
        rows = jnp.concatenate([acc_p[...], cot_ref[...].astype(F32), acc_m[...]], axis=1)
        shifted = ids_ref[...] + 1
        fan = shifted.shape[0]
        gap = jnp.zeros((fan, IDS_AT - node_dev), F32)
        high, low = (shifted >> 4).astype(F32), (shifted & 15).astype(F32)
        blank = jnp.zeros((fan, IDS_COLS - 2 * IDS_AT), F32)
        ids = jnp.concatenate([high, gap, low, gap, blank], axis=1)
        wide = 3 * cols
        rest = jnp.concatenate([rows[TOP:, : wide // 2], rows[TOP:, wide // 2 :]], axis=0)
        out_ref[:, :wide] = rows[:TOP].astype(BF)
        out_ref[:, wide : wide + wide // 2] = rest.astype(BF)
        out_ref[:, wide + wide // 2 :] = ids.astype(BF)


def unpack(got, cols, part):
    got = got.astype(F32)
    wide, at = 3 * cols, part * cols
    pieces, left = [], at
    while left < at + cols:
        side, inside = divmod(left, wide // 2)
        right = min(at + cols, (side + 1) * (wide // 2))
        low = wide + inside
        pieces.append(got[:, side * (TOP // 2) : (side + 1) * (TOP // 2), low : low + right - left])
        left = right
    rest = jnp.concatenate(pieces, axis=2) if len(pieces) > 1 else pieces[0]
    return jnp.concatenate([got[:, :, at : at + cols], rest], axis=1)


def attention(texts, w_qkv, cotangent, ids):
    node_dev, seq, width = texts.shape
    cols = w_qkv.shape[1] // 3
    heads = cols // HD
    tokens = node_dev * seq
    nodes = NODES_STEP
    packed = (TOP, 3 * cols + 3 * cols // 2 + IDS_COLS)
    return pl.pallas_call(
        functools.partial(attention_kernel, heads),
        out_shape=jax.ShapeDtypeStruct(packed, BF),
        grid=(node_dev // nodes,),
        in_specs=[
            pl.BlockSpec((nodes, seq, width), lambda i: (i, 0, 0)),
            pl.BlockSpec((width, 3 * cols), lambda i: (0, 0)),
            pl.BlockSpec((node_dev, cols), lambda i: (0, 0)),
            pl.BlockSpec(ids.shape, lambda i: (0, 0)),
        ],
        out_specs=pl.BlockSpec(packed, lambda i: (0, 0)),
        scratch_shapes=[
            pltpu.VMEM((width, 3 * cols), BF),
            pltpu.VMEM((node_dev, cols), F32),
            pltpu.VMEM((node_dev, cols), F32),
        ],
        compiler_params=pltpu.CompilerParams(vmem_limit_bytes=ATTENTION_VMEM * MIB),
        cost_estimate=pl.CostEstimate(
            flops=2 * tokens * width * 3 * cols + 8 * tokens * seq * cols,
            bytes_accessed=2 * tokens * width + 6 * width * cols,
            transcendentals=tokens * seq * heads,
        ),
    )(texts, w_qkv, cotangent, ids)


def gelu_parts(z):
    root = 0.7978845608028654
    cube = 0.044715
    t = jnp.tanh(root * (z + cube * (z * z * z)))
    half = 0.5 * (1.0 + t)
    slope = half + 0.5 * z * (1.0 - t * t) * (root * (1.0 + 3.0 * cube * (z * z)))
    return z * half, slope


def block_place(r, cols):
    return pl.ds(pl.multiple_of((lax.axis_index("mp") ^ r) * cols, 128), cols)


def embed_kernel(order, fan, node_dev, *refs):
    parts = 4
    got, blocks, refs = refs[:parts], refs[parts : 2 * parts], refs[2 * parts :]
    both, cot, pooled_ref, counts_ref, share_ref, mean = refs
    dp = lax.axis_index("dp")
    groups = got[0].shape[0]
    nodes = groups * node_dev
    cols = blocks[0].shape[0]

    def part(r, i):
        return unpack(got[r][...], cols, i).reshape(nodes, cols)

    packed = got[0][:, :, got[0].shape[2] - IDS_COLS :].astype(F32)
    ids = jnp.concatenate(
        [
            packed[i, :fan, :node_dev] * 16.0 + packed[i, :fan, IDS_AT : IDS_AT + node_dev] - 1.0
            for i in range(groups)
        ],
        axis=1,
    )
    place_of = lax.broadcasted_iota(jnp.int32, (nodes, 1), 0)
    names = place_of
    for i, o in enumerate(order):
        shift = ((dp ^ o) - i) * node_dev
        inside = (place_of >= i * node_dev) & (place_of < (i + 1) * node_dev)
        names = jnp.where(inside, place_of + shift, names)
    names = names.astype(F32)
    counts_t = jnp.zeros((nodes, nodes), F32)
    for s in range(fan):
        counts_t += (ids[s : s + 1, :] == names).astype(F32)
    counts = counts_t.T
    share = 1.0 / jnp.maximum(jnp.sum(counts, axis=1, keepdims=True), 1.0)
    counts_ref[...] = counts_t.astype(BF)
    share_ref[...] = jnp.broadcast_to(share, share_ref.shape)

    pooled = [part(r, 0).astype(BF) for r in range(parts)]
    pooled_ref[...] = pooled[0]
    for r in range(parts):
        cot[:, block_place(r, cols)] = part(r, 1).astype(BF)
        mean[:, block_place(r, cols)] = part(r, 2)
    sums = sum(dot(pooled[r], blocks[r][...]) for r in range(parts))
    both[0] = (mean[...] + sums).astype(BF)
    both[1] = (dot(counts.astype(BF), both[0]) * share).astype(BF)


def graph_kernel(node_dev, both, cot, pooled, counts, share_ref, *refs):
    parts = 4
    blocks, refs = refs[: 2 * parts], refs[2 * parts :]
    mixed_ref, grad_ref, g_self, g_neigh, g_out, dz, wide, grads, sem = refs
    side = (lax.axis_index("dp") // 2) % 2
    cols, width = g_self.shape
    nodes = counts.shape[0]
    factor = 1.0 / jnp.sqrt(jnp.float32(nodes))
    own = block_place(0, cols)

    z = 0.0
    for r in range(parts):
        first = 0 if r < 2 else side
        z += dot(both[first, :, block_place(r, cols)], blocks[2 * r][...])
        z += dot(both[1 - first, :, block_place(r, cols)], blocks[2 * r + 1][...])
    mixed, slope = gelu_parts(z)
    dz[...] = (cot[...].astype(F32) * slope).astype(BF)
    wide[...] = mixed[:node_dev, :]
    mixed_ref[...] = wide[:, own].astype(BF)

    copies = []
    for i, out in enumerate((g_self, g_neigh)):
        grads[i] = t_dot(both[i, :, own], dz[...]) * factor
        copies.append(pltpu.make_async_copy(grads.at[i], out, sem.at[i]))
        copies[-1].start()
    share = share_ref[:, :1]
    for r in range(parts):
        to_self, to_agg = dot_t(dz[...], blocks[2 * r][...]), dot_t(dz[...], blocks[2 * r + 1][...])
        if r >= 2:
            even = side == 0
            to_self, to_agg = jnp.where(even, to_self, to_agg), jnp.where(even, to_agg, to_self)
        total = to_self + dot(counts[...], (to_agg * share).astype(BF))
        if r == 0:
            grad_ref[...] = total[:node_dev, :].astype(BF)
        at = slice(r * cols, (r + 1) * cols)
        grads[2, :, at] = t_dot(pooled[...], total.astype(BF)) * factor
        copies.append(
            pltpu.make_async_copy(grads.at[2, :, at], g_out.at[:, block_place(r, cols)], sem.at[2 + r])
        )
        copies[-1].start()
    for copy in copies:
        copy.wait()


def graph(order, fan, node_dev, got, weights):
    parts = len(got)
    cols, width = weights[0][0].shape
    nodes = got[0].shape[0] * node_dev
    vmem = pl.BlockSpec(memory_space=pltpu.VMEM)
    known = pl.pallas_call(
        functools.partial(embed_kernel, order, fan, node_dev),
        out_shape=(
            jax.ShapeDtypeStruct((2, nodes, width), BF),
            jax.ShapeDtypeStruct((nodes, width), BF),
            jax.ShapeDtypeStruct((nodes, cols), BF),
            jax.ShapeDtypeStruct((nodes, nodes), BF),
            jax.ShapeDtypeStruct((nodes, 128), F32),
        ),
        in_specs=[vmem] * (2 * parts),
        out_specs=(vmem,) * 5,
        scratch_shapes=[pltpu.VMEM((nodes, width), F32)],
        compiler_params=pltpu.CompilerParams(vmem_limit_bytes=24 * MIB),
        cost_estimate=pl.CostEstimate(
            flops=2 * nodes * width * width * 2, bytes_accessed=4 * MIB, transcendentals=0
        ),
    )(*got, *[group[0] for group in weights])
    slab = jax.ShapeDtypeStruct((node_dev, cols), BF)
    big = jax.ShapeDtypeStruct((cols, width), F32)
    anywhere = pl.BlockSpec(memory_space=pl.ANY)
    return pl.pallas_call(
        functools.partial(graph_kernel, node_dev),
        out_shape=(slab, slab, big, big, big),
        in_specs=[vmem] * (5 + 2 * parts),
        out_specs=(vmem, vmem, anywhere, anywhere, anywhere),
        scratch_shapes=[
            pltpu.VMEM((nodes, width), BF),
            pltpu.VMEM((node_dev, width), F32),
            pltpu.VMEM((3, cols, width), F32),
            pltpu.SemaphoreType.DMA((2 + parts,)),
        ],
        compiler_params=pltpu.CompilerParams(vmem_limit_bytes=36 * MIB),
        cost_estimate=pl.CostEstimate(
            flops=2 * nodes * width * width * 5, bytes_accessed=8 * MIB, transcendentals=nodes * width
        ),
    )(*known, *sum((group[1:] for group in weights), ()))


def graph_wide(order, fan, node_dev, got, weights):
    mp, dp = lax.axis_index("mp"), lax.axis_index("dp")
    parts = len(got)
    cols, width = weights[0][0].shape
    nodes = got[0].shape[0] * node_dev
    owners = jnp.array(order, jnp.int32) ^ dp
    names = (owners[:, None] * node_dev + jnp.arange(node_dev)[None, :]).reshape(1, 1, nodes)
    order = jnp.arange(parts) ^ mp
    even = (dp // 2) % 2 == 0
    kinds = [
        [group[0], jnp.where(even, group[1], group[2]), jnp.where(even, group[2], group[1])]
        for group in weights[2:]
    ]
    blocks = [*weights[:2], *kinds]
    w_out, w_self, w_neigh = (
        jnp.stack([group[k] for group in blocks])[order].reshape(width, width) for k in range(3)
    )

    def part(i):
        block = jnp.stack([unpack(g, cols, i) for g in got])[order]
        return block.transpose(1, 2, 0, 3).reshape(nodes, width)

    pooled = part(0).astype(BF)
    packed = got[0][:, :fan, got[0].shape[2] - IDS_COLS :].astype(jnp.int32)
    ids = packed[:, :, :node_dev] * 16 + packed[:, :, IDS_AT : IDS_AT + node_dev] - 1
    ids = ids.transpose(0, 2, 1).reshape(nodes, fan)
    cnt = jnp.maximum(jnp.sum(ids >= 0, axis=1).astype(F32), 1.0)[:, None]
    counts = jnp.sum(ids[:, :, None] == names, axis=1).astype(BF)
    embed = (part(2) + dot(pooled, w_out)).astype(BF)
    agg = (dot(counts, embed) / cnt).astype(BF)
    mixed, slope = gelu_parts(dot(embed, w_self) + dot(agg, w_neigh))
    dz = (part(1) * slope).astype(BF)
    msg = (dot_t(dz, w_neigh) / cnt).astype(BF)
    node_grad = (dot_t(dz, w_self) + t_dot(counts, msg)).astype(BF)
    factor = 1.0 / jnp.sqrt(jnp.float32(nodes))

    def own(a):
        return lax.dynamic_slice_in_dim(a, mp * cols, cols, 1)

    grads = [t_dot(own(a), b) * factor for a, b in ((embed, dz), (agg, dz), (pooled, node_grad))]
    return (own(mixed[:node_dev]).astype(BF), own(node_grad[:node_dev]), *grads)


def join_kernel(*refs):
    out, at = refs[-1], 0
    for ref in refs[:-1]:
        out[at : at + ref.shape[0]] = ref[...]
        at += ref.shape[0]


def join(*blocks):
    count = sum(b.shape[0] for b in blocks)
    if count > 8:
        return jnp.concatenate(blocks)
    vmem = pl.BlockSpec(memory_space=pltpu.VMEM)
    return pl.pallas_call(
        join_kernel,
        out_shape=jax.ShapeDtypeStruct((count, *blocks[0].shape[1:]), BF),
        in_specs=[vmem] * len(blocks),
        out_specs=vmem,
        compiler_params=pltpu.CompilerParams(vmem_limit_bytes=8 * MIB),
    )(*blocks)


def hop(x, axis, bit):
    return lax.ppermute(x, axis, [(i, i ^ bit) for i in range(lax.axis_size(axis))])


def gather_dp(block, later):
    size = lax.axis_size("dp")
    if size == 8:
        far = [hop(block, "dp", i) for i in range(1, size)]
        mine = join(block)
        mine, far, later = lax.optimization_barrier((mine, far, later))
        block = join(mine, *far)
        order, bit = list(range(size)), 0
    else:
        order, bit = [0], size // 2
    while bit:
        block = join(block, hop(block, "dp", bit))
        order = order + [i ^ bit for i in order]
        bit //= 2
    return block, order, later


def per_device(texts, w_qkv, w_out, w_self, w_neigh, neighbours, cotangent):
    node_dev, fan = neighbours.shape
    nodes = node_dev * lax.axis_size("dp")
    own = (w_out, w_self, w_neigh)
    even = (lax.axis_index("dp") // 2) % 2 == 0
    picked, w_out = lax.optimization_barrier((jnp.where(even, w_self, w_neigh), w_out))
    x_half = hop(picked, "mp", 2)
    x_out = hop(w_out, "mp", 2)
    here = tuple(hop(a, "mp", 1) for a in own)

    sent = attention(texts, w_qkv, cotangent, neighbours.T)[None]
    sent, here, x_half = lax.optimization_barrier((sent, here, x_half))
    sent, order, x_half = gather_dp(sent, x_half)
    sent, x_out = lax.optimization_barrier((sent, x_out))
    z_half = hop(x_half, "dp", 2)
    across = (x_out, x_half, z_half)
    there = tuple(hop(a, "mp", 1) for a in across)

    got_across = hop(sent, "mp", 2)
    got = (sent, hop(sent, "mp", 1), got_across, hop(got_across, "mp", 1))
    body = graph if nodes <= WIDE_LIMIT else graph_wide
    return body(order, fan, node_dev, got, (own, here, across, there))


def solution(mesh):
    return jax.shard_map(
        per_device,
        mesh=mesh,
        in_specs=(
            P("dp", None, None),
            P(None, "mp"),
            P("mp", None),
            P("mp", None),
            P("mp", None),
            P("dp", None),
            P("dp", "mp"),
        ),
        out_specs=(P("dp", "mp"), P("dp", "mp"), P("mp", None), P("mp", None), P("mp", None)),
        check_vma=False,
    )
```

```python
import functools

import jax
import jax.numpy as jnp
from jax import lax
from jax.experimental import pallas as pl
from jax.experimental.pallas import tpu as pltpu
from jax.sharding import PartitionSpec as P

HD = 64
BF = jnp.bfloat16
F32 = jnp.float32
NODES_STEP = 6
WIDE_LIMIT = 256
IDS_COLS = 128
IDS_AT = 32
TOP = 16
LOG2E = 1.4426950408889634
ATTENTION_VMEM = 58
MIB = 1 << 20


def dot_t(a, b):
    return lax.dot_general(a, b, (((1,), (1,)), ((), ())), preferred_element_type=F32)


def t_dot(a, b):
    return lax.dot_general(a, b, (((0,), (0,)), ((), ())), preferred_element_type=F32)


def dot(a, b):
    return jnp.dot(a, b, preferred_element_type=F32)


def attend(q, k, v, heads):
    seq, cols = q.shape
    lane = lax.broadcasted_iota(jnp.int32, (seq, cols), 1) // HD
    zero = jnp.zeros((seq, cols), BF)
    spread = jnp.concatenate([jnp.where(lane == h, k, zero) for h in range(heads)], axis=0)
    s = dot_t(spread, q).reshape(heads, seq, seq)
    e = jnp.exp2((s - jnp.max(s, axis=1, keepdims=True)) * (HD**-0.5 * LOG2E))
    p = (e * (1.0 / jnp.sum(e, axis=1, keepdims=True))).astype(BF)
    weight = jnp.sum(p.astype(F32), axis=2, keepdims=True)
    left = lax.broadcasted_iota(jnp.int32, (seq, 2 * HD), 1) < HD
    pairs = [jnp.where(left, weight[h], weight[h + 1]) for h in range(0, heads, 2)]
    context = jnp.concatenate(pairs, axis=1) * v.astype(F32)
    return jnp.sum(context, axis=0, keepdims=True) * (1.0 / seq)


def attention_kernel(heads, x_ref, w_ref, cot_ref, ids_ref, out_ref, wp, acc_p, acc_m):
    step = pl.program_id(0)
    nodes, seq, width = x_ref.shape
    node_dev = cot_ref.shape[0]
    cols = heads * HD

    @pl.when(step == 0)
    def _():
        for part in range(3):
            for h in range(0, heads, 2):
                a = h * 3 * HD + part * HD
                b = a + 3 * HD
                wp[:, part * cols + h * HD : part * cols + (h + 2) * HD] = jnp.concatenate(
                    [w_ref[:, a : a + HD], w_ref[:, b : b + HD]], axis=1
                )

    own = pl.ds(pl.multiple_of(lax.axis_index("mp") * cols, 128), cols)
    qkv = dot(x_ref[...].reshape(nodes * seq, width), wp[...]).astype(BF)
    for n in range(nodes):
        at = slice(n * seq, (n + 1) * seq)
        row = pl.ds(step * nodes + n, 1)
        acc_p[row, :] = attend(*(qkv[at, i * cols : (i + 1) * cols] for i in range(3)), heads)
        mean = jnp.sum(x_ref[n, :, own].astype(F32), axis=0, keepdims=True)
        acc_m[row, :] = mean * (1.0 / seq)

    @pl.when(step == pl.num_programs(0) - 1)
    def _():
        rows = jnp.concatenate([acc_p[...], cot_ref[...].astype(F32), acc_m[...]], axis=1)
        shifted = ids_ref[...] + 1
        fan = shifted.shape[0]
        gap = jnp.zeros((fan, IDS_AT - node_dev), F32)
        high, low = (shifted >> 4).astype(F32), (shifted & 15).astype(F32)
        blank = jnp.zeros((fan, IDS_COLS - 2 * IDS_AT), F32)
        ids = jnp.concatenate([high, gap, low, gap, blank], axis=1)
        wide = 3 * cols
        rest = jnp.concatenate([rows[TOP:, : wide // 2], rows[TOP:, wide // 2 :]], axis=0)
        out_ref[:, :wide] = rows[:TOP].astype(BF)
        out_ref[:, wide : wide + wide // 2] = rest.astype(BF)
        out_ref[:, wide + wide // 2 :] = ids.astype(BF)


def unpack(got, cols, part):
    got = got.astype(F32)
    wide, at = 3 * cols, part * cols
    pieces, left = [], at
    while left < at + cols:
        side, inside = divmod(left, wide // 2)
        right = min(at + cols, (side + 1) * (wide // 2))
        low = wide + inside
        pieces.append(got[:, side * (TOP // 2) : (side + 1) * (TOP // 2), low : low + right - left])
        left = right
    rest = jnp.concatenate(pieces, axis=2) if len(pieces) > 1 else pieces[0]
    return jnp.concatenate([got[:, :, at : at + cols], rest], axis=1)


def attention(texts, w_qkv, cotangent, ids):
    node_dev, seq, width = texts.shape
    cols = w_qkv.shape[1] // 3
    heads = cols // HD
    tokens = node_dev * seq
    nodes = NODES_STEP
    packed = (TOP, 3 * cols + 3 * cols // 2 + IDS_COLS)
    return pl.pallas_call(
        functools.partial(attention_kernel, heads),
        out_shape=jax.ShapeDtypeStruct(packed, BF),
        grid=(node_dev // nodes,),
        in_specs=[
            pl.BlockSpec((nodes, seq, width), lambda i: (i, 0, 0)),
            pl.BlockSpec((width, 3 * cols), lambda i: (0, 0)),
            pl.BlockSpec((node_dev, cols), lambda i: (0, 0)),
            pl.BlockSpec(ids.shape, lambda i: (0, 0)),
        ],
        out_specs=pl.BlockSpec(packed, lambda i: (0, 0)),
        scratch_shapes=[
            pltpu.VMEM((width, 3 * cols), BF),
            pltpu.VMEM((node_dev, cols), F32),
            pltpu.VMEM((node_dev, cols), F32),
        ],
        compiler_params=pltpu.CompilerParams(vmem_limit_bytes=ATTENTION_VMEM * MIB),
        cost_estimate=pl.CostEstimate(
            flops=2 * tokens * width * 3 * cols + 8 * tokens * seq * cols,
            bytes_accessed=2 * tokens * width + 6 * width * cols,
            transcendentals=tokens * seq * heads,
        ),
    )(texts, w_qkv, cotangent, ids)


def gelu_parts(z):
    root = 0.7978845608028654
    cube = 0.044715
    t = jnp.tanh(root * (z + cube * (z * z * z)))
    half = 0.5 * (1.0 + t)
    slope = half + 0.5 * z * (1.0 - t * t) * (root * (1.0 + 3.0 * cube * (z * z)))
    return z * half, slope


def block_place(r, cols):
    return pl.ds(pl.multiple_of((lax.axis_index("mp") ^ r) * cols, 128), cols)


def embed_kernel(order, fan, node_dev, *refs):
    parts = 4
    got, blocks, refs = refs[:parts], refs[parts : 2 * parts], refs[2 * parts :]
    both, cot, pooled_ref, counts_ref, share_ref, mean = refs
    dp = lax.axis_index("dp")
    groups = got[0].shape[0]
    nodes = groups * node_dev
    cols = blocks[0].shape[0]

    def part(r, i):
        return unpack(got[r][...], cols, i).reshape(nodes, cols)

    packed = got[0][:, :, got[0].shape[2] - IDS_COLS :].astype(F32)
    ids = jnp.concatenate(
        [
            packed[i, :fan, :node_dev] * 16.0 + packed[i, :fan, IDS_AT : IDS_AT + node_dev] - 1.0
            for i in range(groups)
        ],
        axis=1,
    )
    place_of = lax.broadcasted_iota(jnp.int32, (nodes, 1), 0)
    names = place_of
    for i, o in enumerate(order):
        shift = ((dp ^ o) - i) * node_dev
        inside = (place_of >= i * node_dev) & (place_of < (i + 1) * node_dev)
        names = jnp.where(inside, place_of + shift, names)
    names = names.astype(F32)
    counts_t = jnp.zeros((nodes, nodes), F32)
    for s in range(fan):
        counts_t += (ids[s : s + 1, :] == names).astype(F32)
    counts = counts_t.T
    share = 1.0 / jnp.maximum(jnp.sum(counts, axis=1, keepdims=True), 1.0)
    counts_ref[...] = counts_t.astype(BF)
    share_ref[...] = jnp.broadcast_to(share, share_ref.shape)

    pooled = [part(r, 0).astype(BF) for r in range(parts)]
    pooled_ref[...] = pooled[0]
    for r in range(parts):
        cot[:, block_place(r, cols)] = part(r, 1).astype(BF)
        mean[:, block_place(r, cols)] = part(r, 2)
    sums = sum(dot(pooled[r], blocks[r][...]) for r in range(parts))
    both[0] = (mean[...] + sums).astype(BF)
    both[1] = (dot(counts.astype(BF), both[0]) * share).astype(BF)


def graph_kernel(node_dev, both, cot, pooled, counts, share_ref, *refs):
    parts = 4
    blocks, refs = refs[: 2 * parts], refs[2 * parts :]
    mixed_ref, grad_ref, g_self, g_neigh, g_out, dz, wide, grads, sem = refs
    side = (lax.axis_index("dp") // 2) % 2
    cols, width = g_self.shape
    nodes = counts.shape[0]
    factor = 1.0 / jnp.sqrt(jnp.float32(nodes))
    own = block_place(0, cols)

    z = 0.0
    for r in range(parts):
        first = 0 if r < 2 else side
        z += dot(both[first, :, block_place(r, cols)], blocks[2 * r][...])
        z += dot(both[1 - first, :, block_place(r, cols)], blocks[2 * r + 1][...])
    mixed, slope = gelu_parts(z)
    dz[...] = (cot[...].astype(F32) * slope).astype(BF)
    wide[...] = mixed[:node_dev, :]
    mixed_ref[...] = wide[:, own].astype(BF)

    copies = []
    for i, out in enumerate((g_self, g_neigh)):
        grads[i] = t_dot(both[i, :, own], dz[...]) * factor
        copies.append(pltpu.make_async_copy(grads.at[i], out, sem.at[i]))
        copies[-1].start()
    share = share_ref[:, :1]
    for r in range(parts):
        to_self, to_agg = dot_t(dz[...], blocks[2 * r][...]), dot_t(dz[...], blocks[2 * r + 1][...])
        if r >= 2:
            even = side == 0
            to_self, to_agg = jnp.where(even, to_self, to_agg), jnp.where(even, to_agg, to_self)
        total = to_self + dot(counts[...], (to_agg * share).astype(BF))
        if r == 0:
            grad_ref[...] = total[:node_dev, :].astype(BF)
        at = slice(r * cols, (r + 1) * cols)
        grads[2, :, at] = t_dot(pooled[...], total.astype(BF)) * factor
        copies.append(
            pltpu.make_async_copy(grads.at[2, :, at], g_out.at[:, block_place(r, cols)], sem.at[2 + r])
        )
        copies[-1].start()
    for copy in copies:
        copy.wait()


def graph(order, fan, node_dev, got, weights):
    parts = len(got)
    cols, width = weights[0][0].shape
    nodes = got[0].shape[0] * node_dev
    vmem = pl.BlockSpec(memory_space=pltpu.VMEM)
    known = pl.pallas_call(
        functools.partial(embed_kernel, order, fan, node_dev),
        out_shape=(
            jax.ShapeDtypeStruct((2, nodes, width), BF),
            jax.ShapeDtypeStruct((nodes, width), BF),
            jax.ShapeDtypeStruct((nodes, cols), BF),
            jax.ShapeDtypeStruct((nodes, nodes), BF),
            jax.ShapeDtypeStruct((nodes, 128), F32),
        ),
        in_specs=[vmem] * (2 * parts),
        out_specs=(vmem,) * 5,
        scratch_shapes=[pltpu.VMEM((nodes, width), F32)],
        compiler_params=pltpu.CompilerParams(vmem_limit_bytes=24 * MIB),
        cost_estimate=pl.CostEstimate(
            flops=2 * nodes * width * width * 2, bytes_accessed=4 * MIB, transcendentals=0
        ),
    )(*got, *[group[0] for group in weights])
    slab = jax.ShapeDtypeStruct((node_dev, cols), BF)
    big = jax.ShapeDtypeStruct((cols, width), F32)
    anywhere = pl.BlockSpec(memory_space=pl.ANY)
    return pl.pallas_call(
        functools.partial(graph_kernel, node_dev),
        out_shape=(slab, slab, big, big, big),
        in_specs=[vmem] * (5 + 2 * parts),
        out_specs=(vmem, vmem, anywhere, anywhere, anywhere),
        scratch_shapes=[
            pltpu.VMEM((nodes, width), BF),
            pltpu.VMEM((node_dev, width), F32),
            pltpu.VMEM((3, cols, width), F32),
            pltpu.SemaphoreType.DMA((2 + parts,)),
        ],
        compiler_params=pltpu.CompilerParams(vmem_limit_bytes=36 * MIB),
        cost_estimate=pl.CostEstimate(
            flops=2 * nodes * width * width * 5, bytes_accessed=8 * MIB, transcendentals=nodes * width
        ),
    )(*known, *sum((group[1:] for group in weights), ()))


def graph_wide(order, fan, node_dev, got, weights):
    mp, dp = lax.axis_index("mp"), lax.axis_index("dp")
    parts = len(got)
    cols, width = weights[0][0].shape
    nodes = got[0].shape[0] * node_dev
    owners = jnp.array(order, jnp.int32) ^ dp
    names = (owners[:, None] * node_dev + jnp.arange(node_dev)[None, :]).reshape(1, 1, nodes)
    order = jnp.arange(parts) ^ mp
    even = (dp // 2) % 2 == 0
    kinds = [
        [group[0], jnp.where(even, group[1], group[2]), jnp.where(even, group[2], group[1])]
        for group in weights[2:]
    ]
    blocks = [*weights[:2], *kinds]
    w_out, w_self, w_neigh = (
        jnp.stack([group[k] for group in blocks])[order].reshape(width, width) for k in range(3)
    )

    def part(i):
        block = jnp.stack([unpack(g, cols, i) for g in got])[order]
        return block.transpose(1, 2, 0, 3).reshape(nodes, width)

    pooled = part(0).astype(BF)
    packed = got[0][:, :fan, got[0].shape[2] - IDS_COLS :].astype(jnp.int32)
    ids = packed[:, :, :node_dev] * 16 + packed[:, :, IDS_AT : IDS_AT + node_dev] - 1
    ids = ids.transpose(0, 2, 1).reshape(nodes, fan)
    cnt = jnp.maximum(jnp.sum(ids >= 0, axis=1).astype(F32), 1.0)[:, None]
    counts = jnp.sum(ids[:, :, None] == names, axis=1).astype(BF)
    embed = (part(2) + dot(pooled, w_out)).astype(BF)
    agg = (dot(counts, embed) / cnt).astype(BF)
    mixed, slope = gelu_parts(dot(embed, w_self) + dot(agg, w_neigh))
    dz = (part(1) * slope).astype(BF)
    msg = (dot_t(dz, w_neigh) / cnt).astype(BF)
    node_grad = (dot_t(dz, w_self) + t_dot(counts, msg)).astype(BF)
    factor = 1.0 / jnp.sqrt(jnp.float32(nodes))

    def own(a):
        return lax.dynamic_slice_in_dim(a, mp * cols, cols, 1)

    grads = [t_dot(own(a), b) * factor for a, b in ((embed, dz), (agg, dz), (pooled, node_grad))]
    return (own(mixed[:node_dev]).astype(BF), own(node_grad[:node_dev]), *grads)


def join_kernel(*refs):
    out, at = refs[-1], 0
    for ref in refs[:-1]:
        out[at : at + ref.shape[0]] = ref[...]
        at += ref.shape[0]


def join(*blocks):
    count = sum(b.shape[0] for b in blocks)
    if count > 8:
        return jnp.concatenate(blocks)
    vmem = pl.BlockSpec(memory_space=pltpu.VMEM)
    return pl.pallas_call(
        join_kernel,
        out_shape=jax.ShapeDtypeStruct((count, *blocks[0].shape[1:]), BF),
        in_specs=[vmem] * len(blocks),
        out_specs=vmem,
        compiler_params=pltpu.CompilerParams(vmem_limit_bytes=8 * MIB),
    )(*blocks)


def hop(x, axis, bit):
    return lax.ppermute(x, axis, [(i, i ^ bit) for i in range(lax.axis_size(axis))])


def gather_dp(block, later):
    size = lax.axis_size("dp")
    if size == 8:
        far = [hop(block, "dp", i) for i in (2, 4, 6)]
        mine = join(block)
        mine, far, later = lax.optimization_barrier((mine, far, later))
        block = join(mine, *far)
        order, bit = [0, 2, 4, 6], 1
    else:
        order, bit = [0], size // 2
    while bit:
        block = join(block, hop(block, "dp", bit))
        order = order + [i ^ bit for i in order]
        bit //= 2
    return block, order, later


def per_device(texts, w_qkv, w_out, w_self, w_neigh, neighbours, cotangent):
    node_dev, fan = neighbours.shape
    nodes = node_dev * lax.axis_size("dp")
    own = (w_out, w_self, w_neigh)
    even = (lax.axis_index("dp") // 2) % 2 == 0
    picked, w_out = lax.optimization_barrier((jnp.where(even, w_self, w_neigh), w_out))
    x_half = hop(picked, "mp", 2)
    x_out = hop(w_out, "mp", 2)
    here = tuple(hop(a, "mp", 1) for a in own)

    sent = attention(texts, w_qkv, cotangent, neighbours.T)[None]
    sent, here, x_half = lax.optimization_barrier((sent, here, x_half))
    sent, order, x_half = gather_dp(sent, x_half)
    sent, x_out = lax.optimization_barrier((sent, x_out))
    z_half = hop(x_half, "dp", 2)
    across = (x_out, x_half, z_half)
    there = tuple(hop(a, "mp", 1) for a in across)

    got_across = hop(sent, "mp", 2)
    got = (sent, hop(sent, "mp", 1), got_across, hop(got_across, "mp", 1))
    body = graph if nodes <= WIDE_LIMIT else graph_wide
    return body(order, fan, node_dev, got, (own, here, across, there))


def solution(mesh):
    return jax.shard_map(
        per_device,
        mesh=mesh,
        in_specs=(
            P("dp", None, None),
            P(None, "mp"),
            P("mp", None),
            P("mp", None),
            P("mp", None),
            P("dp", None),
            P("dp", "mp"),
        ),
        out_specs=(P("dp", "mp"), P("dp", "mp"), P("mp", None), P("mp", None), P("mp", None)),
        check_vma=False,
    )
```

```python
import functools

import jax
import jax.numpy as jnp
from jax import lax
from jax.experimental import pallas as pl
from jax.experimental.pallas import tpu as pltpu
from jax.sharding import PartitionSpec as P

HD = 64
BF = jnp.bfloat16
F32 = jnp.float32
NODES_STEP = 8
IDS_COLS = 128
IDS_AT = 32
TOP = 16
LOG2E = 1.4426950408889634
ATTENTION_VMEM = 58
MIB = 1 << 20


def dot_t(a, b):
    return lax.dot_general(a, b, (((1,), (1,)), ((), ())), preferred_element_type=F32)


def t_dot(a, b):
    return lax.dot_general(a, b, (((0,), (0,)), ((), ())), preferred_element_type=F32)


def dot(a, b):
    return jnp.dot(a, b, preferred_element_type=F32)


def attend(q, k, v):
    seq, cols = q.shape
    pair = 2 * HD
    left = lax.broadcasted_iota(jnp.int32, (seq, pair), 1) < HD
    zero = jnp.zeros((seq, pair), BF)
    out = []
    for at in range(0, cols, pair):
        both = q[:, at : at + pair]
        spread = jnp.concatenate([jnp.where(left, both, zero), jnp.where(left, zero, both)], axis=0)
        s = dot_t(k[:, at : at + pair], spread)
        e = jnp.exp2((s - jnp.max(s, axis=0, keepdims=True)) * (HD**-0.5 * LOG2E))
        p = (e * (1.0 / jnp.sum(e, axis=0, keepdims=True))).astype(BF).astype(F32)
        first = jnp.sum(p[:, :seq], axis=1, keepdims=True)
        second = jnp.sum(p[:, seq:], axis=1, keepdims=True)
        context = jnp.where(left, first, second) * v[:, at : at + pair].astype(F32)
        out.append(jnp.sum(context, axis=0, keepdims=True) * (1.0 / seq))
    return jnp.concatenate(out, axis=1)


def attention_kernel(heads, x_ref, w_ref, cot_ref, ids_ref, out_ref, wp, acc_p, acc_m):
    step = pl.program_id(0)
    nodes, seq, width = x_ref.shape
    node_dev = cot_ref.shape[0]
    cols = heads * HD

    @pl.when(step == 0)
    def _():
        for part in range(3):
            for h in range(0, heads, 2):
                a = h * 3 * HD + part * HD
                b = a + 3 * HD
                wp[:, part * cols + h * HD : part * cols + (h + 2) * HD] = jnp.concatenate(
                    [w_ref[:, a : a + HD], w_ref[:, b : b + HD]], axis=1
                )

    own = pl.ds(pl.multiple_of(lax.axis_index("mp") * cols, 128), cols)
    qkv = dot(x_ref[...].reshape(nodes * seq, width), wp[...]).astype(BF)
    for n in range(nodes):
        at = slice(n * seq, (n + 1) * seq)
        row = pl.ds(step * nodes + n, 1)
        acc_p[row, :] = attend(*(qkv[at, i * cols : (i + 1) * cols] for i in range(3)))
        mean = jnp.sum(x_ref[n, :, own].astype(F32), axis=0, keepdims=True)
        acc_m[row, :] = mean * (1.0 / seq)

    @pl.when(step == pl.num_programs(0) - 1)
    def _():
        rows = jnp.concatenate([acc_p[...], cot_ref[...].astype(F32), acc_m[...]], axis=1)
        shifted = ids_ref[...] + 1
        fan = shifted.shape[0]
        gap = jnp.zeros((fan, IDS_AT - node_dev), F32)
        high, low = (shifted >> 4).astype(F32), (shifted & 15).astype(F32)
        blank = jnp.zeros((fan, IDS_COLS - 2 * IDS_AT), F32)
        ids = jnp.concatenate([high, gap, low, gap, blank], axis=1)
        wide = 3 * cols
        rest = jnp.concatenate([rows[TOP:, : wide // 2], rows[TOP:, wide // 2 :]], axis=0)
        out_ref[:, :wide] = rows[:TOP].astype(BF)
        out_ref[:, wide : wide + wide // 2] = rest.astype(BF)
        out_ref[:, wide + wide // 2 :] = ids.astype(BF)


def unpack(got, cols, part):
    got = got.astype(F32)
    wide, at = 3 * cols, part * cols
    pieces, left = [], at
    while left < at + cols:
        side, inside = divmod(left, wide // 2)
        right = min(at + cols, (side + 1) * (wide // 2))
        low = wide + inside
        pieces.append(got[:, side * (TOP // 2) : (side + 1) * (TOP // 2), low : low + right - left])
        left = right
    rest = jnp.concatenate(pieces, axis=2) if len(pieces) > 1 else pieces[0]
    return jnp.concatenate([got[:, :, at : at + cols], rest], axis=1)


def attention(texts, w_qkv, cotangent, ids):
    node_dev, seq, width = texts.shape
    cols = w_qkv.shape[1] // 3
    heads = cols // HD
    tokens = node_dev * seq
    nodes = NODES_STEP
    packed = (TOP, 3 * cols + 3 * cols // 2 + IDS_COLS)
    return pl.pallas_call(
        functools.partial(attention_kernel, heads),
        out_shape=jax.ShapeDtypeStruct(packed, BF),
        grid=(node_dev // nodes,),
        in_specs=[
            pl.BlockSpec((nodes, seq, width), lambda i: (i, 0, 0)),
            pl.BlockSpec((width, 3 * cols), lambda i: (0, 0)),
            pl.BlockSpec((node_dev, cols), lambda i: (0, 0)),
            pl.BlockSpec(ids.shape, lambda i: (0, 0)),
        ],
        out_specs=pl.BlockSpec(packed, lambda i: (0, 0)),
        scratch_shapes=[
            pltpu.VMEM((width, 3 * cols), BF),
            pltpu.VMEM((node_dev, cols), F32),
            pltpu.VMEM((node_dev, cols), F32),
        ],
        compiler_params=pltpu.CompilerParams(vmem_limit_bytes=ATTENTION_VMEM * MIB),
        cost_estimate=pl.CostEstimate(
            flops=2 * tokens * width * 3 * cols + 8 * tokens * seq * cols,
            bytes_accessed=2 * tokens * width + 6 * width * cols,
            transcendentals=tokens * seq * heads,
        ),
    )(texts, w_qkv, cotangent, ids)


def gelu_parts(z):
    root = 0.7978845608028654
    cube = 0.044715
    t = jnp.tanh(root * (z + cube * (z * z * z)))
    half = 0.5 * (1.0 + t)
    slope = half + 0.5 * z * (1.0 - t * t) * (root * (1.0 + 3.0 * cube * (z * z)))
    return z * half, slope


def block_place(r, cols):
    return pl.ds(pl.multiple_of((lax.axis_index("mp") ^ r) * cols, 128), cols)


def embed_kernel(order, fan, node_dev, *refs):
    parts, near, far, diagonal = 4, refs[0:2], refs[2:4], refs[4:6]
    blocks, refs = refs[6 : 6 + parts], refs[6 + parts :]
    both, cot, pooled_ref, counts_ref, share_ref, mean = refs
    dp = lax.axis_index("dp")
    some = near[0].shape[0]
    groups = 2 * some
    nodes = groups * node_dev
    cols = blocks[0].shape[0]

    def payload(r):
        core = r % 2
        if r < 2:
            pieces = [near[core][...], far[core][:some]]
        else:
            pieces = [far[core][some:], diagonal[core][...]]
        return jnp.concatenate(pieces, axis=0)

    got = [payload(r) for r in range(parts)]

    def part(r, i):
        return unpack(got[r], cols, i).reshape(nodes, cols)

    packed = got[0][:, :, got[0].shape[2] - IDS_COLS :].astype(F32)
    ids = jnp.concatenate(
        [
            packed[i, :fan, :node_dev] * 16.0 + packed[i, :fan, IDS_AT : IDS_AT + node_dev] - 1.0
            for i in range(groups)
        ],
        axis=1,
    )
    place_of = lax.broadcasted_iota(jnp.int32, (nodes, 1), 0)
    names = place_of
    for i, o in enumerate(order):
        shift = ((dp ^ o) - i) * node_dev
        inside = (place_of >= i * node_dev) & (place_of < (i + 1) * node_dev)
        names = jnp.where(inside, place_of + shift, names)
    names = names.astype(F32)
    counts_t = jnp.zeros((nodes, nodes), F32)
    for s in range(fan):
        counts_t += (ids[s : s + 1, :] == names).astype(F32)
    counts = counts_t.T
    share = 1.0 / jnp.maximum(jnp.sum(counts, axis=1, keepdims=True), 1.0)
    counts_ref[...] = counts_t.astype(BF)
    share_ref[...] = jnp.broadcast_to(share, share_ref.shape)

    pooled = [part(r, 0).astype(BF) for r in range(parts)]
    pooled_ref[...] = pooled[0]
    for r in range(parts):
        cot[:, block_place(r, cols)] = part(r, 1).astype(BF)
        mean[:, block_place(r, cols)] = part(r, 2)
    sums = sum(dot(pooled[r], blocks[r][...]) for r in range(parts))
    both[0] = (mean[...] + sums).astype(BF)
    both[1] = (dot(counts.astype(BF), both[0]) * share).astype(BF)


def graph_kernel(node_dev, both, cot, pooled, counts, share_ref, *refs):
    parts = 4
    blocks, refs = refs[: 2 * parts], refs[2 * parts :]
    mixed_ref, grad_ref, g_self, g_neigh, g_out, dz, wide, grads, sem = refs
    side = (lax.axis_index("dp") // 2) % 2
    cols, width = g_self.shape
    nodes = counts.shape[0]
    factor = 1.0 / jnp.sqrt(jnp.float32(nodes))
    own = block_place(0, cols)

    z = 0.0
    for r in range(parts):
        first = 0 if r < 2 else side
        z += dot(both[first, :, block_place(r, cols)], blocks[2 * r][...])
        z += dot(both[1 - first, :, block_place(r, cols)], blocks[2 * r + 1][...])
    mixed, slope = gelu_parts(z)
    dz[...] = (cot[...].astype(F32) * slope).astype(BF)
    wide[...] = mixed[:node_dev, :]
    mixed_ref[...] = wide[:, own].astype(BF)

    copies = []
    for i, out in enumerate((g_self, g_neigh)):
        grads[i] = t_dot(both[i, :, own], dz[...]) * factor
        copies.append(pltpu.make_async_copy(grads.at[i], out, sem.at[i]))
        copies[-1].start()
    share = share_ref[:, :1]
    for r in range(parts):
        to_self, to_agg = dot_t(dz[...], blocks[2 * r][...]), dot_t(dz[...], blocks[2 * r + 1][...])
        if r >= 2:
            even = side == 0
            to_self, to_agg = jnp.where(even, to_self, to_agg), jnp.where(even, to_agg, to_self)
        total = to_self + dot(counts[...], (to_agg * share).astype(BF))
        if r == 0:
            grad_ref[...] = total[:node_dev, :].astype(BF)
        at = slice(r * cols, (r + 1) * cols)
        grads[2, :, at] = t_dot(pooled[...], total.astype(BF)) * factor
        copies.append(
            pltpu.make_async_copy(grads.at[2, :, at], g_out.at[:, block_place(r, cols)], sem.at[2 + r])
        )
        copies[-1].start()
    for copy in copies:
        copy.wait()


def graph(order, fan, node_dev, got, weights):
    parts = len(weights)
    cols, width = weights[0][0].shape
    nodes = len(order) * node_dev
    vmem = pl.BlockSpec(memory_space=pltpu.VMEM)
    known = pl.pallas_call(
        functools.partial(embed_kernel, order, fan, node_dev),
        out_shape=(
            jax.ShapeDtypeStruct((2, nodes, width), BF),
            jax.ShapeDtypeStruct((nodes, width), BF),
            jax.ShapeDtypeStruct((nodes, cols), BF),
            jax.ShapeDtypeStruct((nodes, nodes), BF),
            jax.ShapeDtypeStruct((nodes, 128), F32),
        ),
        in_specs=[vmem] * (len(got) + parts),
        out_specs=(vmem,) * 5,
        scratch_shapes=[pltpu.VMEM((nodes, width), F32)],
        compiler_params=pltpu.CompilerParams(vmem_limit_bytes=24 * MIB),
        cost_estimate=pl.CostEstimate(
            flops=2 * nodes * width * width * 2, bytes_accessed=4 * MIB, transcendentals=0
        ),
    )(*got, *[group[0] for group in weights])
    slab = jax.ShapeDtypeStruct((node_dev, cols), BF)
    big = jax.ShapeDtypeStruct((cols, width), F32)
    anywhere = pl.BlockSpec(memory_space=pl.ANY)
    return pl.pallas_call(
        functools.partial(graph_kernel, node_dev),
        out_shape=(slab, slab, big, big, big),
        in_specs=[vmem] * (5 + 2 * parts),
        out_specs=(vmem, vmem, anywhere, anywhere, anywhere),
        scratch_shapes=[
            pltpu.VMEM((nodes, width), BF),
            pltpu.VMEM((node_dev, width), F32),
            pltpu.VMEM((3, cols, width), F32),
            pltpu.SemaphoreType.DMA((2 + parts,)),
        ],
        compiler_params=pltpu.CompilerParams(vmem_limit_bytes=36 * MIB),
        cost_estimate=pl.CostEstimate(
            flops=2 * nodes * width * width * 5, bytes_accessed=8 * MIB, transcendentals=nodes * width
        ),
    )(*known, *sum((group[1:] for group in weights), ()))


def graph_wide(order, fan, node_dev, got, weights):
    mp, dp = lax.axis_index("mp"), lax.axis_index("dp")
    parts = len(got)
    cols, width = weights[0][0].shape
    nodes = got[0].shape[0] * node_dev
    owners = jnp.array(order, jnp.int32) ^ dp
    names = (owners[:, None] * node_dev + jnp.arange(node_dev)[None, :]).reshape(1, 1, nodes)
    order = jnp.arange(parts) ^ mp
    even = (dp // 2) % 2 == 0
    kinds = [
        [group[0], jnp.where(even, group[1], group[2]), jnp.where(even, group[2], group[1])]
        for group in weights[2:]
    ]
    blocks = [*weights[:2], *kinds]
    w_out, w_self, w_neigh = (
        jnp.stack([group[k] for group in blocks])[order].reshape(width, width) for k in range(3)
    )

    def part(i):
        block = jnp.stack([unpack(g, cols, i) for g in got])[order]
        return block.transpose(1, 2, 0, 3).reshape(nodes, width)

    pooled = part(0).astype(BF)
    packed = got[0][:, :fan, got[0].shape[2] - IDS_COLS :].astype(jnp.int32)
    ids = packed[:, :, :node_dev] * 16 + packed[:, :, IDS_AT : IDS_AT + node_dev] - 1
    ids = ids.transpose(0, 2, 1).reshape(nodes, fan)
    cnt = jnp.maximum(jnp.sum(ids >= 0, axis=1).astype(F32), 1.0)[:, None]
    counts = jnp.sum(ids[:, :, None] == names, axis=1).astype(BF)
    embed = (part(2) + dot(pooled, w_out)).astype(BF)
    agg = (dot(counts, embed) / cnt).astype(BF)
    mixed, slope = gelu_parts(dot(embed, w_self) + dot(agg, w_neigh))
    dz = (part(1) * slope).astype(BF)
    msg = (dot_t(dz, w_neigh) / cnt).astype(BF)
    node_grad = (dot_t(dz, w_self) + t_dot(counts, msg)).astype(BF)
    factor = 1.0 / jnp.sqrt(jnp.float32(nodes))

    def own(a):
        return lax.dynamic_slice_in_dim(a, mp * cols, cols, 1)

    grads = [t_dot(own(a), b) * factor for a, b in ((embed, dz), (agg, dz), (pooled, node_grad))]
    return (own(mixed[:node_dev]).astype(BF), own(node_grad[:node_dev]), *grads)


def join_kernel(*refs):
    out, at = refs[-1], 0
    for ref in refs[:-1]:
        out[at : at + ref.shape[0]] = ref[...]
        at += ref.shape[0]


def join(*blocks):
    count = sum(b.shape[0] for b in blocks)
    if count > 8:
        return jnp.concatenate(blocks)
    vmem = pl.BlockSpec(memory_space=pltpu.VMEM)
    return pl.pallas_call(
        join_kernel,
        out_shape=jax.ShapeDtypeStruct((count, *blocks[0].shape[1:]), BF),
        in_specs=[vmem] * len(blocks),
        out_specs=vmem,
        compiler_params=pltpu.CompilerParams(vmem_limit_bytes=8 * MIB),
    )(*blocks)


def hop(x, axis, bit):
    return lax.ppermute(x, axis, [(i, i ^ bit) for i in range(lax.axis_size(axis))])


def cross_kernel(y, x, y_part, x_part, both):
    half = y.shape[0] // 2
    y_part[...] = y[:half]
    x_part[...] = x[half:]
    both[: 2 * half] = y[...]
    both[2 * half :] = x[...]


def cross(y, x):
    count, rows, cols = y.shape
    vmem = pl.BlockSpec(memory_space=pltpu.VMEM)
    half = jax.ShapeDtypeStruct((count // 2, rows, cols), BF)
    return pl.pallas_call(
        cross_kernel,
        out_shape=(half, half, jax.ShapeDtypeStruct((2 * count, rows, cols), BF)),
        in_specs=[vmem] * 2,
        out_specs=(vmem,) * 3,
        compiler_params=pltpu.CompilerParams(vmem_limit_bytes=8 * MIB),
    )(y, x)


def core(x):
    return hop(x, "mp", 1)


def gather(block, x_half, x_out):
    z = [hop(block, "dp", i) for i in (2, 4, 6)]
    mine = join(block)
    mine, z, x_half = lax.optimization_barrier((mine, z, x_half))
    block = join(mine, *z)
    order = [0, 2, 4, 6, 1, 3, 5, 7]
    z_half = hop(x_half, "dp", 2)
    y, x, same = hop(block, "dp", 1), hop(block, "mp", 2), core(block)
    y_part, x_part, far = cross(y, x)
    y_part, x_out = lax.optimization_barrier((y_part, x_out))
    y_part, x_part = hop(y_part, "mp", 2), hop(x_part, "dp", 1)
    far = join(far)
    far, x_half, x_out = lax.optimization_barrier((far, x_half, x_out))
    core_far = core(far)
    y_part, x_part, core_far, same = lax.optimization_barrier((y_part, x_part, core_far, same))
    diagonal = join(y_part, x_part)
    z_half, core_diagonal = lax.optimization_barrier((z_half, core(diagonal)))
    got = (block, same, far, core_far, diagonal, core_diagonal)
    return got, order, (x_out, x_half, z_half), (core(x_out), core(x_half), core(z_half))


def gather_wide(block):
    order, bit = [0], lax.axis_size("dp") // 2
    while bit:
        block = join(block, hop(block, "dp", bit))
        order = order + [i ^ bit for i in order]
        bit //= 2
    across = hop(block, "mp", 2)
    return (block, hop(block, "mp", 1), across, hop(across, "mp", 1)), order


def per_device(texts, w_qkv, w_out, w_self, w_neigh, neighbours, cotangent):
    node_dev, fan = neighbours.shape
    own = (w_out, w_self, w_neigh)
    even = (lax.axis_index("dp") // 2) % 2 == 0
    picked, w_out = lax.optimization_barrier((jnp.where(even, w_self, w_neigh), w_out))
    x_half = hop(picked, "mp", 2)
    x_out = hop(w_out, "mp", 2)
    here = tuple(core(a) for a in own)

    sent = attention(texts, w_qkv, cotangent, neighbours.T)[None]
    sent, here, x_half = lax.optimization_barrier((sent, here, x_half))
    if lax.axis_size("dp") == 8:
        got, order, across, there = gather(sent, x_half, x_out)
        return graph(order, fan, node_dev, got, (own, here, across, there))
    got, order = gather_wide(sent)
    across = (x_out, x_half, hop(x_half, "dp", 2))
    there = tuple(core(a) for a in across)
    return graph_wide(order, fan, node_dev, got, (own, here, across, there))


def solution(mesh):
    return jax.shard_map(
        per_device,
        mesh=mesh,
        in_specs=(
            P("dp", None, None),
            P(None, "mp"),
            P("mp", None),
            P("mp", None),
            P("mp", None),
            P("dp", None),
            P("dp", "mp"),
        ),
        out_specs=(P("dp", "mp"), P("dp", "mp"), P("mp", None), P("mp", None), P("mp", None)),
        check_vma=False,
    )
```

```python
import functools

import jax
import jax.numpy as jnp
from jax import lax
from jax.experimental import pallas as pl
from jax.experimental.pallas import tpu as pltpu
from jax.sharding import PartitionSpec as P

HD = 64
BF = jnp.bfloat16
F32 = jnp.float32
NODES_STEP = 8
WIDE_LIMIT = 256
IDS_COLS = 128
IDS_AT = 32
TOP = 16
LOG2E = 1.4426950408889634
ATTENTION_VMEM = 50
MIB = 1 << 20


def dot_t(a, b):
    return lax.dot_general(a, b, (((1,), (1,)), ((), ())), preferred_element_type=F32)


def t_dot(a, b):
    return lax.dot_general(a, b, (((0,), (0,)), ((), ())), preferred_element_type=F32)


def dot(a, b):
    return jnp.dot(a, b, preferred_element_type=F32)


def attend(q, k, v):
    seq, cols = q.shape
    pair = 2 * HD
    left = lax.broadcasted_iota(jnp.int32, (seq, pair), 1) < HD
    zero = jnp.zeros((seq, pair), BF)
    out = []
    for at in range(0, cols, pair):
        both = q[:, at : at + pair]
        spread = jnp.concatenate([jnp.where(left, both, zero), jnp.where(left, zero, both)], axis=0)
        s = dot_t(k[:, at : at + pair], spread)
        e = jnp.exp2((s - jnp.max(s, axis=0, keepdims=True)) * (HD**-0.5 * LOG2E))
        p = (e * (1.0 / jnp.sum(e, axis=0, keepdims=True))).astype(BF).astype(F32)
        first = jnp.sum(p[:, :seq], axis=1, keepdims=True)
        second = jnp.sum(p[:, seq:], axis=1, keepdims=True)
        context = jnp.where(left, first, second) * v[:, at : at + pair].astype(F32)
        out.append(jnp.sum(context, axis=0, keepdims=True) * (1.0 / seq))
    return jnp.concatenate(out, axis=1)


def attention_kernel(
    heads, texts_ref, w_ref, cot_ref, ids_ref, out_ref, wp, acc_p, acc_m, held, sem
):
    step = pl.program_id(0)
    nodes, seq, width = held.shape[1:]
    node_dev = cot_ref.shape[0]
    cols = heads * HD

    def fetch(i):
        source = texts_ref.at[pl.ds(i * nodes, nodes)]
        return pltpu.make_async_copy(source, held.at[i % 2], sem.at[i % 2])

    @pl.when(step == 0)
    def _():
        fetch(0).start()
        for part in range(3):
            for h in range(0, heads, 2):
                a = h * 3 * HD + part * HD
                b = a + 3 * HD
                wp[:, part * cols + h * HD : part * cols + (h + 2) * HD] = jnp.concatenate(
                    [w_ref[:, a : a + HD], w_ref[:, b : b + HD]], axis=1
                )

    @pl.when(step + 1 < pl.num_programs(0))
    def _():
        fetch(step + 1).start()

    fetch(step).wait()
    x_ref = held.at[step % 2]
    own = pl.ds(pl.multiple_of(lax.axis_index("mp") * cols, 128), cols)
    qkv = dot(x_ref[...].reshape(nodes * seq, width), wp[...]).astype(BF)
    for n in range(nodes):
        at = slice(n * seq, (n + 1) * seq)
        row = pl.ds(step * nodes + n, 1)
        acc_p[row, :] = attend(*(qkv[at, i * cols : (i + 1) * cols] for i in range(3)))
        mean = jnp.sum(x_ref[n, :, own].astype(F32), axis=0, keepdims=True)
        acc_m[row, :] = mean * (1.0 / seq)

    @pl.when(step == pl.num_programs(0) - 1)
    def _():
        rows = jnp.concatenate([acc_p[...], cot_ref[...].astype(F32), acc_m[...]], axis=1)
        shifted = ids_ref[...] + 1
        fan = shifted.shape[0]
        gap = jnp.zeros((fan, IDS_AT - node_dev), F32)
        high, low = (shifted >> 4).astype(F32), (shifted & 15).astype(F32)
        blank = jnp.zeros((fan, IDS_COLS - 2 * IDS_AT), F32)
        ids = jnp.concatenate([high, gap, low, gap, blank], axis=1)
        wide = 3 * cols
        rest = jnp.concatenate([rows[TOP:, : wide // 2], rows[TOP:, wide // 2 :]], axis=0)
        out_ref[:, :wide] = rows[:TOP].astype(BF)
        out_ref[:, wide : wide + wide // 2] = rest.astype(BF)
        out_ref[:, wide + wide // 2 :] = ids.astype(BF)


def unpack(got, cols, part):
    got = got.astype(F32)
    wide, at = 3 * cols, part * cols
    pieces, left = [], at
    while left < at + cols:
        side, inside = divmod(left, wide // 2)
        right = min(at + cols, (side + 1) * (wide // 2))
        low = wide + inside
        pieces.append(got[:, side * (TOP // 2) : (side + 1) * (TOP // 2), low : low + right - left])
        left = right
    rest = jnp.concatenate(pieces, axis=2) if len(pieces) > 1 else pieces[0]
    return jnp.concatenate([got[:, :, at : at + cols], rest], axis=1)


def attention(texts, w_qkv, cotangent, ids):
    node_dev, seq, width = texts.shape
    cols = w_qkv.shape[1] // 3
    heads = cols // HD
    tokens = node_dev * seq
    nodes = NODES_STEP
    packed = (TOP, 3 * cols + 3 * cols // 2 + IDS_COLS)
    return pl.pallas_call(
        functools.partial(attention_kernel, heads),
        out_shape=jax.ShapeDtypeStruct(packed, BF),
        grid=(node_dev // nodes,),
        in_specs=[
            pl.BlockSpec(memory_space=pl.ANY),
            pl.BlockSpec((width, 3 * cols), lambda i: (0, 0)),
            pl.BlockSpec((node_dev, cols), lambda i: (0, 0)),
            pl.BlockSpec(ids.shape, lambda i: (0, 0)),
        ],
        out_specs=pl.BlockSpec(packed, lambda i: (0, 0)),
        scratch_shapes=[
            pltpu.VMEM((width, 3 * cols), BF),
            pltpu.VMEM((node_dev, cols), F32),
            pltpu.VMEM((node_dev, cols), F32),
            pltpu.VMEM((2, nodes, seq, width), BF),
            pltpu.SemaphoreType.DMA((2,)),
        ],
        compiler_params=pltpu.CompilerParams(vmem_limit_bytes=ATTENTION_VMEM * MIB),
        cost_estimate=pl.CostEstimate(
            flops=2 * tokens * width * 3 * cols + 8 * tokens * seq * cols,
            bytes_accessed=2 * tokens * width + 6 * width * cols,
            transcendentals=tokens * seq * heads,
        ),
    )(texts, w_qkv, cotangent, ids)


def gelu_parts(z):
    root = 0.7978845608028654
    cube = 0.044715
    t = jnp.tanh(root * (z + cube * (z * z * z)))
    half = 0.5 * (1.0 + t)
    slope = half + 0.5 * z * (1.0 - t * t) * (root * (1.0 + 3.0 * cube * (z * z)))
    return z * half, slope


def block_place(r, cols):
    return pl.ds(pl.multiple_of((lax.axis_index("mp") ^ r) * cols, 128), cols)


def embed_kernel(order, fan, node_dev, *refs):
    parts = 4
    got, blocks, refs = refs[:parts], refs[parts : 2 * parts], refs[2 * parts :]
    both, cot, pooled_ref, counts_ref, share_ref, mean = refs
    dp = lax.axis_index("dp")
    groups = got[0].shape[0]
    nodes = groups * node_dev
    cols = blocks[0].shape[0]

    def part(r, i):
        return unpack(got[r][...], cols, i).reshape(nodes, cols)

    packed = got[0][:, :, got[0].shape[2] - IDS_COLS :].astype(F32)
    ids = jnp.concatenate(
        [
            packed[i, :fan, :node_dev] * 16.0 + packed[i, :fan, IDS_AT : IDS_AT + node_dev] - 1.0
            for i in range(groups)
        ],
        axis=1,
    )
    place_of = lax.broadcasted_iota(jnp.int32, (nodes, 1), 0)
    names = place_of
    for i, o in enumerate(order):
        shift = ((dp ^ o) - i) * node_dev
        inside = (place_of >= i * node_dev) & (place_of < (i + 1) * node_dev)
        names = jnp.where(inside, place_of + shift, names)
    names = names.astype(F32)
    counts_t = jnp.zeros((nodes, nodes), F32)
    for s in range(fan):
        counts_t += (ids[s : s + 1, :] == names).astype(F32)
    counts = counts_t.T
    share = 1.0 / jnp.maximum(jnp.sum(counts, axis=1, keepdims=True), 1.0)
    counts_ref[...] = counts_t.astype(BF)
    share_ref[...] = jnp.broadcast_to(share, share_ref.shape)

    pooled = [part(r, 0).astype(BF) for r in range(parts)]
    pooled_ref[...] = pooled[0]
    for r in range(parts):
        cot[:, block_place(r, cols)] = part(r, 1).astype(BF)
        mean[:, block_place(r, cols)] = part(r, 2)
    sums = sum(dot(pooled[r], blocks[r][...]) for r in range(parts))
    both[0] = (mean[...] + sums).astype(BF)
    both[1] = (dot(counts.astype(BF), both[0]) * share).astype(BF)


def graph_kernel(node_dev, both, cot, pooled, counts, share_ref, *refs):
    parts = 4
    blocks, refs = refs[: 2 * parts], refs[2 * parts :]
    mixed_ref, grad_ref, g_self, g_neigh, g_out, dz, wide, grads, sem = refs
    side = (lax.axis_index("dp") // 2) % 2
    cols, width = g_self.shape
    nodes = counts.shape[0]
    factor = 1.0 / jnp.sqrt(jnp.float32(nodes))
    own = block_place(0, cols)

    z = 0.0
    for r in range(parts):
        first = 0 if r < 2 else side
        z += dot(both[first, :, block_place(r, cols)], blocks[2 * r][...])
        z += dot(both[1 - first, :, block_place(r, cols)], blocks[2 * r + 1][...])
    mixed, slope = gelu_parts(z)
    dz[...] = (cot[...].astype(F32) * slope).astype(BF)
    wide[...] = mixed[:node_dev, :]
    mixed_ref[...] = wide[:, own].astype(BF)

    copies = []
    for i, out in enumerate((g_self, g_neigh)):
        grads[i] = t_dot(both[i, :, own], dz[...]) * factor
        copies.append(pltpu.make_async_copy(grads.at[i], out, sem.at[i]))
        copies[-1].start()
    share = share_ref[:, :1]
    for r in range(parts):
        to_self, to_agg = dot_t(dz[...], blocks[2 * r][...]), dot_t(dz[...], blocks[2 * r + 1][...])
        if r >= 2:
            even = side == 0
            to_self, to_agg = jnp.where(even, to_self, to_agg), jnp.where(even, to_agg, to_self)
        total = to_self + dot(counts[...], (to_agg * share).astype(BF))
        if r == 0:
            grad_ref[...] = total[:node_dev, :].astype(BF)
        at = slice(r * cols, (r + 1) * cols)
        grads[2, :, at] = t_dot(pooled[...], total.astype(BF)) * factor
        copies.append(
            pltpu.make_async_copy(grads.at[2, :, at], g_out.at[:, block_place(r, cols)], sem.at[2 + r])
        )
        copies[-1].start()
    for copy in copies:
        copy.wait()


def graph(order, fan, node_dev, got, weights):
    parts = len(got)
    cols, width = weights[0][0].shape
    nodes = got[0].shape[0] * node_dev
    vmem = pl.BlockSpec(memory_space=pltpu.VMEM)
    known = pl.pallas_call(
        functools.partial(embed_kernel, order, fan, node_dev),
        out_shape=(
            jax.ShapeDtypeStruct((2, nodes, width), BF),
            jax.ShapeDtypeStruct((nodes, width), BF),
            jax.ShapeDtypeStruct((nodes, cols), BF),
            jax.ShapeDtypeStruct((nodes, nodes), BF),
            jax.ShapeDtypeStruct((nodes, 128), F32),
        ),
        in_specs=[vmem] * (2 * parts),
        out_specs=(vmem,) * 5,
        scratch_shapes=[pltpu.VMEM((nodes, width), F32)],
        compiler_params=pltpu.CompilerParams(vmem_limit_bytes=24 * MIB),
        cost_estimate=pl.CostEstimate(
            flops=2 * nodes * width * width * 2, bytes_accessed=4 * MIB, transcendentals=0
        ),
    )(*got, *[group[0] for group in weights])
    slab = jax.ShapeDtypeStruct((node_dev, cols), BF)
    big = jax.ShapeDtypeStruct((cols, width), F32)
    anywhere = pl.BlockSpec(memory_space=pl.ANY)
    return pl.pallas_call(
        functools.partial(graph_kernel, node_dev),
        out_shape=(slab, slab, big, big, big),
        in_specs=[vmem] * (5 + 2 * parts),
        out_specs=(vmem, vmem, anywhere, anywhere, anywhere),
        scratch_shapes=[
            pltpu.VMEM((nodes, width), BF),
            pltpu.VMEM((node_dev, width), F32),
            pltpu.VMEM((3, cols, width), F32),
            pltpu.SemaphoreType.DMA((2 + parts,)),
        ],
        compiler_params=pltpu.CompilerParams(vmem_limit_bytes=36 * MIB),
        cost_estimate=pl.CostEstimate(
            flops=2 * nodes * width * width * 5, bytes_accessed=8 * MIB, transcendentals=nodes * width
        ),
    )(*known, *sum((group[1:] for group in weights), ()))


def graph_wide(order, fan, node_dev, got, weights):
    mp, dp = lax.axis_index("mp"), lax.axis_index("dp")
    parts = len(got)
    cols, width = weights[0][0].shape
    nodes = got[0].shape[0] * node_dev
    owners = jnp.array(order, jnp.int32) ^ dp
    names = (owners[:, None] * node_dev + jnp.arange(node_dev)[None, :]).reshape(1, 1, nodes)
    order = jnp.arange(parts) ^ mp
    even = (dp // 2) % 2 == 0
    kinds = [
        [group[0], jnp.where(even, group[1], group[2]), jnp.where(even, group[2], group[1])]
        for group in weights[2:]
    ]
    blocks = [*weights[:2], *kinds]
    w_out, w_self, w_neigh = (
        jnp.stack([group[k] for group in blocks])[order].reshape(width, width) for k in range(3)
    )

    def part(i):
        block = jnp.stack([unpack(g, cols, i) for g in got])[order]
        return block.transpose(1, 2, 0, 3).reshape(nodes, width)

    pooled = part(0).astype(BF)
    packed = got[0][:, :fan, got[0].shape[2] - IDS_COLS :].astype(jnp.int32)
    ids = packed[:, :, :node_dev] * 16 + packed[:, :, IDS_AT : IDS_AT + node_dev] - 1
    ids = ids.transpose(0, 2, 1).reshape(nodes, fan)
    cnt = jnp.maximum(jnp.sum(ids >= 0, axis=1).astype(F32), 1.0)[:, None]
    counts = jnp.sum(ids[:, :, None] == names, axis=1).astype(BF)
    embed = (part(2) + dot(pooled, w_out)).astype(BF)
    agg = (dot(counts, embed) / cnt).astype(BF)
    mixed, slope = gelu_parts(dot(embed, w_self) + dot(agg, w_neigh))
    dz = (part(1) * slope).astype(BF)
    msg = (dot_t(dz, w_neigh) / cnt).astype(BF)
    node_grad = (dot_t(dz, w_self) + t_dot(counts, msg)).astype(BF)
    factor = 1.0 / jnp.sqrt(jnp.float32(nodes))

    def own(a):
        return lax.dynamic_slice_in_dim(a, mp * cols, cols, 1)

    grads = [t_dot(own(a), b) * factor for a, b in ((embed, dz), (agg, dz), (pooled, node_grad))]
    return (own(mixed[:node_dev]).astype(BF), own(node_grad[:node_dev]), *grads)


def join_kernel(*refs):
    out, at = refs[-1], 0
    for ref in refs[:-1]:
        out[at : at + ref.shape[0]] = ref[...]
        at += ref.shape[0]


def join(*blocks):
    count = sum(b.shape[0] for b in blocks)
    if count > 8:
        return jnp.concatenate(blocks)
    vmem = pl.BlockSpec(memory_space=pltpu.VMEM)
    return pl.pallas_call(
        join_kernel,
        out_shape=jax.ShapeDtypeStruct((count, *blocks[0].shape[1:]), BF),
        in_specs=[vmem] * len(blocks),
        out_specs=vmem,
        compiler_params=pltpu.CompilerParams(vmem_limit_bytes=8 * MIB),
    )(*blocks)


def hop(x, axis, bit):
    return lax.ppermute(x, axis, [(i, i ^ bit) for i in range(lax.axis_size(axis))])


def gather_dp(block, later):
    size = lax.axis_size("dp")
    if size == 8:
        far = [hop(block, "dp", i) for i in (2, 4, 6)]
        mine = join(block)
        mine, far, later = lax.optimization_barrier((mine, far, later))
        block = join(mine, *far)
        order, bit = [0, 2, 4, 6], 1
    else:
        order, bit = [0], size // 2
    while bit:
        block = join(block, hop(block, "dp", bit))
        order = order + [i ^ bit for i in order]
        bit //= 2
    return block, order, later


def per_device(texts, w_qkv, w_out, w_self, w_neigh, neighbours, cotangent):
    node_dev, fan = neighbours.shape
    nodes = node_dev * lax.axis_size("dp")
    own = (w_out, w_self, w_neigh)
    even = (lax.axis_index("dp") // 2) % 2 == 0
    picked, w_out = lax.optimization_barrier((jnp.where(even, w_self, w_neigh), w_out))
    x_half = hop(picked, "mp", 2)
    x_out = hop(w_out, "mp", 2)
    here = tuple(hop(a, "mp", 1) for a in own)

    sent = attention(texts, w_qkv, cotangent, neighbours.T)[None]
    sent, here, x_half = lax.optimization_barrier((sent, here, x_half))
    sent, order, x_half = gather_dp(sent, x_half)
    sent, x_out = lax.optimization_barrier((sent, x_out))
    z_half = hop(x_half, "dp", 2)
    across = (x_out, x_half, z_half)
    there = tuple(hop(a, "mp", 1) for a in across)

    got_across = hop(sent, "mp", 2)
    got = (sent, hop(sent, "mp", 1), got_across, hop(got_across, "mp", 1))
    body = graph if nodes <= WIDE_LIMIT else graph_wide
    return body(order, fan, node_dev, got, (own, here, across, there))


def solution(mesh):
    return jax.shard_map(
        per_device,
        mesh=mesh,
        in_specs=(
            P("dp", None, None),
            P(None, "mp"),
            P("mp", None),
            P("mp", None),
            P("mp", None),
            P("dp", None),
            P("dp", "mp"),
        ),
        out_specs=(P("dp", "mp"), P("dp", "mp"), P("mp", None), P("mp", None), P("mp", None)),
        check_vma=False,
    )
```

```python
import functools

import jax
import jax.numpy as jnp
from jax import lax
from jax.experimental import pallas as pl
from jax.experimental.pallas import tpu as pltpu
from jax.sharding import PartitionSpec as P

HD = 64
BF = jnp.bfloat16
F32 = jnp.float32
NODES_STEP = 8
WIDE_LIMIT = 256
IDS_COLS = 128
IDS_AT = 32
TOP = 16
LOG2E = 1.4426950408889634
ATTENTION_VMEM = 58
MIB = 1 << 20


def dot_t(a, b):
    return lax.dot_general(a, b, (((1,), (1,)), ((), ())), preferred_element_type=F32)


def t_dot(a, b):
    return lax.dot_general(a, b, (((0,), (0,)), ((), ())), preferred_element_type=F32)


def dot(a, b):
    return jnp.dot(a, b, preferred_element_type=F32)


def attend(q, k, v):
    seq, cols = q.shape
    pair = 2 * HD
    left = lax.broadcasted_iota(jnp.int32, (seq, pair), 1) < HD
    zero = jnp.zeros((seq, pair), BF)
    out = []
    for at in range(0, cols, pair):
        both = q[:, at : at + pair]
        spread = jnp.concatenate([jnp.where(left, both, zero), jnp.where(left, zero, both)], axis=0)
        s = dot_t(k[:, at : at + pair], spread)
        e = jnp.exp2((s - jnp.max(s, axis=0, keepdims=True)) * (HD**-0.5 * LOG2E))
        p = (e * (1.0 / jnp.sum(e, axis=0, keepdims=True))).astype(BF).astype(F32)
        first = jnp.sum(p[:, :seq], axis=1, keepdims=True)
        second = jnp.sum(p[:, seq:], axis=1, keepdims=True)
        context = jnp.where(left, first, second) * v[:, at : at + pair].astype(F32)
        out.append(jnp.sum(context, axis=0, keepdims=True) * (1.0 / seq))
    return jnp.concatenate(out, axis=1)


def attention_kernel(
    heads, texts_ref, w_hbm, cot_ref, ids_ref, out_ref, wp, acc_p, acc_m, held, w_ref, sem
):
    step = pl.program_id(0)
    nodes, seq, width = held.shape[1:]
    node_dev = cot_ref.shape[0]
    cols = heads * HD

    def fetch(i):
        source = texts_ref.at[pl.ds(i * nodes, nodes)]
        return pltpu.make_async_copy(source, held.at[i % 2], sem.at[i % 2])

    @pl.when(step == 0)
    def _():
        weights = pltpu.make_async_copy(w_hbm, w_ref, sem.at[2])
        weights.start()
        fetch(0).start()
        weights.wait()
        for part in range(3):
            for h in range(0, heads, 2):
                a = h * 3 * HD + part * HD
                b = a + 3 * HD
                wp[:, part * cols + h * HD : part * cols + (h + 2) * HD] = jnp.concatenate(
                    [w_ref[:, a : a + HD], w_ref[:, b : b + HD]], axis=1
                )

    @pl.when(step + 1 < pl.num_programs(0))
    def _():
        fetch(step + 1).start()

    fetch(step).wait()
    x_ref = held.at[step % 2]
    own = pl.ds(pl.multiple_of(lax.axis_index("mp") * cols, 128), cols)
    qkv = dot(x_ref[...].reshape(nodes * seq, width), wp[...]).astype(BF)
    for n in range(nodes):
        at = slice(n * seq, (n + 1) * seq)
        row = pl.ds(step * nodes + n, 1)
        acc_p[row, :] = attend(*(qkv[at, i * cols : (i + 1) * cols] for i in range(3)))
        mean = jnp.sum(x_ref[n, :, own].astype(F32), axis=0, keepdims=True)
        acc_m[row, :] = mean * (1.0 / seq)

    @pl.when(step == pl.num_programs(0) - 1)
    def _():
        rows = jnp.concatenate([acc_p[...], cot_ref[...].astype(F32), acc_m[...]], axis=1)
        shifted = ids_ref[...] + 1
        fan = shifted.shape[0]
        gap = jnp.zeros((fan, IDS_AT - node_dev), F32)
        high, low = (shifted >> 4).astype(F32), (shifted & 15).astype(F32)
        blank = jnp.zeros((fan, IDS_COLS - 2 * IDS_AT), F32)
        ids = jnp.concatenate([high, gap, low, gap, blank], axis=1)
        wide = 3 * cols
        rest = jnp.concatenate([rows[TOP:, : wide // 2], rows[TOP:, wide // 2 :]], axis=0)
        out_ref[:, :wide] = rows[:TOP].astype(BF)
        out_ref[:, wide : wide + wide // 2] = rest.astype(BF)
        out_ref[:, wide + wide // 2 :] = ids.astype(BF)


def unpack(got, cols, part):
    got = got.astype(F32)
    wide, at = 3 * cols, part * cols
    pieces, left = [], at
    while left < at + cols:
        side, inside = divmod(left, wide // 2)
        right = min(at + cols, (side + 1) * (wide // 2))
        low = wide + inside
        pieces.append(got[:, side * (TOP // 2) : (side + 1) * (TOP // 2), low : low + right - left])
        left = right
    rest = jnp.concatenate(pieces, axis=2) if len(pieces) > 1 else pieces[0]
    return jnp.concatenate([got[:, :, at : at + cols], rest], axis=1)


def attention(texts, w_qkv, cotangent, ids):
    node_dev, seq, width = texts.shape
    cols = w_qkv.shape[1] // 3
    heads = cols // HD
    tokens = node_dev * seq
    nodes = NODES_STEP
    packed = (TOP, 3 * cols + 3 * cols // 2 + IDS_COLS)
    return pl.pallas_call(
        functools.partial(attention_kernel, heads),
        out_shape=jax.ShapeDtypeStruct(packed, BF),
        grid=(node_dev // nodes,),
        in_specs=[
            pl.BlockSpec(memory_space=pl.ANY),
            pl.BlockSpec(memory_space=pl.ANY),
            pl.BlockSpec((node_dev, cols), lambda i: (0, 0)),
            pl.BlockSpec(ids.shape, lambda i: (0, 0)),
        ],
        out_specs=pl.BlockSpec(packed, lambda i: (0, 0)),
        scratch_shapes=[
            pltpu.VMEM((width, 3 * cols), BF),
            pltpu.VMEM((node_dev, cols), F32),
            pltpu.VMEM((node_dev, cols), F32),
            pltpu.VMEM((2, nodes, seq, width), BF),
            pltpu.VMEM((width, 3 * cols), BF),
            pltpu.SemaphoreType.DMA((3,)),
        ],
        compiler_params=pltpu.CompilerParams(vmem_limit_bytes=ATTENTION_VMEM * MIB),
        cost_estimate=pl.CostEstimate(
            flops=2 * tokens * width * 3 * cols + 8 * tokens * seq * cols,
            bytes_accessed=2 * tokens * width + 6 * width * cols,
            transcendentals=tokens * seq * heads,
        ),
    )(texts, w_qkv, cotangent, ids)


def gelu_parts(z):
    root = 0.7978845608028654
    cube = 0.044715
    t = jnp.tanh(root * (z + cube * (z * z * z)))
    half = 0.5 * (1.0 + t)
    slope = half + 0.5 * z * (1.0 - t * t) * (root * (1.0 + 3.0 * cube * (z * z)))
    return z * half, slope


def block_place(r, cols):
    return pl.ds(pl.multiple_of((lax.axis_index("mp") ^ r) * cols, 128), cols)


def embed_kernel(order, fan, node_dev, *refs):
    parts = 4
    got, blocks, refs = refs[:parts], refs[parts : 2 * parts], refs[2 * parts :]
    both, cot, pooled_ref, counts_ref, share_ref, mean = refs
    dp = lax.axis_index("dp")
    groups = got[0].shape[0]
    nodes = groups * node_dev
    cols = blocks[0].shape[0]

    def part(r, i):
        return unpack(got[r][...], cols, i).reshape(nodes, cols)

    packed = got[0][:, :, got[0].shape[2] - IDS_COLS :].astype(F32)
    ids = jnp.concatenate(
        [
            packed[i, :fan, :node_dev] * 16.0 + packed[i, :fan, IDS_AT : IDS_AT + node_dev] - 1.0
            for i in range(groups)
        ],
        axis=1,
    )
    place_of = lax.broadcasted_iota(jnp.int32, (nodes, 1), 0)
    names = place_of
    for i, o in enumerate(order):
        shift = ((dp ^ o) - i) * node_dev
        inside = (place_of >= i * node_dev) & (place_of < (i + 1) * node_dev)
        names = jnp.where(inside, place_of + shift, names)
    names = names.astype(F32)
    counts_t = jnp.zeros((nodes, nodes), F32)
    for s in range(fan):
        counts_t += (ids[s : s + 1, :] == names).astype(F32)
    counts = counts_t.T
    share = 1.0 / jnp.maximum(jnp.sum(counts, axis=1, keepdims=True), 1.0)
    counts_ref[...] = counts_t.astype(BF)
    share_ref[...] = jnp.broadcast_to(share, share_ref.shape)

    pooled = [part(r, 0).astype(BF) for r in range(parts)]
    pooled_ref[...] = pooled[0]
    for r in range(parts):
        cot[:, block_place(r, cols)] = part(r, 1).astype(BF)
        mean[:, block_place(r, cols)] = part(r, 2)
    sums = sum(dot(pooled[r], blocks[r][...]) for r in range(parts))
    both[0] = (mean[...] + sums).astype(BF)
    both[1] = (dot(counts.astype(BF), both[0]) * share).astype(BF)


def graph_kernel(node_dev, both, cot, pooled, counts, share_ref, *refs):
    parts = 4
    blocks, refs = refs[: 2 * parts], refs[2 * parts :]
    mixed_ref, grad_ref, g_self, g_neigh, g_out, dz, wide, grads, sem = refs
    side = (lax.axis_index("dp") // 2) % 2
    cols, width = g_self.shape
    nodes = counts.shape[0]
    factor = 1.0 / jnp.sqrt(jnp.float32(nodes))
    own = block_place(0, cols)

    z = 0.0
    for r in range(parts):
        first = 0 if r < 2 else side
        z += dot(both[first, :, block_place(r, cols)], blocks[2 * r][...])
        z += dot(both[1 - first, :, block_place(r, cols)], blocks[2 * r + 1][...])
    mixed, slope = gelu_parts(z)
    dz[...] = (cot[...].astype(F32) * slope).astype(BF)
    wide[...] = mixed[:node_dev, :]
    mixed_ref[...] = wide[:, own].astype(BF)

    copies = []
    for i, out in enumerate((g_self, g_neigh)):
        grads[i] = t_dot(both[i, :, own], dz[...]) * factor
        copies.append(pltpu.make_async_copy(grads.at[i], out, sem.at[i]))
        copies[-1].start()
    share = share_ref[:, :1]
    for r in range(parts):
        to_self, to_agg = dot_t(dz[...], blocks[2 * r][...]), dot_t(dz[...], blocks[2 * r + 1][...])
        if r >= 2:
            even = side == 0
            to_self, to_agg = jnp.where(even, to_self, to_agg), jnp.where(even, to_agg, to_self)
        total = to_self + dot(counts[...], (to_agg * share).astype(BF))
        if r == 0:
            grad_ref[...] = total[:node_dev, :].astype(BF)
        at = slice(r * cols, (r + 1) * cols)
        grads[2, :, at] = t_dot(pooled[...], total.astype(BF)) * factor
        copies.append(
            pltpu.make_async_copy(grads.at[2, :, at], g_out.at[:, block_place(r, cols)], sem.at[2 + r])
        )
        copies[-1].start()
    for copy in copies:
        copy.wait()


def graph(order, fan, node_dev, got, weights):
    parts = len(got)
    cols, width = weights[0][0].shape
    nodes = got[0].shape[0] * node_dev
    vmem = pl.BlockSpec(memory_space=pltpu.VMEM)
    known = pl.pallas_call(
        functools.partial(embed_kernel, order, fan, node_dev),
        out_shape=(
            jax.ShapeDtypeStruct((2, nodes, width), BF),
            jax.ShapeDtypeStruct((nodes, width), BF),
            jax.ShapeDtypeStruct((nodes, cols), BF),
            jax.ShapeDtypeStruct((nodes, nodes), BF),
            jax.ShapeDtypeStruct((nodes, 128), F32),
        ),
        in_specs=[vmem] * (2 * parts),
        out_specs=(vmem,) * 5,
        scratch_shapes=[pltpu.VMEM((nodes, width), F32)],
        compiler_params=pltpu.CompilerParams(vmem_limit_bytes=24 * MIB),
        cost_estimate=pl.CostEstimate(
            flops=2 * nodes * width * width * 2, bytes_accessed=4 * MIB, transcendentals=0
        ),
    )(*got, *[group[0] for group in weights])
    slab = jax.ShapeDtypeStruct((node_dev, cols), BF)
    big = jax.ShapeDtypeStruct((cols, width), F32)
    anywhere = pl.BlockSpec(memory_space=pl.ANY)
    return pl.pallas_call(
        functools.partial(graph_kernel, node_dev),
        out_shape=(slab, slab, big, big, big),
        in_specs=[vmem] * (5 + 2 * parts),
        out_specs=(vmem, vmem, anywhere, anywhere, anywhere),
        scratch_shapes=[
            pltpu.VMEM((nodes, width), BF),
            pltpu.VMEM((node_dev, width), F32),
            pltpu.VMEM((3, cols, width), F32),
            pltpu.SemaphoreType.DMA((2 + parts,)),
        ],
        compiler_params=pltpu.CompilerParams(vmem_limit_bytes=36 * MIB),
        cost_estimate=pl.CostEstimate(
            flops=2 * nodes * width * width * 5, bytes_accessed=8 * MIB, transcendentals=nodes * width
        ),
    )(*known, *sum((group[1:] for group in weights), ()))


def graph_wide(order, fan, node_dev, got, weights):
    mp, dp = lax.axis_index("mp"), lax.axis_index("dp")
    parts = len(got)
    cols, width = weights[0][0].shape
    nodes = got[0].shape[0] * node_dev
    owners = jnp.array(order, jnp.int32) ^ dp
    names = (owners[:, None] * node_dev + jnp.arange(node_dev)[None, :]).reshape(1, 1, nodes)
    order = jnp.arange(parts) ^ mp
    even = (dp // 2) % 2 == 0
    kinds = [
        [group[0], jnp.where(even, group[1], group[2]), jnp.where(even, group[2], group[1])]
        for group in weights[2:]
    ]
    blocks = [*weights[:2], *kinds]
    w_out, w_self, w_neigh = (
        jnp.stack([group[k] for group in blocks])[order].reshape(width, width) for k in range(3)
    )

    def part(i):
        block = jnp.stack([unpack(g, cols, i) for g in got])[order]
        return block.transpose(1, 2, 0, 3).reshape(nodes, width)

    pooled = part(0).astype(BF)
    packed = got[0][:, :fan, got[0].shape[2] - IDS_COLS :].astype(jnp.int32)
    ids = packed[:, :, :node_dev] * 16 + packed[:, :, IDS_AT : IDS_AT + node_dev] - 1
    ids = ids.transpose(0, 2, 1).reshape(nodes, fan)
    cnt = jnp.maximum(jnp.sum(ids >= 0, axis=1).astype(F32), 1.0)[:, None]
    counts = jnp.sum(ids[:, :, None] == names, axis=1).astype(BF)
    embed = (part(2) + dot(pooled, w_out)).astype(BF)
    agg = (dot(counts, embed) / cnt).astype(BF)
    mixed, slope = gelu_parts(dot(embed, w_self) + dot(agg, w_neigh))
    dz = (part(1) * slope).astype(BF)
    msg = (dot_t(dz, w_neigh) / cnt).astype(BF)
    node_grad = (dot_t(dz, w_self) + t_dot(counts, msg)).astype(BF)
    factor = 1.0 / jnp.sqrt(jnp.float32(nodes))

    def own(a):
        return lax.dynamic_slice_in_dim(a, mp * cols, cols, 1)

    grads = [t_dot(own(a), b) * factor for a, b in ((embed, dz), (agg, dz), (pooled, node_grad))]
    return (own(mixed[:node_dev]).astype(BF), own(node_grad[:node_dev]), *grads)


def join_kernel(*refs):
    out, at = refs[-1], 0
    for ref in refs[:-1]:
        out[at : at + ref.shape[0]] = ref[...]
        at += ref.shape[0]


def join(*blocks):
    count = sum(b.shape[0] for b in blocks)
    if count > 8:
        return jnp.concatenate(blocks)
    vmem = pl.BlockSpec(memory_space=pltpu.VMEM)
    return pl.pallas_call(
        join_kernel,
        out_shape=jax.ShapeDtypeStruct((count, *blocks[0].shape[1:]), BF),
        in_specs=[vmem] * len(blocks),
        out_specs=vmem,
        compiler_params=pltpu.CompilerParams(vmem_limit_bytes=8 * MIB),
    )(*blocks)


def hop(x, axis, bit):
    return lax.ppermute(x, axis, [(i, i ^ bit) for i in range(lax.axis_size(axis))])


def gather_dp(block, later):
    size = lax.axis_size("dp")
    if size == 8:
        far = [hop(block, "dp", i) for i in (2, 4, 6)]
        mine = join(block)
        mine, far, later = lax.optimization_barrier((mine, far, later))
        block = join(mine, *far)
        order, bit = [0, 2, 4, 6], 1
    else:
        order, bit = [0], size // 2
    while bit:
        block = join(block, hop(block, "dp", bit))
        order = order + [i ^ bit for i in order]
        bit //= 2
    return block, order, later


def per_device(texts, w_qkv, w_out, w_self, w_neigh, neighbours, cotangent):
    node_dev, fan = neighbours.shape
    nodes = node_dev * lax.axis_size("dp")
    own = (w_out, w_self, w_neigh)
    even = (lax.axis_index("dp") // 2) % 2 == 0
    picked, w_out = lax.optimization_barrier((jnp.where(even, w_self, w_neigh), w_out))
    x_half = hop(picked, "mp", 2)
    x_out = hop(w_out, "mp", 2)
    here = tuple(hop(a, "mp", 1) for a in own)

    sent = attention(texts, w_qkv, cotangent, neighbours.T)[None]
    sent, here, x_half = lax.optimization_barrier((sent, here, x_half))
    sent, order, x_half = gather_dp(sent, x_half)
    sent, x_out = lax.optimization_barrier((sent, x_out))
    z_half = hop(x_half, "dp", 2)
    across = (x_out, x_half, z_half)
    there = tuple(hop(a, "mp", 1) for a in across)

    got_across = hop(sent, "mp", 2)
    got = (sent, hop(sent, "mp", 1), got_across, hop(got_across, "mp", 1))
    body = graph if nodes <= WIDE_LIMIT else graph_wide
    return body(order, fan, node_dev, got, (own, here, across, there))


def solution(mesh):
    return jax.shard_map(
        per_device,
        mesh=mesh,
        in_specs=(
            P("dp", None, None),
            P(None, "mp"),
            P("mp", None),
            P("mp", None),
            P("mp", None),
            P("dp", None),
            P("dp", "mp"),
        ),
        out_specs=(P("dp", "mp"), P("dp", "mp"), P("mp", None), P("mp", None), P("mp", None)),
        check_vma=False,
    )
```

```python
import functools

import jax
import jax.numpy as jnp
from jax import lax
from jax.experimental import pallas as pl
from jax.experimental.pallas import tpu as pltpu
from jax.sharding import PartitionSpec as P

HD = 64
BF = jnp.bfloat16
F32 = jnp.float32
NODES_STEP = 8
WIDE_LIMIT = 256
IDS_COLS = 128
IDS_AT = 32
TOP = 16
LOG2E = 1.4426950408889634
ATTENTION_VMEM = 58
COPIES = 4
MIB = 1 << 20


def dot_t(a, b):
    return lax.dot_general(a, b, (((1,), (1,)), ((), ())), preferred_element_type=F32)


def t_dot(a, b):
    return lax.dot_general(a, b, (((0,), (0,)), ((), ())), preferred_element_type=F32)


def dot(a, b):
    return jnp.dot(a, b, preferred_element_type=F32)


def attend(q, k, v):
    seq, cols = q.shape
    pair = 2 * HD
    left = lax.broadcasted_iota(jnp.int32, (seq, pair), 1) < HD
    zero = jnp.zeros((seq, pair), BF)
    out = []
    for at in range(0, cols, pair):
        both = q[:, at : at + pair]
        spread = jnp.concatenate([jnp.where(left, both, zero), jnp.where(left, zero, both)], axis=0)
        s = dot_t(k[:, at : at + pair], spread)
        e = jnp.exp2((s - jnp.max(s, axis=0, keepdims=True)) * (HD**-0.5 * LOG2E))
        p = (e * (1.0 / jnp.sum(e, axis=0, keepdims=True))).astype(BF).astype(F32)
        first = jnp.sum(p[:, :seq], axis=1, keepdims=True)
        second = jnp.sum(p[:, seq:], axis=1, keepdims=True)
        context = jnp.where(left, first, second) * v[:, at : at + pair].astype(F32)
        out.append(jnp.sum(context, axis=0, keepdims=True) * (1.0 / seq))
    return jnp.concatenate(out, axis=1)


def attention_kernel(
    heads, texts_ref, w_hbm, cot_ref, ids_ref, out_ref, wp, acc_p, acc_m, held, w_ref, sem
):
    step = pl.program_id(0)
    nodes, seq, width = held.shape[1:]
    node_dev = cot_ref.shape[0]
    cols = heads * HD

    some, deep = nodes // COPIES, width // COPIES

    def fetch(i):
        return [
            pltpu.make_async_copy(
                texts_ref.at[pl.ds(i * nodes + c * some, some)],
                held.at[i % 2, pl.ds(c * some, some)],
                sem.at[i % 2, c],
            )
            for c in range(COPIES)
        ]

    @pl.when(step == 0)
    def _():
        weights = [
            pltpu.make_async_copy(
                w_hbm.at[pl.ds(c * deep, deep)], w_ref.at[pl.ds(c * deep, deep)], sem.at[2, c]
            )
            for c in range(COPIES)
        ]
        for copy in weights + fetch(0):
            copy.start()
        for copy in weights:
            copy.wait()
        for part in range(3):
            for h in range(0, heads, 2):
                a = h * 3 * HD + part * HD
                b = a + 3 * HD
                wp[:, part * cols + h * HD : part * cols + (h + 2) * HD] = jnp.concatenate(
                    [w_ref[:, a : a + HD], w_ref[:, b : b + HD]], axis=1
                )

    @pl.when(step + 1 < pl.num_programs(0))
    def _():
        for copy in fetch(step + 1):
            copy.start()

    for copy in fetch(step):
        copy.wait()
    x_ref = held.at[step % 2]
    own = pl.ds(pl.multiple_of(lax.axis_index("mp") * cols, 128), cols)
    qkv = dot(x_ref[...].reshape(nodes * seq, width), wp[...]).astype(BF)
    for n in range(nodes):
        at = slice(n * seq, (n + 1) * seq)
        row = pl.ds(step * nodes + n, 1)
        acc_p[row, :] = attend(*(qkv[at, i * cols : (i + 1) * cols] for i in range(3)))
        mean = jnp.sum(x_ref[n, :, own].astype(F32), axis=0, keepdims=True)
        acc_m[row, :] = mean * (1.0 / seq)

    @pl.when(step == pl.num_programs(0) - 1)
    def _():
        rows = jnp.concatenate([acc_p[...], cot_ref[...].astype(F32), acc_m[...]], axis=1)
        shifted = ids_ref[...] + 1
        fan = shifted.shape[0]
        gap = jnp.zeros((fan, IDS_AT - node_dev), F32)
        high, low = (shifted >> 4).astype(F32), (shifted & 15).astype(F32)
        blank = jnp.zeros((fan, IDS_COLS - 2 * IDS_AT), F32)
        ids = jnp.concatenate([high, gap, low, gap, blank], axis=1)
        wide = 3 * cols
        rest = jnp.concatenate([rows[TOP:, : wide // 2], rows[TOP:, wide // 2 :]], axis=0)
        out_ref[:, :wide] = rows[:TOP].astype(BF)
        out_ref[:, wide : wide + wide // 2] = rest.astype(BF)
        out_ref[:, wide + wide // 2 :] = ids.astype(BF)


def unpack(got, cols, part):
    got = got.astype(F32)
    wide, at = 3 * cols, part * cols
    pieces, left = [], at
    while left < at + cols:
        side, inside = divmod(left, wide // 2)
        right = min(at + cols, (side + 1) * (wide // 2))
        low = wide + inside
        pieces.append(got[:, side * (TOP // 2) : (side + 1) * (TOP // 2), low : low + right - left])
        left = right
    rest = jnp.concatenate(pieces, axis=2) if len(pieces) > 1 else pieces[0]
    return jnp.concatenate([got[:, :, at : at + cols], rest], axis=1)


def attention(texts, w_qkv, cotangent, ids):
    node_dev, seq, width = texts.shape
    cols = w_qkv.shape[1] // 3
    heads = cols // HD
    tokens = node_dev * seq
    nodes = NODES_STEP
    packed = (TOP, 3 * cols + 3 * cols // 2 + IDS_COLS)
    return pl.pallas_call(
        functools.partial(attention_kernel, heads),
        out_shape=jax.ShapeDtypeStruct(packed, BF),
        grid=(node_dev // nodes,),
        in_specs=[
            pl.BlockSpec(memory_space=pl.ANY),
            pl.BlockSpec(memory_space=pl.ANY),
            pl.BlockSpec((node_dev, cols), lambda i: (0, 0)),
            pl.BlockSpec(ids.shape, lambda i: (0, 0)),
        ],
        out_specs=pl.BlockSpec(packed, lambda i: (0, 0)),
        scratch_shapes=[
            pltpu.VMEM((width, 3 * cols), BF),
            pltpu.VMEM((node_dev, cols), F32),
            pltpu.VMEM((node_dev, cols), F32),
            pltpu.VMEM((2, nodes, seq, width), BF),
            pltpu.VMEM((width, 3 * cols), BF),
            pltpu.SemaphoreType.DMA((3, COPIES)),
        ],
        compiler_params=pltpu.CompilerParams(vmem_limit_bytes=ATTENTION_VMEM * MIB),
        cost_estimate=pl.CostEstimate(
            flops=2 * tokens * width * 3 * cols + 8 * tokens * seq * cols,
            bytes_accessed=2 * tokens * width + 6 * width * cols,
            transcendentals=tokens * seq * heads,
        ),
    )(texts, w_qkv, cotangent, ids)


def gelu_parts(z):
    root = 0.7978845608028654
    cube = 0.044715
    t = jnp.tanh(root * (z + cube * (z * z * z)))
    half = 0.5 * (1.0 + t)
    slope = half + 0.5 * z * (1.0 - t * t) * (root * (1.0 + 3.0 * cube * (z * z)))
    return z * half, slope


def block_place(r, cols):
    return pl.ds(pl.multiple_of((lax.axis_index("mp") ^ r) * cols, 128), cols)


def embed_kernel(order, fan, node_dev, *refs):
    parts = 4
    got, blocks, refs = refs[:parts], refs[parts : 2 * parts], refs[2 * parts :]
    both, cot, pooled_ref, counts_ref, share_ref, mean = refs
    dp = lax.axis_index("dp")
    groups = got[0].shape[0]
    nodes = groups * node_dev
    cols = blocks[0].shape[0]

    def part(r, i):
        return unpack(got[r][...], cols, i).reshape(nodes, cols)

    packed = got[0][:, :, got[0].shape[2] - IDS_COLS :].astype(F32)
    ids = jnp.concatenate(
        [
            packed[i, :fan, :node_dev] * 16.0 + packed[i, :fan, IDS_AT : IDS_AT + node_dev] - 1.0
            for i in range(groups)
        ],
        axis=1,
    )
    place_of = lax.broadcasted_iota(jnp.int32, (nodes, 1), 0)
    names = place_of
    for i, o in enumerate(order):
        shift = ((dp ^ o) - i) * node_dev
        inside = (place_of >= i * node_dev) & (place_of < (i + 1) * node_dev)
        names = jnp.where(inside, place_of + shift, names)
    names = names.astype(F32)
    counts_t = jnp.zeros((nodes, nodes), F32)
    for s in range(fan):
        counts_t += (ids[s : s + 1, :] == names).astype(F32)
    counts = counts_t.T
    share = 1.0 / jnp.maximum(jnp.sum(counts, axis=1, keepdims=True), 1.0)
    counts_ref[...] = counts_t.astype(BF)
    share_ref[...] = jnp.broadcast_to(share, share_ref.shape)

    pooled = [part(r, 0).astype(BF) for r in range(parts)]
    pooled_ref[...] = pooled[0]
    for r in range(parts):
        cot[:, block_place(r, cols)] = part(r, 1).astype(BF)
        mean[:, block_place(r, cols)] = part(r, 2)
    sums = sum(dot(pooled[r], blocks[r][...]) for r in range(parts))
    both[0] = (mean[...] + sums).astype(BF)
    both[1] = (dot(counts.astype(BF), both[0]) * share).astype(BF)


def graph_kernel(node_dev, both, cot, pooled, counts, share_ref, *refs):
    parts = 4
    blocks, refs = refs[: 2 * parts], refs[2 * parts :]
    mixed_ref, grad_ref, g_self, g_neigh, g_out, dz, wide, grads, sem = refs
    side = (lax.axis_index("dp") // 2) % 2
    cols, width = g_self.shape
    nodes = counts.shape[0]
    factor = 1.0 / jnp.sqrt(jnp.float32(nodes))
    own = block_place(0, cols)

    z = 0.0
    for r in range(parts):
        first = 0 if r < 2 else side
        z += dot(both[first, :, block_place(r, cols)], blocks[2 * r][...])
        z += dot(both[1 - first, :, block_place(r, cols)], blocks[2 * r + 1][...])
    mixed, slope = gelu_parts(z)
    dz[...] = (cot[...].astype(F32) * slope).astype(BF)
    wide[...] = mixed[:node_dev, :]
    mixed_ref[...] = wide[:, own].astype(BF)

    copies = []
    for i, out in enumerate((g_self, g_neigh)):
        grads[i] = t_dot(both[i, :, own], dz[...]) * factor
        copies.append(pltpu.make_async_copy(grads.at[i], out, sem.at[i]))
        copies[-1].start()
    share = share_ref[:, :1]
    for r in range(parts):
        to_self, to_agg = dot_t(dz[...], blocks[2 * r][...]), dot_t(dz[...], blocks[2 * r + 1][...])
        if r >= 2:
            even = side == 0
            to_self, to_agg = jnp.where(even, to_self, to_agg), jnp.where(even, to_agg, to_self)
        total = to_self + dot(counts[...], (to_agg * share).astype(BF))
        if r == 0:
            grad_ref[...] = total[:node_dev, :].astype(BF)
        at = slice(r * cols, (r + 1) * cols)
        grads[2, :, at] = t_dot(pooled[...], total.astype(BF)) * factor
        copies.append(
            pltpu.make_async_copy(grads.at[2, :, at], g_out.at[:, block_place(r, cols)], sem.at[2 + r])
        )
        copies[-1].start()
    for copy in copies:
        copy.wait()


def graph(order, fan, node_dev, got, weights):
    parts = len(got)
    cols, width = weights[0][0].shape
    nodes = got[0].shape[0] * node_dev
    vmem = pl.BlockSpec(memory_space=pltpu.VMEM)
    known = pl.pallas_call(
        functools.partial(embed_kernel, order, fan, node_dev),
        out_shape=(
            jax.ShapeDtypeStruct((2, nodes, width), BF),
            jax.ShapeDtypeStruct((nodes, width), BF),
            jax.ShapeDtypeStruct((nodes, cols), BF),
            jax.ShapeDtypeStruct((nodes, nodes), BF),
            jax.ShapeDtypeStruct((nodes, 128), F32),
        ),
        in_specs=[vmem] * (2 * parts),
        out_specs=(vmem,) * 5,
        scratch_shapes=[pltpu.VMEM((nodes, width), F32)],
        compiler_params=pltpu.CompilerParams(vmem_limit_bytes=24 * MIB),
        cost_estimate=pl.CostEstimate(
            flops=2 * nodes * width * width * 2, bytes_accessed=4 * MIB, transcendentals=0
        ),
    )(*got, *[group[0] for group in weights])
    slab = jax.ShapeDtypeStruct((node_dev, cols), BF)
    big = jax.ShapeDtypeStruct((cols, width), F32)
    anywhere = pl.BlockSpec(memory_space=pl.ANY)
    return pl.pallas_call(
        functools.partial(graph_kernel, node_dev),
        out_shape=(slab, slab, big, big, big),
        in_specs=[vmem] * (5 + 2 * parts),
        out_specs=(vmem, vmem, anywhere, anywhere, anywhere),
        scratch_shapes=[
            pltpu.VMEM((nodes, width), BF),
            pltpu.VMEM((node_dev, width), F32),
            pltpu.VMEM((3, cols, width), F32),
            pltpu.SemaphoreType.DMA((2 + parts,)),
        ],
        compiler_params=pltpu.CompilerParams(vmem_limit_bytes=36 * MIB),
        cost_estimate=pl.CostEstimate(
            flops=2 * nodes * width * width * 5, bytes_accessed=8 * MIB, transcendentals=nodes * width
        ),
    )(*known, *sum((group[1:] for group in weights), ()))


def graph_wide(order, fan, node_dev, got, weights):
    mp, dp = lax.axis_index("mp"), lax.axis_index("dp")
    parts = len(got)
    cols, width = weights[0][0].shape
    nodes = got[0].shape[0] * node_dev
    owners = jnp.array(order, jnp.int32) ^ dp
    names = (owners[:, None] * node_dev + jnp.arange(node_dev)[None, :]).reshape(1, 1, nodes)
    order = jnp.arange(parts) ^ mp
    even = (dp // 2) % 2 == 0
    kinds = [
        [group[0], jnp.where(even, group[1], group[2]), jnp.where(even, group[2], group[1])]
        for group in weights[2:]
    ]
    blocks = [*weights[:2], *kinds]
    w_out, w_self, w_neigh = (
        jnp.stack([group[k] for group in blocks])[order].reshape(width, width) for k in range(3)
    )

    def part(i):
        block = jnp.stack([unpack(g, cols, i) for g in got])[order]
        return block.transpose(1, 2, 0, 3).reshape(nodes, width)

    pooled = part(0).astype(BF)
    packed = got[0][:, :fan, got[0].shape[2] - IDS_COLS :].astype(jnp.int32)
    ids = packed[:, :, :node_dev] * 16 + packed[:, :, IDS_AT : IDS_AT + node_dev] - 1
    ids = ids.transpose(0, 2, 1).reshape(nodes, fan)
    cnt = jnp.maximum(jnp.sum(ids >= 0, axis=1).astype(F32), 1.0)[:, None]
    counts = jnp.sum(ids[:, :, None] == names, axis=1).astype(BF)
    embed = (part(2) + dot(pooled, w_out)).astype(BF)
    agg = (dot(counts, embed) / cnt).astype(BF)
    mixed, slope = gelu_parts(dot(embed, w_self) + dot(agg, w_neigh))
    dz = (part(1) * slope).astype(BF)
    msg = (dot_t(dz, w_neigh) / cnt).astype(BF)
    node_grad = (dot_t(dz, w_self) + t_dot(counts, msg)).astype(BF)
    factor = 1.0 / jnp.sqrt(jnp.float32(nodes))

    def own(a):
        return lax.dynamic_slice_in_dim(a, mp * cols, cols, 1)

    grads = [t_dot(own(a), b) * factor for a, b in ((embed, dz), (agg, dz), (pooled, node_grad))]
    return (own(mixed[:node_dev]).astype(BF), own(node_grad[:node_dev]), *grads)


def join_kernel(*refs):
    out, at = refs[-1], 0
    for ref in refs[:-1]:
        out[at : at + ref.shape[0]] = ref[...]
        at += ref.shape[0]


def join(*blocks):
    count = sum(b.shape[0] for b in blocks)
    if count > 8:
        return jnp.concatenate(blocks)
    vmem = pl.BlockSpec(memory_space=pltpu.VMEM)
    return pl.pallas_call(
        join_kernel,
        out_shape=jax.ShapeDtypeStruct((count, *blocks[0].shape[1:]), BF),
        in_specs=[vmem] * len(blocks),
        out_specs=vmem,
        compiler_params=pltpu.CompilerParams(vmem_limit_bytes=8 * MIB),
    )(*blocks)


def hop(x, axis, bit):
    return lax.ppermute(x, axis, [(i, i ^ bit) for i in range(lax.axis_size(axis))])


def gather_dp(block, later):
    size = lax.axis_size("dp")
    if size == 8:
        far = [hop(block, "dp", i) for i in (2, 4, 6)]
        mine = join(block)
        mine, far, later = lax.optimization_barrier((mine, far, later))
        block = join(mine, *far)
        order, bit = [0, 2, 4, 6], 1
    else:
        order, bit = [0], size // 2
    while bit:
        block = join(block, hop(block, "dp", bit))
        order = order + [i ^ bit for i in order]
        bit //= 2
    return block, order, later


def per_device(texts, w_qkv, w_out, w_self, w_neigh, neighbours, cotangent):
    node_dev, fan = neighbours.shape
    nodes = node_dev * lax.axis_size("dp")
    own = (w_out, w_self, w_neigh)
    even = (lax.axis_index("dp") // 2) % 2 == 0
    picked, w_out = lax.optimization_barrier((jnp.where(even, w_self, w_neigh), w_out))
    x_half = hop(picked, "mp", 2)
    x_out = hop(w_out, "mp", 2)
    here = tuple(hop(a, "mp", 1) for a in own)

    sent = attention(texts, w_qkv, cotangent, neighbours.T)[None]
    sent, here = lax.optimization_barrier((sent, here))
    sent, order, x_half = gather_dp(sent, x_half)
    sent, x_out = lax.optimization_barrier((sent, x_out))
    z_half = hop(x_half, "dp", 2)
    across = (x_out, x_half, z_half)
    there = tuple(hop(a, "mp", 1) for a in across)

    got_across = hop(sent, "mp", 2)
    got = (sent, hop(sent, "mp", 1), got_across, hop(got_across, "mp", 1))
    body = graph if nodes <= WIDE_LIMIT else graph_wide
    return body(order, fan, node_dev, got, (own, here, across, there))


def solution(mesh):
    return jax.shard_map(
        per_device,
        mesh=mesh,
        in_specs=(
            P("dp", None, None),
            P(None, "mp"),
            P("mp", None),
            P("mp", None),
            P("mp", None),
            P("dp", None),
            P("dp", "mp"),
        ),
        out_specs=(P("dp", "mp"), P("dp", "mp"), P("mp", None), P("mp", None), P("mp", None)),
        check_vma=False,
    )
```

```python
import functools

import jax
import jax.numpy as jnp
from jax import lax
from jax.experimental import pallas as pl
from jax.experimental.pallas import tpu as pltpu
from jax.sharding import PartitionSpec as P

HD = 64
BF = jnp.bfloat16
F32 = jnp.float32
NODES_STEP = 8
WIDE_LIMIT = 256
IDS_COLS = 128
IDS_AT = 32
TOP = 16
LOG2E = 1.4426950408889634
ATTENTION_VMEM = 58
COPIES = 4
MIB = 1 << 20


def dot_t(a, b):
    return lax.dot_general(a, b, (((1,), (1,)), ((), ())), preferred_element_type=F32)


def t_dot(a, b):
    return lax.dot_general(a, b, (((0,), (0,)), ((), ())), preferred_element_type=F32)


def dot(a, b):
    return jnp.dot(a, b, preferred_element_type=F32)


def attend(q, k, v):
    seq, cols = q.shape
    pair = 2 * HD
    left = lax.broadcasted_iota(jnp.int32, (seq, pair), 1) < HD
    zero = jnp.zeros((seq, pair), BF)
    out = []
    for at in range(0, cols, pair):
        both = q[:, at : at + pair]
        spread = jnp.concatenate([jnp.where(left, both, zero), jnp.where(left, zero, both)], axis=0)
        s = dot_t(k[:, at : at + pair], spread)
        e = jnp.exp2((s - jnp.max(s, axis=0, keepdims=True)) * (HD**-0.5 * LOG2E))
        p = (e * (1.0 / jnp.sum(e, axis=0, keepdims=True))).astype(BF).astype(F32)
        first = jnp.sum(p[:, :seq], axis=1, keepdims=True)
        second = jnp.sum(p[:, seq:], axis=1, keepdims=True)
        context = jnp.where(left, first, second) * v[:, at : at + pair].astype(F32)
        out.append(jnp.sum(context, axis=0, keepdims=True) * (1.0 / seq))
    return jnp.concatenate(out, axis=1)


def attention_kernel(
    heads, texts_ref, w_hbm, cot_ref, ids_ref, out_ref, wp, acc_p, acc_m, held, w_ref, sem
):
    step = pl.program_id(0)
    nodes, seq, width = held.shape[1:]
    node_dev = cot_ref.shape[0]
    cols = heads * HD

    some, deep = nodes // COPIES, width // COPIES

    def fetch(i):
        return [
            pltpu.make_async_copy(
                texts_ref.at[pl.ds(i * nodes + c * some, some)],
                held.at[i % 2, pl.ds(c * some, some)],
                sem.at[i % 2, c],
            )
            for c in range(COPIES)
        ]

    @pl.when(step == 0)
    def _():
        weights = [
            pltpu.make_async_copy(
                w_hbm.at[pl.ds(c * deep, deep)], w_ref.at[pl.ds(c * deep, deep)], sem.at[2, c]
            )
            for c in range(COPIES)
        ]
        for copy in weights + fetch(0):
            copy.start()
        for copy in weights:
            copy.wait()
        for part in range(3):
            for h in range(0, heads, 2):
                a = h * 3 * HD + part * HD
                b = a + 3 * HD
                wp[:, part * cols + h * HD : part * cols + (h + 2) * HD] = jnp.concatenate(
                    [w_ref[:, a : a + HD], w_ref[:, b : b + HD]], axis=1
                )

    @pl.when(step + 1 < pl.num_programs(0))
    def _():
        for copy in fetch(step + 1):
            copy.start()

    for copy in fetch(step):
        copy.wait()
    x_ref = held.at[step % 2]
    own = pl.ds(pl.multiple_of(lax.axis_index("mp") * cols, 128), cols)
    qkv = dot(x_ref[...].reshape(nodes * seq, width), wp[...]).astype(BF)
    for n in range(nodes):
        at = slice(n * seq, (n + 1) * seq)
        row = pl.ds(step * nodes + n, 1)
        acc_p[row, :] = attend(*(qkv[at, i * cols : (i + 1) * cols] for i in range(3)))
        mean = jnp.sum(x_ref[n, :, own].astype(F32), axis=0, keepdims=True)
        acc_m[row, :] = mean * (1.0 / seq)

    @pl.when(step == pl.num_programs(0) - 1)
    def _():
        rows = jnp.concatenate([acc_p[...], cot_ref[...].astype(F32), acc_m[...]], axis=1)
        shifted = ids_ref[...] + 1
        fan = shifted.shape[0]
        gap = jnp.zeros((fan, IDS_AT - node_dev), F32)
        high, low = (shifted >> 4).astype(F32), (shifted & 15).astype(F32)
        blank = jnp.zeros((fan, IDS_COLS - 2 * IDS_AT), F32)
        ids = jnp.concatenate([high, gap, low, gap, blank], axis=1)
        wide = 3 * cols
        rest = jnp.concatenate([rows[TOP:, : wide // 2], rows[TOP:, wide // 2 :]], axis=0)
        out_ref[:, :wide] = rows[:TOP].astype(BF)
        out_ref[:, wide : wide + wide // 2] = rest.astype(BF)
        out_ref[:, wide + wide // 2 :] = ids.astype(BF)


def unpack(got, cols, part):
    got = got.astype(F32)
    wide, at = 3 * cols, part * cols
    pieces, left = [], at
    while left < at + cols:
        side, inside = divmod(left, wide // 2)
        right = min(at + cols, (side + 1) * (wide // 2))
        low = wide + inside
        pieces.append(got[:, side * (TOP // 2) : (side + 1) * (TOP // 2), low : low + right - left])
        left = right
    rest = jnp.concatenate(pieces, axis=2) if len(pieces) > 1 else pieces[0]
    return jnp.concatenate([got[:, :, at : at + cols], rest], axis=1)


def attention(texts, w_qkv, cotangent, ids):
    node_dev, seq, width = texts.shape
    cols = w_qkv.shape[1] // 3
    heads = cols // HD
    tokens = node_dev * seq
    nodes = NODES_STEP
    packed = (TOP, 3 * cols + 3 * cols // 2 + IDS_COLS)
    return pl.pallas_call(
        functools.partial(attention_kernel, heads),
        out_shape=jax.ShapeDtypeStruct(packed, BF),
        grid=(node_dev // nodes,),
        in_specs=[
            pl.BlockSpec(memory_space=pl.ANY),
            pl.BlockSpec(memory_space=pl.ANY),
            pl.BlockSpec((node_dev, cols), lambda i: (0, 0)),
            pl.BlockSpec(ids.shape, lambda i: (0, 0)),
        ],
        out_specs=pl.BlockSpec(packed, lambda i: (0, 0)),
        scratch_shapes=[
            pltpu.VMEM((width, 3 * cols), BF),
            pltpu.VMEM((node_dev, cols), F32),
            pltpu.VMEM((node_dev, cols), F32),
            pltpu.VMEM((2, nodes, seq, width), BF),
            pltpu.VMEM((width, 3 * cols), BF),
            pltpu.SemaphoreType.DMA((3, COPIES)),
        ],
        compiler_params=pltpu.CompilerParams(vmem_limit_bytes=ATTENTION_VMEM * MIB),
        cost_estimate=pl.CostEstimate(
            flops=2 * tokens * width * 3 * cols + 8 * tokens * seq * cols,
            bytes_accessed=2 * tokens * width + 6 * width * cols,
            transcendentals=tokens * seq * heads,
        ),
    )(texts, w_qkv, cotangent, ids)


def gelu_parts(z):
    root = 0.7978845608028654
    cube = 0.044715
    t = jnp.tanh(root * (z + cube * (z * z * z)))
    half = 0.5 * (1.0 + t)
    slope = half + 0.5 * z * (1.0 - t * t) * (root * (1.0 + 3.0 * cube * (z * z)))
    return z * half, slope


def block_place(r, cols):
    return pl.ds(pl.multiple_of((lax.axis_index("mp") ^ r) * cols, 128), cols)


def embed_kernel(order, fan, node_dev, *refs):
    parts = 4
    got, blocks, refs = refs[:parts], refs[parts : 2 * parts], refs[2 * parts :]
    both, cot, pooled_ref, counts_ref, share_ref, mean = refs
    dp = lax.axis_index("dp")
    groups = got[0].shape[0]
    nodes = groups * node_dev
    cols = blocks[0].shape[0]

    def part(r, i):
        return unpack(got[r][...], cols, i).reshape(nodes, cols)

    packed = got[0][:, :, got[0].shape[2] - IDS_COLS :].astype(F32)
    ids = jnp.concatenate(
        [
            packed[i, :fan, :node_dev] * 16.0 + packed[i, :fan, IDS_AT : IDS_AT + node_dev] - 1.0
            for i in range(groups)
        ],
        axis=1,
    )
    place_of = lax.broadcasted_iota(jnp.int32, (nodes, 1), 0)
    names = place_of
    for i, o in enumerate(order):
        shift = ((dp ^ o) - i) * node_dev
        inside = (place_of >= i * node_dev) & (place_of < (i + 1) * node_dev)
        names = jnp.where(inside, place_of + shift, names)
    names = names.astype(F32)
    counts_t = jnp.zeros((nodes, nodes), F32)
    for s in range(fan):
        counts_t += (ids[s : s + 1, :] == names).astype(F32)
    counts = counts_t.T
    share = 1.0 / jnp.maximum(jnp.sum(counts, axis=1, keepdims=True), 1.0)
    counts_ref[...] = counts_t.astype(BF)
    share_ref[...] = jnp.broadcast_to(share, share_ref.shape)

    pooled = [part(r, 0).astype(BF) for r in range(parts)]
    pooled_ref[...] = pooled[0]
    for r in range(parts):
        cot[:, block_place(r, cols)] = part(r, 1).astype(BF)
        mean[:, block_place(r, cols)] = part(r, 2)
    sums = sum(dot(pooled[r], blocks[r][...]) for r in range(parts))
    both[0] = (mean[...] + sums).astype(BF)
    both[1] = (dot(counts.astype(BF), both[0]) * share).astype(BF)


def graph_kernel(node_dev, both, cot, pooled, counts, share_ref, *refs):
    parts = 4
    blocks, refs = refs[: 2 * parts], refs[2 * parts :]
    mixed_ref, grad_ref, g_self, g_neigh, g_out, dz, wide, grads, sem = refs
    side = (lax.axis_index("dp") // 2) % 2
    cols, width = g_self.shape
    nodes = counts.shape[0]
    factor = 1.0 / jnp.sqrt(jnp.float32(nodes))
    own = block_place(0, cols)

    z = 0.0
    for r in range(parts):
        first = 0 if r < 2 else side
        z += dot(both[first, :, block_place(r, cols)], blocks[2 * r][...])
        z += dot(both[1 - first, :, block_place(r, cols)], blocks[2 * r + 1][...])
    mixed, slope = gelu_parts(z)
    dz[...] = (cot[...].astype(F32) * slope).astype(BF)
    wide[...] = mixed[:node_dev, :]
    mixed_ref[...] = wide[:, own].astype(BF)

    copies = []
    for i, out in enumerate((g_self, g_neigh)):
        grads[i] = t_dot(both[i, :, own], dz[...]) * factor
        copies.append(pltpu.make_async_copy(grads.at[i], out, sem.at[i]))
        copies[-1].start()
    share = share_ref[:, :1]
    for r in range(parts):
        to_self, to_agg = dot_t(dz[...], blocks[2 * r][...]), dot_t(dz[...], blocks[2 * r + 1][...])
        if r >= 2:
            even = side == 0
            to_self, to_agg = jnp.where(even, to_self, to_agg), jnp.where(even, to_agg, to_self)
        total = to_self + dot(counts[...], (to_agg * share).astype(BF))
        if r == 0:
            grad_ref[...] = total[:node_dev, :].astype(BF)
        at = slice(r * cols, (r + 1) * cols)
        grads[2, :, at] = t_dot(pooled[...], total.astype(BF)) * factor
        copies.append(
            pltpu.make_async_copy(grads.at[2, :, at], g_out.at[:, block_place(r, cols)], sem.at[2 + r])
        )
        copies[-1].start()
    for copy in copies:
        copy.wait()


def graph(order, fan, node_dev, got, weights):
    parts = len(got)
    cols, width = weights[0][0].shape
    nodes = got[0].shape[0] * node_dev
    vmem = pl.BlockSpec(memory_space=pltpu.VMEM)
    known = pl.pallas_call(
        functools.partial(embed_kernel, order, fan, node_dev),
        out_shape=(
            jax.ShapeDtypeStruct((2, nodes, width), BF),
            jax.ShapeDtypeStruct((nodes, width), BF),
            jax.ShapeDtypeStruct((nodes, cols), BF),
            jax.ShapeDtypeStruct((nodes, nodes), BF),
            jax.ShapeDtypeStruct((nodes, 128), F32),
        ),
        in_specs=[vmem] * (2 * parts),
        out_specs=(vmem,) * 5,
        scratch_shapes=[pltpu.VMEM((nodes, width), F32)],
        compiler_params=pltpu.CompilerParams(vmem_limit_bytes=24 * MIB),
        cost_estimate=pl.CostEstimate(
            flops=2 * nodes * width * width * 2, bytes_accessed=4 * MIB, transcendentals=0
        ),
    )(*got, *[group[0] for group in weights])
    slab = jax.ShapeDtypeStruct((node_dev, cols), BF)
    big = jax.ShapeDtypeStruct((cols, width), F32)
    anywhere = pl.BlockSpec(memory_space=pl.ANY)
    return pl.pallas_call(
        functools.partial(graph_kernel, node_dev),
        out_shape=(slab, slab, big, big, big),
        in_specs=[vmem] * (5 + 2 * parts),
        out_specs=(vmem, vmem, anywhere, anywhere, anywhere),
        scratch_shapes=[
            pltpu.VMEM((nodes, width), BF),
            pltpu.VMEM((node_dev, width), F32),
            pltpu.VMEM((3, cols, width), F32),
            pltpu.SemaphoreType.DMA((2 + parts,)),
        ],
        compiler_params=pltpu.CompilerParams(vmem_limit_bytes=36 * MIB),
        cost_estimate=pl.CostEstimate(
            flops=2 * nodes * width * width * 5, bytes_accessed=8 * MIB, transcendentals=nodes * width
        ),
    )(*known, *sum((group[1:] for group in weights), ()))


def graph_wide(order, fan, node_dev, got, weights):
    mp, dp = lax.axis_index("mp"), lax.axis_index("dp")
    parts = len(got)
    cols, width = weights[0][0].shape
    nodes = got[0].shape[0] * node_dev
    owners = jnp.array(order, jnp.int32) ^ dp
    names = (owners[:, None] * node_dev + jnp.arange(node_dev)[None, :]).reshape(1, 1, nodes)
    order = jnp.arange(parts) ^ mp
    even = (dp // 2) % 2 == 0
    kinds = [
        [group[0], jnp.where(even, group[1], group[2]), jnp.where(even, group[2], group[1])]
        for group in weights[2:]
    ]
    blocks = [*weights[:2], *kinds]
    w_out, w_self, w_neigh = (
        jnp.stack([group[k] for group in blocks])[order].reshape(width, width) for k in range(3)
    )

    def part(i):
        block = jnp.stack([unpack(g, cols, i) for g in got])[order]
        return block.transpose(1, 2, 0, 3).reshape(nodes, width)

    pooled = part(0).astype(BF)
    packed = got[0][:, :fan, got[0].shape[2] - IDS_COLS :].astype(jnp.int32)
    ids = packed[:, :, :node_dev] * 16 + packed[:, :, IDS_AT : IDS_AT + node_dev] - 1
    ids = ids.transpose(0, 2, 1).reshape(nodes, fan)
    cnt = jnp.maximum(jnp.sum(ids >= 0, axis=1).astype(F32), 1.0)[:, None]
    counts = jnp.sum(ids[:, :, None] == names, axis=1).astype(BF)
    embed = (part(2) + dot(pooled, w_out)).astype(BF)
    agg = (dot(counts, embed) / cnt).astype(BF)
    mixed, slope = gelu_parts(dot(embed, w_self) + dot(agg, w_neigh))
    dz = (part(1) * slope).astype(BF)
    msg = (dot_t(dz, w_neigh) / cnt).astype(BF)
    node_grad = (dot_t(dz, w_self) + t_dot(counts, msg)).astype(BF)
    factor = 1.0 / jnp.sqrt(jnp.float32(nodes))

    def own(a):
        return lax.dynamic_slice_in_dim(a, mp * cols, cols, 1)

    grads = [t_dot(own(a), b) * factor for a, b in ((embed, dz), (agg, dz), (pooled, node_grad))]
    return (own(mixed[:node_dev]).astype(BF), own(node_grad[:node_dev]), *grads)


def join_kernel(*refs):
    out, at = refs[-1], 0
    for ref in refs[:-1]:
        out[at : at + ref.shape[0]] = ref[...]
        at += ref.shape[0]


def join(*blocks):
    count = sum(b.shape[0] for b in blocks)
    if count > 8:
        return jnp.concatenate(blocks)
    vmem = pl.BlockSpec(memory_space=pltpu.VMEM)
    return pl.pallas_call(
        join_kernel,
        out_shape=jax.ShapeDtypeStruct((count, *blocks[0].shape[1:]), BF),
        in_specs=[vmem] * len(blocks),
        out_specs=vmem,
        compiler_params=pltpu.CompilerParams(vmem_limit_bytes=8 * MIB),
    )(*blocks)


def hop(x, axis, bit):
    return lax.ppermute(x, axis, [(i, i ^ bit) for i in range(lax.axis_size(axis))])


def gather_dp(block, later):
    size = lax.axis_size("dp")
    if size == 8:
        far = [hop(block, "dp", i) for i in (2, 4, 6)]
        mine = join(block)
        mine, far, later = lax.optimization_barrier((mine, far, later))
        block = join(mine, *far)
        order, bit = [0, 2, 4, 6], 1
    else:
        order, bit = [0], size // 2
    while bit:
        block = join(block, hop(block, "dp", bit))
        order = order + [i ^ bit for i in order]
        bit //= 2
    return block, order, later


def per_device(texts, w_qkv, w_out, w_self, w_neigh, neighbours, cotangent):
    node_dev, fan = neighbours.shape
    nodes = node_dev * lax.axis_size("dp")
    own = (w_out, w_self, w_neigh)
    even = (lax.axis_index("dp") // 2) % 2 == 0
    picked, w_out = lax.optimization_barrier((jnp.where(even, w_self, w_neigh), w_out))
    x_half = hop(picked, "mp", 2)
    x_out = hop(w_out, "mp", 2)
    here = tuple(hop(a, "mp", 1) for a in own)

    sent = attention(texts, w_qkv, cotangent, neighbours.T)[None]
    sent, here = lax.optimization_barrier((sent, here))
    sent, order, x_half = gather_dp(sent, x_half)
    sent, x_out = lax.optimization_barrier((sent, x_out))
    z_half = hop(x_half, "dp", 2)
    core_sent = hop(sent, "mp", 1)
    z_half, core_sent = lax.optimization_barrier((z_half, core_sent))
    across = (x_out, x_half, z_half)
    there = tuple(hop(a, "mp", 1) for a in across)

    got_across = hop(sent, "mp", 2)
    got = (sent, core_sent, got_across, hop(got_across, "mp", 1))
    body = graph if nodes <= WIDE_LIMIT else graph_wide
    return body(order, fan, node_dev, got, (own, here, across, there))


def solution(mesh):
    return jax.shard_map(
        per_device,
        mesh=mesh,
        in_specs=(
            P("dp", None, None),
            P(None, "mp"),
            P("mp", None),
            P("mp", None),
            P("mp", None),
            P("dp", None),
            P("dp", "mp"),
        ),
        out_specs=(P("dp", "mp"), P("dp", "mp"), P("mp", None), P("mp", None), P("mp", None)),
        check_vma=False,
    )
```

```python
import functools

import jax
import jax.numpy as jnp
from jax import lax
from jax.experimental import pallas as pl
from jax.experimental.pallas import tpu as pltpu
from jax.sharding import PartitionSpec as P

HD = 64
BF = jnp.bfloat16
F32 = jnp.float32
NODES_STEP = 8
WIDE_LIMIT = 256
IDS_COLS = 128
IDS_AT = 32
TOP = 16
LOG2E = 1.4426950408889634
ATTENTION_VMEM = 58
COPIES = 4
MIB = 1 << 20


def dot_t(a, b):
    return lax.dot_general(a, b, (((1,), (1,)), ((), ())), preferred_element_type=F32)


def t_dot(a, b):
    return lax.dot_general(a, b, (((0,), (0,)), ((), ())), preferred_element_type=F32)


def dot(a, b):
    return jnp.dot(a, b, preferred_element_type=F32)


def attend(q, k, v):
    seq, cols = q.shape
    pair = 2 * HD
    left = lax.broadcasted_iota(jnp.int32, (seq, pair), 1) < HD
    zero = jnp.zeros((seq, pair), BF)
    out = []
    for at in range(0, cols, pair):
        both = q[:, at : at + pair]
        spread = jnp.concatenate([jnp.where(left, both, zero), jnp.where(left, zero, both)], axis=0)
        s = dot_t(k[:, at : at + pair], spread)
        e = jnp.exp2((s - jnp.max(s, axis=0, keepdims=True)) * (HD**-0.5 * LOG2E))
        p = (e * (1.0 / jnp.sum(e, axis=0, keepdims=True))).astype(BF).astype(F32)
        first = jnp.sum(p[:, :seq], axis=1, keepdims=True)
        second = jnp.sum(p[:, seq:], axis=1, keepdims=True)
        context = jnp.where(left, first, second) * v[:, at : at + pair].astype(F32)
        out.append(jnp.sum(context, axis=0, keepdims=True) * (1.0 / seq))
    return jnp.concatenate(out, axis=1)


def attention_kernel(
    heads, texts_ref, w_hbm, cot_ref, ids_ref, out_ref, wp, acc_p, acc_m, held, w_ref, sem
):
    step = pl.program_id(0)
    nodes, seq, width = held.shape[1:]
    node_dev = cot_ref.shape[0]
    cols = heads * HD

    some, deep = nodes // COPIES, width // COPIES

    def fetch(i):
        return [
            pltpu.make_async_copy(
                texts_ref.at[pl.ds(i * nodes + c * some, some)],
                held.at[i % 2, pl.ds(c * some, some)],
                sem.at[i % 2, c],
            )
            for c in range(COPIES)
        ]

    @pl.when(step == 0)
    def _():
        weights = [
            pltpu.make_async_copy(
                w_hbm.at[pl.ds(c * deep, deep)], w_ref.at[pl.ds(c * deep, deep)], sem.at[2, c]
            )
            for c in range(COPIES)
        ]
        for copy in weights + fetch(0):
            copy.start()
        for copy in weights:
            copy.wait()
        for part in range(3):
            for h in range(0, heads, 2):
                a = h * 3 * HD + part * HD
                b = a + 3 * HD
                wp[:, part * cols + h * HD : part * cols + (h + 2) * HD] = jnp.concatenate(
                    [w_ref[:, a : a + HD], w_ref[:, b : b + HD]], axis=1
                )

    @pl.when(step + 1 < pl.num_programs(0))
    def _():
        for copy in fetch(step + 1):
            copy.start()

    for copy in fetch(step):
        copy.wait()
    x_ref = held.at[step % 2]
    own = pl.ds(pl.multiple_of(lax.axis_index("mp") * cols, 128), cols)
    qkv = dot(x_ref[...].reshape(nodes * seq, width), wp[...]).astype(BF)
    for n in range(nodes):
        at = slice(n * seq, (n + 1) * seq)
        row = pl.ds(step * nodes + n, 1)
        acc_p[row, :] = attend(*(qkv[at, i * cols : (i + 1) * cols] for i in range(3)))
        mean = jnp.sum(x_ref[n, :, own].astype(F32), axis=0, keepdims=True)
        acc_m[row, :] = mean * (1.0 / seq)

    @pl.when(step == pl.num_programs(0) - 1)
    def _():
        rows = jnp.concatenate([acc_p[...], cot_ref[...].astype(F32), acc_m[...]], axis=1)
        shifted = ids_ref[...] + 1
        fan = shifted.shape[0]
        gap = jnp.zeros((fan, IDS_AT - node_dev), F32)
        high, low = (shifted >> 4).astype(F32), (shifted & 15).astype(F32)
        blank = jnp.zeros((fan, IDS_COLS - 2 * IDS_AT), F32)
        ids = jnp.concatenate([high, gap, low, gap, blank], axis=1)
        wide = 3 * cols
        rest = jnp.concatenate([rows[TOP:, : wide // 2], rows[TOP:, wide // 2 :]], axis=0)
        out_ref[:, :wide] = rows[:TOP].astype(BF)
        out_ref[:, wide : wide + wide // 2] = rest.astype(BF)
        out_ref[:, wide + wide // 2 :] = ids.astype(BF)


def unpack(got, cols, part):
    got = got.astype(F32)
    wide, at = 3 * cols, part * cols
    pieces, left = [], at
    while left < at + cols:
        side, inside = divmod(left, wide // 2)
        right = min(at + cols, (side + 1) * (wide // 2))
        low = wide + inside
        pieces.append(got[:, side * (TOP // 2) : (side + 1) * (TOP // 2), low : low + right - left])
        left = right
    rest = jnp.concatenate(pieces, axis=2) if len(pieces) > 1 else pieces[0]
    return jnp.concatenate([got[:, :, at : at + cols], rest], axis=1)


def attention(texts, w_qkv, cotangent, ids):
    node_dev, seq, width = texts.shape
    cols = w_qkv.shape[1] // 3
    heads = cols // HD
    tokens = node_dev * seq
    nodes = NODES_STEP
    packed = (TOP, 3 * cols + 3 * cols // 2 + IDS_COLS)
    return pl.pallas_call(
        functools.partial(attention_kernel, heads),
        out_shape=jax.ShapeDtypeStruct(packed, BF),
        grid=(node_dev // nodes,),
        in_specs=[
            pl.BlockSpec(memory_space=pl.ANY),
            pl.BlockSpec(memory_space=pl.ANY),
            pl.BlockSpec((node_dev, cols), lambda i: (0, 0)),
            pl.BlockSpec(ids.shape, lambda i: (0, 0)),
        ],
        out_specs=pl.BlockSpec(packed, lambda i: (0, 0)),
        scratch_shapes=[
            pltpu.VMEM((width, 3 * cols), BF),
            pltpu.VMEM((node_dev, cols), F32),
            pltpu.VMEM((node_dev, cols), F32),
            pltpu.VMEM((2, nodes, seq, width), BF),
            pltpu.VMEM((width, 3 * cols), BF),
            pltpu.SemaphoreType.DMA((3, COPIES)),
        ],
        compiler_params=pltpu.CompilerParams(vmem_limit_bytes=ATTENTION_VMEM * MIB),
        cost_estimate=pl.CostEstimate(
            flops=2 * tokens * width * 3 * cols + 8 * tokens * seq * cols,
            bytes_accessed=2 * tokens * width + 6 * width * cols,
            transcendentals=tokens * seq * heads,
        ),
    )(texts, w_qkv, cotangent, ids)


def gelu_parts(z):
    root = 0.7978845608028654
    cube = 0.044715
    t = jnp.tanh(root * (z + cube * (z * z * z)))
    half = 0.5 * (1.0 + t)
    slope = half + 0.5 * z * (1.0 - t * t) * (root * (1.0 + 3.0 * cube * (z * z)))
    return z * half, slope


def block_place(r, cols):
    return pl.ds(pl.multiple_of((lax.axis_index("mp") ^ r) * cols, 128), cols)


def embed_kernel(order, fan, node_dev, *refs):
    parts = 4
    got, blocks, refs = refs[:parts], refs[parts : 2 * parts], refs[2 * parts :]
    both, cot, pooled_ref, counts_ref, share_ref, mean = refs
    dp = lax.axis_index("dp")
    groups = got[0].shape[0]
    nodes = groups * node_dev
    cols = blocks[0].shape[0]

    def part(r, i):
        return unpack(got[r][...], cols, i).reshape(nodes, cols)

    packed = got[0][:, :, got[0].shape[2] - IDS_COLS :].astype(F32)
    ids = jnp.concatenate(
        [
            packed[i, :fan, :node_dev] * 16.0 + packed[i, :fan, IDS_AT : IDS_AT + node_dev] - 1.0
            for i in range(groups)
        ],
        axis=1,
    )
    place_of = lax.broadcasted_iota(jnp.int32, (nodes, 1), 0)
    names = place_of
    for i, o in enumerate(order):
        shift = ((dp ^ o) - i) * node_dev
        inside = (place_of >= i * node_dev) & (place_of < (i + 1) * node_dev)
        names = jnp.where(inside, place_of + shift, names)
    names = names.astype(F32)
    counts_t = jnp.zeros((nodes, nodes), F32)
    for s in range(fan):
        counts_t += (ids[s : s + 1, :] == names).astype(F32)
    counts = counts_t.T
    share = 1.0 / jnp.maximum(jnp.sum(counts, axis=1, keepdims=True), 1.0)
    counts_ref[...] = counts_t.astype(BF)
    share_ref[...] = jnp.broadcast_to(share, share_ref.shape)

    pooled = [part(r, 0).astype(BF) for r in range(parts)]
    pooled_ref[...] = pooled[0]
    for r in range(parts):
        cot[:, block_place(r, cols)] = part(r, 1).astype(BF)
        mean[:, block_place(r, cols)] = part(r, 2)
    sums = sum(dot(pooled[r], blocks[r][...]) for r in range(parts))
    both[0] = (mean[...] + sums).astype(BF)
    both[1] = (dot(counts.astype(BF), both[0]) * share).astype(BF)


def graph_kernel(node_dev, both, cot, pooled, counts, share_ref, *refs):
    parts = 4
    blocks, refs = refs[: 2 * parts], refs[2 * parts :]
    mixed_ref, grad_ref, g_self, g_neigh, g_out, dz, wide, grads, sem = refs
    side = (lax.axis_index("dp") // 2) % 2
    cols, width = g_self.shape
    nodes = counts.shape[0]
    factor = 1.0 / jnp.sqrt(jnp.float32(nodes))
    own = block_place(0, cols)

    z = 0.0
    for r in range(parts):
        first = 0 if r < 2 else side
        z += dot(both[first, :, block_place(r, cols)], blocks[2 * r][...])
        z += dot(both[1 - first, :, block_place(r, cols)], blocks[2 * r + 1][...])
    mixed, slope = gelu_parts(z)
    dz[...] = (cot[...].astype(F32) * slope).astype(BF)
    wide[...] = mixed[:node_dev, :]
    mixed_ref[...] = wide[:, own].astype(BF)

    copies = []
    for i, out in enumerate((g_self, g_neigh)):
        grads[i] = t_dot(both[i, :, own], dz[...]) * factor
        copies.append(pltpu.make_async_copy(grads.at[i], out, sem.at[i]))
        copies[-1].start()
    share = share_ref[:, :1]
    for r in range(parts):
        to_self, to_agg = dot_t(dz[...], blocks[2 * r][...]), dot_t(dz[...], blocks[2 * r + 1][...])
        if r >= 2:
            even = side == 0
            to_self, to_agg = jnp.where(even, to_self, to_agg), jnp.where(even, to_agg, to_self)
        total = to_self + dot(counts[...], (to_agg * share).astype(BF))
        if r == 0:
            grad_ref[...] = total[:node_dev, :].astype(BF)
        at = slice(r * cols, (r + 1) * cols)
        grads[2, :, at] = t_dot(pooled[...], total.astype(BF)) * factor
        copies.append(
            pltpu.make_async_copy(grads.at[2, :, at], g_out.at[:, block_place(r, cols)], sem.at[2 + r])
        )
        copies[-1].start()
    for copy in copies:
        copy.wait()


def graph(order, fan, node_dev, got, weights):
    parts = len(got)
    cols, width = weights[0][0].shape
    nodes = got[0].shape[0] * node_dev
    vmem = pl.BlockSpec(memory_space=pltpu.VMEM)
    anywhere = pl.BlockSpec(memory_space=pl.ANY)
    slab = jax.ShapeDtypeStruct((node_dev, cols), BF)
    big = jax.ShapeDtypeStruct((cols, width), F32)

    def kernel(*refs):
        first, rest = refs[: 2 * parts], refs[2 * parts : 4 * parts]
        outs, known = refs[4 * parts : 4 * parts + 5], refs[4 * parts + 5 : 4 * parts + 10]
        mean, *own = refs[4 * parts + 10 :]
        embed_kernel(order, fan, node_dev, *first, *known, mean)
        graph_kernel(node_dev, *known, *rest, *outs, *own)

    return pl.pallas_call(
        kernel,
        out_shape=(slab, slab, big, big, big),
        in_specs=[vmem] * (4 * parts),
        out_specs=(vmem, vmem, anywhere, anywhere, anywhere),
        scratch_shapes=[
            pltpu.VMEM((2, nodes, width), BF),
            pltpu.VMEM((nodes, width), BF),
            pltpu.VMEM((nodes, cols), BF),
            pltpu.VMEM((nodes, nodes), BF),
            pltpu.VMEM((nodes, 128), F32),
            pltpu.VMEM((nodes, width), F32),
            pltpu.VMEM((nodes, width), BF),
            pltpu.VMEM((node_dev, width), F32),
            pltpu.VMEM((3, cols, width), F32),
            pltpu.SemaphoreType.DMA((2 + parts,)),
        ],
        compiler_params=pltpu.CompilerParams(vmem_limit_bytes=36 * MIB),
        cost_estimate=pl.CostEstimate(
            flops=2 * nodes * width * width * 6, bytes_accessed=10 * MIB, transcendentals=nodes * width
        ),
    )(*got, *[group[0] for group in weights], *sum((group[1:] for group in weights), ()))


def graph_wide(order, fan, node_dev, got, weights):
    mp, dp = lax.axis_index("mp"), lax.axis_index("dp")
    parts = len(got)
    cols, width = weights[0][0].shape
    nodes = got[0].shape[0] * node_dev
    owners = jnp.array(order, jnp.int32) ^ dp
    names = (owners[:, None] * node_dev + jnp.arange(node_dev)[None, :]).reshape(1, 1, nodes)
    order = jnp.arange(parts) ^ mp
    even = (dp // 2) % 2 == 0
    kinds = [
        [group[0], jnp.where(even, group[1], group[2]), jnp.where(even, group[2], group[1])]
        for group in weights[2:]
    ]
    blocks = [*weights[:2], *kinds]
    w_out, w_self, w_neigh = (
        jnp.stack([group[k] for group in blocks])[order].reshape(width, width) for k in range(3)
    )

    def part(i):
        block = jnp.stack([unpack(g, cols, i) for g in got])[order]
        return block.transpose(1, 2, 0, 3).reshape(nodes, width)

    pooled = part(0).astype(BF)
    packed = got[0][:, :fan, got[0].shape[2] - IDS_COLS :].astype(jnp.int32)
    ids = packed[:, :, :node_dev] * 16 + packed[:, :, IDS_AT : IDS_AT + node_dev] - 1
    ids = ids.transpose(0, 2, 1).reshape(nodes, fan)
    cnt = jnp.maximum(jnp.sum(ids >= 0, axis=1).astype(F32), 1.0)[:, None]
    counts = jnp.sum(ids[:, :, None] == names, axis=1).astype(BF)
    embed = (part(2) + dot(pooled, w_out)).astype(BF)
    agg = (dot(counts, embed) / cnt).astype(BF)
    mixed, slope = gelu_parts(dot(embed, w_self) + dot(agg, w_neigh))
    dz = (part(1) * slope).astype(BF)
    msg = (dot_t(dz, w_neigh) / cnt).astype(BF)
    node_grad = (dot_t(dz, w_self) + t_dot(counts, msg)).astype(BF)
    factor = 1.0 / jnp.sqrt(jnp.float32(nodes))

    def own(a):
        return lax.dynamic_slice_in_dim(a, mp * cols, cols, 1)

    grads = [t_dot(own(a), b) * factor for a, b in ((embed, dz), (agg, dz), (pooled, node_grad))]
    return (own(mixed[:node_dev]).astype(BF), own(node_grad[:node_dev]), *grads)


def join_kernel(*refs):
    out, at = refs[-1], 0
    for ref in refs[:-1]:
        out[at : at + ref.shape[0]] = ref[...]
        at += ref.shape[0]


def join(*blocks):
    count = sum(b.shape[0] for b in blocks)
    if count > 8:
        return jnp.concatenate(blocks)
    vmem = pl.BlockSpec(memory_space=pltpu.VMEM)
    return pl.pallas_call(
        join_kernel,
        out_shape=jax.ShapeDtypeStruct((count, *blocks[0].shape[1:]), BF),
        in_specs=[vmem] * len(blocks),
        out_specs=vmem,
        compiler_params=pltpu.CompilerParams(vmem_limit_bytes=8 * MIB),
    )(*blocks)


def hop(x, axis, bit):
    return lax.ppermute(x, axis, [(i, i ^ bit) for i in range(lax.axis_size(axis))])


def gather_dp(block, later):
    size = lax.axis_size("dp")
    if size == 8:
        far = [hop(block, "dp", i) for i in (2, 4, 6)]
        mine = join(block)
        mine, far, later = lax.optimization_barrier((mine, far, later))
        block = join(mine, *far)
        order, bit = [0, 2, 4, 6], 1
    else:
        order, bit = [0], size // 2
    while bit:
        block = join(block, hop(block, "dp", bit))
        order = order + [i ^ bit for i in order]
        bit //= 2
    return block, order, later


def per_device(texts, w_qkv, w_out, w_self, w_neigh, neighbours, cotangent):
    node_dev, fan = neighbours.shape
    nodes = node_dev * lax.axis_size("dp")
    own = (w_out, w_self, w_neigh)
    even = (lax.axis_index("dp") // 2) % 2 == 0
    picked, w_out = lax.optimization_barrier((jnp.where(even, w_self, w_neigh), w_out))
    x_half = hop(picked, "mp", 2)
    x_out = hop(w_out, "mp", 2)
    here = tuple(hop(a, "mp", 1) for a in own)

    sent = attention(texts, w_qkv, cotangent, neighbours.T)[None]
    sent, here = lax.optimization_barrier((sent, here))
    sent, order, x_half = gather_dp(sent, x_half)
    sent, x_out = lax.optimization_barrier((sent, x_out))
    z_half = hop(x_half, "dp", 2)
    across = (x_out, x_half, z_half)
    there = tuple(hop(a, "mp", 1) for a in across)

    got_across = hop(sent, "mp", 2)
    got = (sent, hop(sent, "mp", 1), got_across, hop(got_across, "mp", 1))
    body = graph if nodes <= WIDE_LIMIT else graph_wide
    return body(order, fan, node_dev, got, (own, here, across, there))


def solution(mesh):
    return jax.shard_map(
        per_device,
        mesh=mesh,
        in_specs=(
            P("dp", None, None),
            P(None, "mp"),
            P("mp", None),
            P("mp", None),
            P("mp", None),
            P("dp", None),
            P("dp", "mp"),
        ),
        out_specs=(P("dp", "mp"), P("dp", "mp"), P("mp", None), P("mp", None), P("mp", None)),
        check_vma=False,
    )
```

```python
import functools

import jax
import jax.numpy as jnp
from jax import lax
from jax.experimental import pallas as pl
from jax.experimental.pallas import tpu as pltpu
from jax.sharding import PartitionSpec as P

HD = 64
BF = jnp.bfloat16
F32 = jnp.float32
NODES_STEP = 12
WIDE_LIMIT = 256
IDS_COLS = 128
IDS_AT = 32
TOP = 16
LOG2E = 1.4426950408889634
ATTENTION_VMEM = 58
COPIES = 4
MIB = 1 << 20


def dot_t(a, b):
    return lax.dot_general(a, b, (((1,), (1,)), ((), ())), preferred_element_type=F32)


def t_dot(a, b):
    return lax.dot_general(a, b, (((0,), (0,)), ((), ())), preferred_element_type=F32)


def dot(a, b):
    return jnp.dot(a, b, preferred_element_type=F32)


def attend(q, k, v):
    seq, cols = q.shape
    pair = 2 * HD
    left = lax.broadcasted_iota(jnp.int32, (seq, pair), 1) < HD
    zero = jnp.zeros((seq, pair), BF)
    out = []
    for at in range(0, cols, pair):
        both = q[:, at : at + pair]
        spread = jnp.concatenate([jnp.where(left, both, zero), jnp.where(left, zero, both)], axis=0)
        s = dot_t(k[:, at : at + pair], spread)
        e = jnp.exp2((s - jnp.max(s, axis=0, keepdims=True)) * (HD**-0.5 * LOG2E))
        p = (e * (1.0 / jnp.sum(e, axis=0, keepdims=True))).astype(BF).astype(F32)
        first = jnp.sum(p[:, :seq], axis=1, keepdims=True)
        second = jnp.sum(p[:, seq:], axis=1, keepdims=True)
        context = jnp.where(left, first, second) * v[:, at : at + pair].astype(F32)
        out.append(jnp.sum(context, axis=0, keepdims=True) * (1.0 / seq))
    return jnp.concatenate(out, axis=1)


def attention_kernel(
    heads, texts_ref, w_hbm, cot_ref, ids_ref, out_ref, wp, acc_p, acc_m, held, w_ref, sem
):
    step = pl.program_id(0)
    nodes, seq, width = held.shape[1:]
    node_dev = cot_ref.shape[0]
    cols = heads * HD

    some, deep = nodes // COPIES, width // COPIES

    def fetch(i):
        return [
            pltpu.make_async_copy(
                texts_ref.at[pl.ds(i * nodes + c * some, some)],
                held.at[i % 2, pl.ds(c * some, some)],
                sem.at[i % 2, c],
            )
            for c in range(COPIES)
        ]

    @pl.when(step == 0)
    def _():
        weights = [
            pltpu.make_async_copy(
                w_hbm.at[pl.ds(c * deep, deep)], w_ref.at[pl.ds(c * deep, deep)], sem.at[2, c]
            )
            for c in range(COPIES)
        ]
        for copy in weights + fetch(0):
            copy.start()
        for copy in weights:
            copy.wait()
        for part in range(3):
            for h in range(0, heads, 2):
                a = h * 3 * HD + part * HD
                b = a + 3 * HD
                wp[:, part * cols + h * HD : part * cols + (h + 2) * HD] = jnp.concatenate(
                    [w_ref[:, a : a + HD], w_ref[:, b : b + HD]], axis=1
                )

    @pl.when(step + 1 < pl.num_programs(0))
    def _():
        for copy in fetch(step + 1):
            copy.start()

    for copy in fetch(step):
        copy.wait()
    x_ref = held.at[step % 2]
    own = pl.ds(pl.multiple_of(lax.axis_index("mp") * cols, 128), cols)
    qkv = dot(x_ref[...].reshape(nodes * seq, width), wp[...]).astype(BF)
    for n in range(nodes):
        at = slice(n * seq, (n + 1) * seq)
        row = pl.ds(step * nodes + n, 1)
        acc_p[row, :] = attend(*(qkv[at, i * cols : (i + 1) * cols] for i in range(3)))
        mean = jnp.sum(x_ref[n, :, own].astype(F32), axis=0, keepdims=True)
        acc_m[row, :] = mean * (1.0 / seq)

    @pl.when(step == pl.num_programs(0) - 1)
    def _():
        rows = jnp.concatenate([acc_p[...], cot_ref[...].astype(F32), acc_m[...]], axis=1)
        shifted = ids_ref[...] + 1
        fan = shifted.shape[0]
        gap = jnp.zeros((fan, IDS_AT - node_dev), F32)
        high, low = (shifted >> 4).astype(F32), (shifted & 15).astype(F32)
        blank = jnp.zeros((fan, IDS_COLS - 2 * IDS_AT), F32)
        ids = jnp.concatenate([high, gap, low, gap, blank], axis=1)
        wide = 3 * cols
        rest = jnp.concatenate([rows[TOP:, : wide // 2], rows[TOP:, wide // 2 :]], axis=0)
        out_ref[:, :wide] = rows[:TOP].astype(BF)
        out_ref[:, wide : wide + wide // 2] = rest.astype(BF)
        out_ref[:, wide + wide // 2 :] = ids.astype(BF)


def unpack(got, cols, part):
    got = got.astype(F32)
    wide, at = 3 * cols, part * cols
    pieces, left = [], at
    while left < at + cols:
        side, inside = divmod(left, wide // 2)
        right = min(at + cols, (side + 1) * (wide // 2))
        low = wide + inside
        pieces.append(got[:, side * (TOP // 2) : (side + 1) * (TOP // 2), low : low + right - left])
        left = right
    rest = jnp.concatenate(pieces, axis=2) if len(pieces) > 1 else pieces[0]
    return jnp.concatenate([got[:, :, at : at + cols], rest], axis=1)


def attention(texts, w_qkv, cotangent, ids):
    node_dev, seq, width = texts.shape
    cols = w_qkv.shape[1] // 3
    heads = cols // HD
    tokens = node_dev * seq
    nodes = NODES_STEP
    packed = (TOP, 3 * cols + 3 * cols // 2 + IDS_COLS)
    return pl.pallas_call(
        functools.partial(attention_kernel, heads),
        out_shape=jax.ShapeDtypeStruct(packed, BF),
        grid=(node_dev // nodes,),
        in_specs=[
            pl.BlockSpec(memory_space=pl.ANY),
            pl.BlockSpec(memory_space=pl.ANY),
            pl.BlockSpec((node_dev, cols), lambda i: (0, 0)),
            pl.BlockSpec(ids.shape, lambda i: (0, 0)),
        ],
        out_specs=pl.BlockSpec(packed, lambda i: (0, 0)),
        scratch_shapes=[
            pltpu.VMEM((width, 3 * cols), BF),
            pltpu.VMEM((node_dev, cols), F32),
            pltpu.VMEM((node_dev, cols), F32),
            pltpu.VMEM((2, nodes, seq, width), BF),
            pltpu.VMEM((width, 3 * cols), BF),
            pltpu.SemaphoreType.DMA((3, COPIES)),
        ],
        compiler_params=pltpu.CompilerParams(vmem_limit_bytes=ATTENTION_VMEM * MIB),
        cost_estimate=pl.CostEstimate(
            flops=2 * tokens * width * 3 * cols + 8 * tokens * seq * cols,
            bytes_accessed=2 * tokens * width + 6 * width * cols,
            transcendentals=tokens * seq * heads,
        ),
    )(texts, w_qkv, cotangent, ids)


def gelu_parts(z):
    root = 0.7978845608028654
    cube = 0.044715
    t = jnp.tanh(root * (z + cube * (z * z * z)))
    half = 0.5 * (1.0 + t)
    slope = half + 0.5 * z * (1.0 - t * t) * (root * (1.0 + 3.0 * cube * (z * z)))
    return z * half, slope


def block_place(r, cols):
    return pl.ds(pl.multiple_of((lax.axis_index("mp") ^ r) * cols, 128), cols)


def embed_kernel(order, fan, node_dev, *refs):
    parts = 4
    got, blocks, refs = refs[:parts], refs[parts : 2 * parts], refs[2 * parts :]
    both, cot, pooled_ref, counts_ref, share_ref, mean = refs
    dp = lax.axis_index("dp")
    groups = got[0].shape[0]
    nodes = groups * node_dev
    cols = blocks[0].shape[0]

    def part(r, i):
        return unpack(got[r][...], cols, i).reshape(nodes, cols)

    packed = got[0][:, :, got[0].shape[2] - IDS_COLS :].astype(F32)
    ids = jnp.concatenate(
        [
            packed[i, :fan, :node_dev] * 16.0 + packed[i, :fan, IDS_AT : IDS_AT + node_dev] - 1.0
            for i in range(groups)
        ],
        axis=1,
    )
    place_of = lax.broadcasted_iota(jnp.int32, (nodes, 1), 0)
    names = place_of
    for i, o in enumerate(order):
        shift = ((dp ^ o) - i) * node_dev
        inside = (place_of >= i * node_dev) & (place_of < (i + 1) * node_dev)
        names = jnp.where(inside, place_of + shift, names)
    names = names.astype(F32)
    counts_t = jnp.zeros((nodes, nodes), F32)
    for s in range(fan):
        counts_t += (ids[s : s + 1, :] == names).astype(F32)
    counts = counts_t.T
    share = 1.0 / jnp.maximum(jnp.sum(counts, axis=1, keepdims=True), 1.0)
    counts_ref[...] = counts_t.astype(BF)
    share_ref[...] = jnp.broadcast_to(share, share_ref.shape)

    pooled = [part(r, 0).astype(BF) for r in range(parts)]
    pooled_ref[...] = pooled[0]
    for r in range(parts):
        cot[:, block_place(r, cols)] = part(r, 1).astype(BF)
        mean[:, block_place(r, cols)] = part(r, 2)
    sums = sum(dot(pooled[r], blocks[r][...]) for r in range(parts))
    both[0] = (mean[...] + sums).astype(BF)
    both[1] = (dot(counts.astype(BF), both[0]) * share).astype(BF)


def graph_kernel(node_dev, both, cot, pooled, counts, share_ref, *refs):
    parts = 4
    blocks, refs = refs[: 2 * parts], refs[2 * parts :]
    mixed_ref, grad_ref, g_self, g_neigh, g_out, dz, wide, grads, sem = refs
    side = (lax.axis_index("dp") // 2) % 2
    cols, width = g_self.shape
    nodes = counts.shape[0]
    factor = 1.0 / jnp.sqrt(jnp.float32(nodes))
    own = block_place(0, cols)

    z = 0.0
    for r in range(parts):
        first = 0 if r < 2 else side
        z += dot(both[first, :, block_place(r, cols)], blocks[2 * r][...])
        z += dot(both[1 - first, :, block_place(r, cols)], blocks[2 * r + 1][...])
    mixed, slope = gelu_parts(z)
    dz[...] = (cot[...].astype(F32) * slope).astype(BF)
    wide[...] = mixed[:node_dev, :]
    mixed_ref[...] = wide[:, own].astype(BF)

    copies = []
    for i, out in enumerate((g_self, g_neigh)):
        grads[i] = t_dot(both[i, :, own], dz[...]) * factor
        copies.append(pltpu.make_async_copy(grads.at[i], out, sem.at[i]))
        copies[-1].start()
    share = share_ref[:, :1]
    for r in range(parts):
        to_self, to_agg = dot_t(dz[...], blocks[2 * r][...]), dot_t(dz[...], blocks[2 * r + 1][...])
        if r >= 2:
            even = side == 0
            to_self, to_agg = jnp.where(even, to_self, to_agg), jnp.where(even, to_agg, to_self)
        total = to_self + dot(counts[...], (to_agg * share).astype(BF))
        if r == 0:
            grad_ref[...] = total[:node_dev, :].astype(BF)
        at = slice(r * cols, (r + 1) * cols)
        grads[2, :, at] = t_dot(pooled[...], total.astype(BF)) * factor
        copies.append(
            pltpu.make_async_copy(grads.at[2, :, at], g_out.at[:, block_place(r, cols)], sem.at[2 + r])
        )
        copies[-1].start()
    for copy in copies:
        copy.wait()


def graph(order, fan, node_dev, got, weights):
    parts = len(got)
    cols, width = weights[0][0].shape
    nodes = got[0].shape[0] * node_dev
    vmem = pl.BlockSpec(memory_space=pltpu.VMEM)
    anywhere = pl.BlockSpec(memory_space=pl.ANY)
    slab = jax.ShapeDtypeStruct((node_dev, cols), BF)
    big = jax.ShapeDtypeStruct((cols, width), F32)

    def kernel(*refs):
        first, rest = refs[: 2 * parts], refs[2 * parts : 4 * parts]
        outs, known = refs[4 * parts : 4 * parts + 5], refs[4 * parts + 5 : 4 * parts + 10]
        mean, *own = refs[4 * parts + 10 :]
        embed_kernel(order, fan, node_dev, *first, *known, mean)
        graph_kernel(node_dev, *known, *rest, *outs, *own)

    return pl.pallas_call(
        kernel,
        out_shape=(slab, slab, big, big, big),
        in_specs=[vmem] * (4 * parts),
        out_specs=(vmem, vmem, anywhere, anywhere, anywhere),
        scratch_shapes=[
            pltpu.VMEM((2, nodes, width), BF),
            pltpu.VMEM((nodes, width), BF),
            pltpu.VMEM((nodes, cols), BF),
            pltpu.VMEM((nodes, nodes), BF),
            pltpu.VMEM((nodes, 128), F32),
            pltpu.VMEM((nodes, width), F32),
            pltpu.VMEM((nodes, width), BF),
            pltpu.VMEM((node_dev, width), F32),
            pltpu.VMEM((3, cols, width), F32),
            pltpu.SemaphoreType.DMA((2 + parts,)),
        ],
        compiler_params=pltpu.CompilerParams(vmem_limit_bytes=36 * MIB),
        cost_estimate=pl.CostEstimate(
            flops=2 * nodes * width * width * 6, bytes_accessed=10 * MIB, transcendentals=nodes * width
        ),
    )(*got, *[group[0] for group in weights], *sum((group[1:] for group in weights), ()))


def graph_wide(order, fan, node_dev, got, weights):
    mp, dp = lax.axis_index("mp"), lax.axis_index("dp")
    parts = len(got)
    cols, width = weights[0][0].shape
    nodes = got[0].shape[0] * node_dev
    owners = jnp.array(order, jnp.int32) ^ dp
    names = (owners[:, None] * node_dev + jnp.arange(node_dev)[None, :]).reshape(1, 1, nodes)
    order = jnp.arange(parts) ^ mp
    even = (dp // 2) % 2 == 0
    kinds = [
        [group[0], jnp.where(even, group[1], group[2]), jnp.where(even, group[2], group[1])]
        for group in weights[2:]
    ]
    blocks = [*weights[:2], *kinds]
    w_out, w_self, w_neigh = (
        jnp.stack([group[k] for group in blocks])[order].reshape(width, width) for k in range(3)
    )

    def part(i):
        block = jnp.stack([unpack(g, cols, i) for g in got])[order]
        return block.transpose(1, 2, 0, 3).reshape(nodes, width)

    pooled = part(0).astype(BF)
    packed = got[0][:, :fan, got[0].shape[2] - IDS_COLS :].astype(jnp.int32)
    ids = packed[:, :, :node_dev] * 16 + packed[:, :, IDS_AT : IDS_AT + node_dev] - 1
    ids = ids.transpose(0, 2, 1).reshape(nodes, fan)
    cnt = jnp.maximum(jnp.sum(ids >= 0, axis=1).astype(F32), 1.0)[:, None]
    counts = jnp.sum(ids[:, :, None] == names, axis=1).astype(BF)
    embed = (part(2) + dot(pooled, w_out)).astype(BF)
    agg = (dot(counts, embed) / cnt).astype(BF)
    mixed, slope = gelu_parts(dot(embed, w_self) + dot(agg, w_neigh))
    dz = (part(1) * slope).astype(BF)
    msg = (dot_t(dz, w_neigh) / cnt).astype(BF)
    node_grad = (dot_t(dz, w_self) + t_dot(counts, msg)).astype(BF)
    factor = 1.0 / jnp.sqrt(jnp.float32(nodes))

    def own(a):
        return lax.dynamic_slice_in_dim(a, mp * cols, cols, 1)

    grads = [t_dot(own(a), b) * factor for a, b in ((embed, dz), (agg, dz), (pooled, node_grad))]
    return (own(mixed[:node_dev]).astype(BF), own(node_grad[:node_dev]), *grads)


def join_kernel(*refs):
    out, at = refs[-1], 0
    for ref in refs[:-1]:
        out[at : at + ref.shape[0]] = ref[...]
        at += ref.shape[0]


def join(*blocks):
    count = sum(b.shape[0] for b in blocks)
    if count > 8:
        return jnp.concatenate(blocks)
    vmem = pl.BlockSpec(memory_space=pltpu.VMEM)
    return pl.pallas_call(
        join_kernel,
        out_shape=jax.ShapeDtypeStruct((count, *blocks[0].shape[1:]), BF),
        in_specs=[vmem] * len(blocks),
        out_specs=vmem,
        compiler_params=pltpu.CompilerParams(vmem_limit_bytes=8 * MIB),
    )(*blocks)


def hop(x, axis, bit):
    return lax.ppermute(x, axis, [(i, i ^ bit) for i in range(lax.axis_size(axis))])


def gather_dp(block, later):
    size = lax.axis_size("dp")
    if size == 8:
        far = [hop(block, "dp", i) for i in (2, 4, 6)]
        mine = join(block)
        mine, far, later = lax.optimization_barrier((mine, far, later))
        block = join(mine, *far)
        order, bit = [0, 2, 4, 6], 1
    else:
        order, bit = [0], size // 2
    while bit:
        block = join(block, hop(block, "dp", bit))
        order = order + [i ^ bit for i in order]
        bit //= 2
    return block, order, later


def per_device(texts, w_qkv, w_out, w_self, w_neigh, neighbours, cotangent):
    node_dev, fan = neighbours.shape
    nodes = node_dev * lax.axis_size("dp")
    own = (w_out, w_self, w_neigh)
    even = (lax.axis_index("dp") // 2) % 2 == 0
    picked, w_out = lax.optimization_barrier((jnp.where(even, w_self, w_neigh), w_out))
    x_half = hop(picked, "mp", 2)
    x_out = hop(w_out, "mp", 2)
    here = tuple(hop(a, "mp", 1) for a in own)

    sent = attention(texts, w_qkv, cotangent, neighbours.T)[None]
    sent, here = lax.optimization_barrier((sent, here))
    sent, order, x_half = gather_dp(sent, x_half)
    sent, x_out = lax.optimization_barrier((sent, x_out))
    z_half = hop(x_half, "dp", 2)
    across = (x_out, x_half, z_half)
    there = tuple(hop(a, "mp", 1) for a in across)

    got_across = hop(sent, "mp", 2)
    got = (sent, hop(sent, "mp", 1), got_across, hop(got_across, "mp", 1))
    body = graph if nodes <= WIDE_LIMIT else graph_wide
    return body(order, fan, node_dev, got, (own, here, across, there))


def solution(mesh):
    return jax.shard_map(
        per_device,
        mesh=mesh,
        in_specs=(
            P("dp", None, None),
            P(None, "mp"),
            P("mp", None),
            P("mp", None),
            P("mp", None),
            P("dp", None),
            P("dp", "mp"),
        ),
        out_specs=(P("dp", "mp"), P("dp", "mp"), P("mp", None), P("mp", None), P("mp", None)),
        check_vma=False,
    )
```

```python
import functools

import jax
import jax.numpy as jnp
from jax import lax
from jax.experimental import pallas as pl
from jax.experimental.pallas import tpu as pltpu
from jax.sharding import PartitionSpec as P

HD = 64
BF = jnp.bfloat16
F32 = jnp.float32
NODES_STEP = 6
WIDE_LIMIT = 256
IDS_COLS = 128
IDS_AT = 32
TOP = 16
LOG2E = 1.4426950408889634
ATTENTION_VMEM = 58
COPIES = 2
MIB = 1 << 20


def dot_t(a, b):
    return lax.dot_general(a, b, (((1,), (1,)), ((), ())), preferred_element_type=F32)


def t_dot(a, b):
    return lax.dot_general(a, b, (((0,), (0,)), ((), ())), preferred_element_type=F32)


def dot(a, b):
    return jnp.dot(a, b, preferred_element_type=F32)


def attend(q, k, v):
    seq, cols = q.shape
    pair = 2 * HD
    left = lax.broadcasted_iota(jnp.int32, (seq, pair), 1) < HD
    zero = jnp.zeros((seq, pair), BF)
    out = []
    for at in range(0, cols, pair):
        both = q[:, at : at + pair]
        spread = jnp.concatenate([jnp.where(left, both, zero), jnp.where(left, zero, both)], axis=0)
        s = dot_t(k[:, at : at + pair], spread)
        e = jnp.exp2((s - jnp.max(s, axis=0, keepdims=True)) * (HD**-0.5 * LOG2E))
        p = (e * (1.0 / jnp.sum(e, axis=0, keepdims=True))).astype(BF).astype(F32)
        first = jnp.sum(p[:, :seq], axis=1, keepdims=True)
        second = jnp.sum(p[:, seq:], axis=1, keepdims=True)
        context = jnp.where(left, first, second) * v[:, at : at + pair].astype(F32)
        out.append(jnp.sum(context, axis=0, keepdims=True) * (1.0 / seq))
    return jnp.concatenate(out, axis=1)


def attention_kernel(
    heads, texts_ref, w_hbm, cot_ref, ids_ref, out_ref, wp, acc_p, acc_m, held, w_ref, sem
):
    step = pl.program_id(0)
    nodes, seq, width = held.shape[1:]
    node_dev = cot_ref.shape[0]
    cols = heads * HD

    some, deep = nodes // COPIES, width // COPIES

    def fetch(i):
        return [
            pltpu.make_async_copy(
                texts_ref.at[pl.ds(i * nodes + c * some, some)],
                held.at[i % 2, pl.ds(c * some, some)],
                sem.at[i % 2, c],
            )
            for c in range(COPIES)
        ]

    @pl.when(step == 0)
    def _():
        weights = [
            pltpu.make_async_copy(
                w_hbm.at[pl.ds(c * deep, deep)], w_ref.at[pl.ds(c * deep, deep)], sem.at[2, c]
            )
            for c in range(COPIES)
        ]
        for copy in weights + fetch(0):
            copy.start()
        for copy in weights:
            copy.wait()
        for part in range(3):
            for h in range(0, heads, 2):
                a = h * 3 * HD + part * HD
                b = a + 3 * HD
                wp[:, part * cols + h * HD : part * cols + (h + 2) * HD] = jnp.concatenate(
                    [w_ref[:, a : a + HD], w_ref[:, b : b + HD]], axis=1
                )

    @pl.when(step + 1 < pl.num_programs(0))
    def _():
        for copy in fetch(step + 1):
            copy.start()

    for copy in fetch(step):
        copy.wait()
    x_ref = held.at[step % 2]
    own = pl.ds(pl.multiple_of(lax.axis_index("mp") * cols, 128), cols)
    qkv = dot(x_ref[...].reshape(nodes * seq, width), wp[...]).astype(BF)
    for n in range(nodes):
        at = slice(n * seq, (n + 1) * seq)
        row = pl.ds(step * nodes + n, 1)
        acc_p[row, :] = attend(*(qkv[at, i * cols : (i + 1) * cols] for i in range(3)))
        mean = jnp.sum(x_ref[n, :, own].astype(F32), axis=0, keepdims=True)
        acc_m[row, :] = mean * (1.0 / seq)

    @pl.when(step == pl.num_programs(0) - 1)
    def _():
        rows = jnp.concatenate([acc_p[...], cot_ref[...].astype(F32), acc_m[...]], axis=1)
        shifted = ids_ref[...] + 1
        fan = shifted.shape[0]
        gap = jnp.zeros((fan, IDS_AT - node_dev), F32)
        high, low = (shifted >> 4).astype(F32), (shifted & 15).astype(F32)
        blank = jnp.zeros((fan, IDS_COLS - 2 * IDS_AT), F32)
        ids = jnp.concatenate([high, gap, low, gap, blank], axis=1)
        wide = 3 * cols
        rest = jnp.concatenate([rows[TOP:, : wide // 2], rows[TOP:, wide // 2 :]], axis=0)
        out_ref[:, :wide] = rows[:TOP].astype(BF)
        out_ref[:, wide : wide + wide // 2] = rest.astype(BF)
        out_ref[:, wide + wide // 2 :] = ids.astype(BF)


def unpack(got, cols, part):
    got = got.astype(F32)
    wide, at = 3 * cols, part * cols
    pieces, left = [], at
    while left < at + cols:
        side, inside = divmod(left, wide // 2)
        right = min(at + cols, (side + 1) * (wide // 2))
        low = wide + inside
        pieces.append(got[:, side * (TOP // 2) : (side + 1) * (TOP // 2), low : low + right - left])
        left = right
    rest = jnp.concatenate(pieces, axis=2) if len(pieces) > 1 else pieces[0]
    return jnp.concatenate([got[:, :, at : at + cols], rest], axis=1)


def attention(texts, w_qkv, cotangent, ids):
    node_dev, seq, width = texts.shape
    cols = w_qkv.shape[1] // 3
    heads = cols // HD
    tokens = node_dev * seq
    nodes = NODES_STEP
    packed = (TOP, 3 * cols + 3 * cols // 2 + IDS_COLS)
    return pl.pallas_call(
        functools.partial(attention_kernel, heads),
        out_shape=jax.ShapeDtypeStruct(packed, BF),
        grid=(node_dev // nodes,),
        in_specs=[
            pl.BlockSpec(memory_space=pl.ANY),
            pl.BlockSpec(memory_space=pl.ANY),
            pl.BlockSpec((node_dev, cols), lambda i: (0, 0)),
            pl.BlockSpec(ids.shape, lambda i: (0, 0)),
        ],
        out_specs=pl.BlockSpec(packed, lambda i: (0, 0)),
        scratch_shapes=[
            pltpu.VMEM((width, 3 * cols), BF),
            pltpu.VMEM((node_dev, cols), F32),
            pltpu.VMEM((node_dev, cols), F32),
            pltpu.VMEM((2, nodes, seq, width), BF),
            pltpu.VMEM((width, 3 * cols), BF),
            pltpu.SemaphoreType.DMA((3, COPIES)),
        ],
        compiler_params=pltpu.CompilerParams(vmem_limit_bytes=ATTENTION_VMEM * MIB),
        cost_estimate=pl.CostEstimate(
            flops=2 * tokens * width * 3 * cols + 8 * tokens * seq * cols,
            bytes_accessed=2 * tokens * width + 6 * width * cols,
            transcendentals=tokens * seq * heads,
        ),
    )(texts, w_qkv, cotangent, ids)


def gelu_parts(z):
    root = 0.7978845608028654
    cube = 0.044715
    t = jnp.tanh(root * (z + cube * (z * z * z)))
    half = 0.5 * (1.0 + t)
    slope = half + 0.5 * z * (1.0 - t * t) * (root * (1.0 + 3.0 * cube * (z * z)))
    return z * half, slope


def block_place(r, cols):
    return pl.ds(pl.multiple_of((lax.axis_index("mp") ^ r) * cols, 128), cols)


def embed_kernel(order, fan, node_dev, *refs):
    parts = 4
    got, blocks, refs = refs[:parts], refs[parts : 2 * parts], refs[2 * parts :]
    both, cot, pooled_ref, counts_ref, share_ref, mean = refs
    dp = lax.axis_index("dp")
    groups = got[0].shape[0]
    nodes = groups * node_dev
    cols = blocks[0].shape[0]

    def part(r, i):
        return unpack(got[r][...], cols, i).reshape(nodes, cols)

    packed = got[0][:, :, got[0].shape[2] - IDS_COLS :].astype(F32)
    ids = jnp.concatenate(
        [
            packed[i, :fan, :node_dev] * 16.0 + packed[i, :fan, IDS_AT : IDS_AT + node_dev] - 1.0
            for i in range(groups)
        ],
        axis=1,
    )
    place_of = lax.broadcasted_iota(jnp.int32, (nodes, 1), 0)
    names = place_of
    for i, o in enumerate(order):
        shift = ((dp ^ o) - i) * node_dev
        inside = (place_of >= i * node_dev) & (place_of < (i + 1) * node_dev)
        names = jnp.where(inside, place_of + shift, names)
    names = names.astype(F32)
    counts_t = jnp.zeros((nodes, nodes), F32)
    for s in range(fan):
        counts_t += (ids[s : s + 1, :] == names).astype(F32)
    counts = counts_t.T
    share = 1.0 / jnp.maximum(jnp.sum(counts, axis=1, keepdims=True), 1.0)
    counts_ref[...] = counts_t.astype(BF)
    share_ref[...] = jnp.broadcast_to(share, share_ref.shape)

    pooled = [part(r, 0).astype(BF) for r in range(parts)]
    pooled_ref[...] = pooled[0]
    for r in range(parts):
        cot[:, block_place(r, cols)] = part(r, 1).astype(BF)
        mean[:, block_place(r, cols)] = part(r, 2)
    sums = sum(dot(pooled[r], blocks[r][...]) for r in range(parts))
    both[0] = (mean[...] + sums).astype(BF)
    both[1] = (dot(counts.astype(BF), both[0]) * share).astype(BF)


def graph_kernel(node_dev, both, cot, pooled, counts, share_ref, *refs):
    parts = 4
    blocks, refs = refs[: 2 * parts], refs[2 * parts :]
    mixed_ref, grad_ref, g_self, g_neigh, g_out, dz, wide, grads, sem = refs
    side = (lax.axis_index("dp") // 2) % 2
    cols, width = g_self.shape
    nodes = counts.shape[0]
    factor = 1.0 / jnp.sqrt(jnp.float32(nodes))
    own = block_place(0, cols)

    z = 0.0
    for r in range(parts):
        first = 0 if r < 2 else side
        z += dot(both[first, :, block_place(r, cols)], blocks[2 * r][...])
        z += dot(both[1 - first, :, block_place(r, cols)], blocks[2 * r + 1][...])
    mixed, slope = gelu_parts(z)
    dz[...] = (cot[...].astype(F32) * slope).astype(BF)
    wide[...] = mixed[:node_dev, :]
    mixed_ref[...] = wide[:, own].astype(BF)

    copies = []
    for i, out in enumerate((g_self, g_neigh)):
        grads[i] = t_dot(both[i, :, own], dz[...]) * factor
        copies.append(pltpu.make_async_copy(grads.at[i], out, sem.at[i]))
        copies[-1].start()
    share = share_ref[:, :1]
    for r in range(parts):
        to_self, to_agg = dot_t(dz[...], blocks[2 * r][...]), dot_t(dz[...], blocks[2 * r + 1][...])
        if r >= 2:
            even = side == 0
            to_self, to_agg = jnp.where(even, to_self, to_agg), jnp.where(even, to_agg, to_self)
        total = to_self + dot(counts[...], (to_agg * share).astype(BF))
        if r == 0:
            grad_ref[...] = total[:node_dev, :].astype(BF)
        at = slice(r * cols, (r + 1) * cols)
        grads[2, :, at] = t_dot(pooled[...], total.astype(BF)) * factor
        copies.append(
            pltpu.make_async_copy(grads.at[2, :, at], g_out.at[:, block_place(r, cols)], sem.at[2 + r])
        )
        copies[-1].start()
    for copy in copies:
        copy.wait()


def graph(order, fan, node_dev, got, weights):
    parts = len(got)
    cols, width = weights[0][0].shape
    nodes = got[0].shape[0] * node_dev
    vmem = pl.BlockSpec(memory_space=pltpu.VMEM)
    anywhere = pl.BlockSpec(memory_space=pl.ANY)
    slab = jax.ShapeDtypeStruct((node_dev, cols), BF)
    big = jax.ShapeDtypeStruct((cols, width), F32)

    def kernel(*refs):
        first, rest = refs[: 2 * parts], refs[2 * parts : 4 * parts]
        outs, known = refs[4 * parts : 4 * parts + 5], refs[4 * parts + 5 : 4 * parts + 10]
        mean, *own = refs[4 * parts + 10 :]
        embed_kernel(order, fan, node_dev, *first, *known, mean)
        graph_kernel(node_dev, *known, *rest, *outs, *own)

    return pl.pallas_call(
        kernel,
        out_shape=(slab, slab, big, big, big),
        in_specs=[vmem] * (4 * parts),
        out_specs=(vmem, vmem, anywhere, anywhere, anywhere),
        scratch_shapes=[
            pltpu.VMEM((2, nodes, width), BF),
            pltpu.VMEM((nodes, width), BF),
            pltpu.VMEM((nodes, cols), BF),
            pltpu.VMEM((nodes, nodes), BF),
            pltpu.VMEM((nodes, 128), F32),
            pltpu.VMEM((nodes, width), F32),
            pltpu.VMEM((nodes, width), BF),
            pltpu.VMEM((node_dev, width), F32),
            pltpu.VMEM((3, cols, width), F32),
            pltpu.SemaphoreType.DMA((2 + parts,)),
        ],
        compiler_params=pltpu.CompilerParams(vmem_limit_bytes=36 * MIB),
        cost_estimate=pl.CostEstimate(
            flops=2 * nodes * width * width * 6, bytes_accessed=10 * MIB, transcendentals=nodes * width
        ),
    )(*got, *[group[0] for group in weights], *sum((group[1:] for group in weights), ()))


def graph_wide(order, fan, node_dev, got, weights):
    mp, dp = lax.axis_index("mp"), lax.axis_index("dp")
    parts = len(got)
    cols, width = weights[0][0].shape
    nodes = got[0].shape[0] * node_dev
    owners = jnp.array(order, jnp.int32) ^ dp
    names = (owners[:, None] * node_dev + jnp.arange(node_dev)[None, :]).reshape(1, 1, nodes)
    order = jnp.arange(parts) ^ mp
    even = (dp // 2) % 2 == 0
    kinds = [
        [group[0], jnp.where(even, group[1], group[2]), jnp.where(even, group[2], group[1])]
        for group in weights[2:]
    ]
    blocks = [*weights[:2], *kinds]
    w_out, w_self, w_neigh = (
        jnp.stack([group[k] for group in blocks])[order].reshape(width, width) for k in range(3)
    )

    def part(i):
        block = jnp.stack([unpack(g, cols, i) for g in got])[order]
        return block.transpose(1, 2, 0, 3).reshape(nodes, width)

    pooled = part(0).astype(BF)
    packed = got[0][:, :fan, got[0].shape[2] - IDS_COLS :].astype(jnp.int32)
    ids = packed[:, :, :node_dev] * 16 + packed[:, :, IDS_AT : IDS_AT + node_dev] - 1
    ids = ids.transpose(0, 2, 1).reshape(nodes, fan)
    cnt = jnp.maximum(jnp.sum(ids >= 0, axis=1).astype(F32), 1.0)[:, None]
    counts = jnp.sum(ids[:, :, None] == names, axis=1).astype(BF)
    embed = (part(2) + dot(pooled, w_out)).astype(BF)
    agg = (dot(counts, embed) / cnt).astype(BF)
    mixed, slope = gelu_parts(dot(embed, w_self) + dot(agg, w_neigh))
    dz = (part(1) * slope).astype(BF)
    msg = (dot_t(dz, w_neigh) / cnt).astype(BF)
    node_grad = (dot_t(dz, w_self) + t_dot(counts, msg)).astype(BF)
    factor = 1.0 / jnp.sqrt(jnp.float32(nodes))

    def own(a):
        return lax.dynamic_slice_in_dim(a, mp * cols, cols, 1)

    grads = [t_dot(own(a), b) * factor for a, b in ((embed, dz), (agg, dz), (pooled, node_grad))]
    return (own(mixed[:node_dev]).astype(BF), own(node_grad[:node_dev]), *grads)


def join_kernel(*refs):
    out, at = refs[-1], 0
    for ref in refs[:-1]:
        out[at : at + ref.shape[0]] = ref[...]
        at += ref.shape[0]


def join(*blocks):
    count = sum(b.shape[0] for b in blocks)
    if count > 8:
        return jnp.concatenate(blocks)
    vmem = pl.BlockSpec(memory_space=pltpu.VMEM)
    return pl.pallas_call(
        join_kernel,
        out_shape=jax.ShapeDtypeStruct((count, *blocks[0].shape[1:]), BF),
        in_specs=[vmem] * len(blocks),
        out_specs=vmem,
        compiler_params=pltpu.CompilerParams(vmem_limit_bytes=8 * MIB),
    )(*blocks)


def hop(x, axis, bit):
    return lax.ppermute(x, axis, [(i, i ^ bit) for i in range(lax.axis_size(axis))])


def gather_dp(block, later):
    size = lax.axis_size("dp")
    if size == 8:
        far = [hop(block, "dp", i) for i in (2, 4, 6)]
        mine = join(block)
        mine, far, later = lax.optimization_barrier((mine, far, later))
        block = join(mine, *far)
        order, bit = [0, 2, 4, 6], 1
    else:
        order, bit = [0], size // 2
    while bit:
        block = join(block, hop(block, "dp", bit))
        order = order + [i ^ bit for i in order]
        bit //= 2
    return block, order, later


def per_device(texts, w_qkv, w_out, w_self, w_neigh, neighbours, cotangent):
    node_dev, fan = neighbours.shape
    nodes = node_dev * lax.axis_size("dp")
    own = (w_out, w_self, w_neigh)
    even = (lax.axis_index("dp") // 2) % 2 == 0
    picked, w_out = lax.optimization_barrier((jnp.where(even, w_self, w_neigh), w_out))
    x_half = hop(picked, "mp", 2)
    x_out = hop(w_out, "mp", 2)
    here = tuple(hop(a, "mp", 1) for a in own)

    sent = attention(texts, w_qkv, cotangent, neighbours.T)[None]
    sent, here = lax.optimization_barrier((sent, here))
    sent, order, x_half = gather_dp(sent, x_half)
    sent, x_out = lax.optimization_barrier((sent, x_out))
    z_half = hop(x_half, "dp", 2)
    across = (x_out, x_half, z_half)
    there = tuple(hop(a, "mp", 1) for a in across)

    got_across = hop(sent, "mp", 2)
    got = (sent, hop(sent, "mp", 1), got_across, hop(got_across, "mp", 1))
    body = graph if nodes <= WIDE_LIMIT else graph_wide
    return body(order, fan, node_dev, got, (own, here, across, there))


def solution(mesh):
    return jax.shard_map(
        per_device,
        mesh=mesh,
        in_specs=(
            P("dp", None, None),
            P(None, "mp"),
            P("mp", None),
            P("mp", None),
            P("mp", None),
            P("dp", None),
            P("dp", "mp"),
        ),
        out_specs=(P("dp", "mp"), P("dp", "mp"), P("mp", None), P("mp", None), P("mp", None)),
        check_vma=False,
    )
```
